32 devices in a mesh: grp: 2 (over y), seq: 4 (over z), ch: 4 (over x, core).
Axes of the slice: x: 2, y: 2, z: 4, core: 2. Of those that a mesh axis runs over, the one named last changes fastest.
Arguments:
- x_saved: bfloat16 [8192, 1536], P(('grp', 'seq'), 'ch'), parts along dimension 0, may hold values from -6 to 6
- pre_act: bfloat16 [8192, 1536], P(('grp', 'seq'), 'ch'), parts along dimension 0, may hold values from -6 to 6
- out_grad: bfloat16 [4096, 1536], P(('grp', 'seq'), 'ch'), parts along dimension 0, may hold values from -6 to 6
- conv_w: bfloat16 [1536, 5, 1536], P(None, None, 'ch'), may hold values from -0.0625 to 0.0625
- coverage_obs: float32 [8, 8, 8, 1536], P(('grp', 'seq'), None, None, 'ch'), parts along dimension 0, may hold values from 1 to 8
- owners: int32 [32], P('grp'), parts along dimension 0, may hold values from 0 to 3, as said below
- exon_blocks: int32 [32, 2], P('grp'), parts along dimension 0, may hold values from 0 to 255, as said below
Outputs:
- in_grad: bfloat16 [8192, 1536], P(('grp', 'seq'), 'ch'), parts along dimension 0
- w_grad: bfloat16 [3072, 5, 1536], P(('grp', 'seq'), None, 'ch'), parts along dimension 0
The draws below stay inside these ranges and needn't reach their ends.
There are 2 independent parts, one for each index of `grp`. The reference program is written for one: setup_inputs(seed, part) draws one part's arguments, and reference() takes and returns one part's arrays. A program takes and returns all parts, laid end to end along the dimension named above; an argument that names none is the same for every part. Nothing has to cross between parts.
Inputs may be any that keep to these rules, and one draw needn't show every extreme that they name: `owners`: no device owns more than 8 transcripts, and some device owns exactly 8. `exon_blocks`: block b holds pooled rows 8 * b to 8 * b + 7, which lie on device b // 64 of seq; the 2 exon blocks of one transcript lie on 2 different devices, and for some owner device one device holds exon blocks of all its transcripts.
All inputs are finite; a program needn't handle non-finite values.
Results may differ from the reference program's by a relative error of at most 0.0095.
Values may be sent and summed in bfloat16 or wider, within the bound.
No kernel may reach another device: no remote copies, remote signals or barrier semaphores. Data moves between devices by JAX's collectives and lax.ppermute only.
A program may use at most 64 MiB of HBM per device.

```python
import jax
import jax.numpy as jnp
from jax import lax

C = 1536
KW = 5
L_DEV = 1024
BLK = 8
TX_DEV = 4
SPAN = 2
MOST = 8
TRANS = 16
L = 4096
PL = 2048
N_SEQ = 4


def routing_tables(key):
    nseq = TRANS // TX_DEV
    nblocks = L_DEV // 2 // BLK
    base_key = jax.random.fold_in(key, 7)
    k_heavy, k_perm, k_start, k_common, k_inner = jax.random.split(base_key, 5)
    base = jnp.arange(TRANS, dtype=jnp.int32) // TX_DEV
    heavy = jax.random.randint(k_heavy, (), 0, nseq, dtype=jnp.int32)
    donor = (heavy + 1) % nseq
    owner = jnp.where(base == donor, heavy, base)
    owner = owner[jax.random.permutation(k_perm, TRANS)]
    starts = jax.random.randint(k_start, (TRANS,), 0, nseq - SPAN + 1, dtype=jnp.int32)
    common = jax.random.randint(k_common, (), 0, nseq - SPAN + 1, dtype=jnp.int32)
    starts = jnp.where(owner == heavy, common, starts)
    devices = starts[:, None] + jnp.arange(SPAN, dtype=jnp.int32)[None, :]
    inner = jax.random.randint(k_inner, (TRANS, SPAN), 0, nblocks, dtype=jnp.int32)
    return (owner.astype(jnp.int32), (devices * nblocks + inner).astype(jnp.int32))


def draw_owners(key, part):
    return routing_tables(key)[0]


def draw_exon_blocks(key, part):
    return routing_tables(key)[1]


def levels(rng, dims, cuts, low, largest):
    level, own = 1.0, jax.random.fold_in(rng, 6)
    for axis_at, blocks in cuts:
        heights = jnp.exp(jax.random.uniform(jax.random.fold_in(own, axis_at), (blocks,), jnp.float32, low / len(cuts), largest / len(cuts)))
        level = level * jnp.repeat(heights, dims[axis_at] // blocks).reshape([-1 if axis == axis_at else 1 for axis in range(len(dims))])
    return level


def normal_values(stream_key, extent, spread, bound, pieces=(), kind=jnp.bfloat16):
    drawn = spread * jax.random.normal(stream_key, extent, jnp.float32)
    if pieces:
        drawn = drawn * levels(stream_key, extent, pieces, -0.22, 0.18)
    return jnp.clip(drawn, -bound, bound).astype(kind)


def setup_inputs(seed: int = 0, part: int = 0) -> dict:
    seeds = jax.random.split(jax.random.key(seed), 8)
    own_keys = jax.random.split(jax.random.fold_in(seeds[7], part), 8)
    return {
        "x_saved": normal_values(own_keys[0], (L, C), 1.0, 6.0, ((0, 4), (1, 4))),
        "pre_act": normal_values(own_keys[1], (L, C), 1.0, 6.0, ((0, 4), (1, 4))),
        "out_grad": normal_values(own_keys[2], (PL, C), 1.0, 6.0, ((0, 4), (1, 4))),
        "conv_w": normal_values(seeds[3], (C, KW, C), (KW * C) ** -0.5, 0.0625, ((2, 4),)),
        "coverage_obs": jnp.clip(1.0 + 7.0 * jax.random.uniform(own_keys[4], (N_SEQ, MOST, BLK, C), jnp.float32) ** levels(own_keys[4], (N_SEQ, MOST, BLK, C), ((0, 4), (3, 4)), -0.2, 0.2), 1.0, 8.0),
        "owners": draw_owners(jax.random.fold_in(jax.random.fold_in(seeds[7], part), 71), part),
        "exon_blocks": draw_exon_blocks(jax.random.fold_in(jax.random.fold_in(seeds[7], part), 71), part),
    }


def gelu_pair(value):
    normal_cdf = 0.5 * (1.0 + jax.scipy.special.erf(value * 0.7071067811865476))
    density = jnp.exp(-0.5 * value * value) * 0.3989422804014327
    return value * normal_cdf, normal_cdf + value * density


def reference(x_saved, pre_act, out_grad, conv_w, coverage_obs, owners, exon_blocks):
    total_rows = x_saved.shape[0]
    width = x_saved.shape[1]
    act, slope = gelu_pair(pre_act.astype(jnp.float32))
    pooled = (0.5 * jnp.sum(act.reshape(total_rows // 2, 2, width), axis=1)).astype(jnp.bfloat16)
    nblocks = total_rows // 2 // BLK
    pblocks = pooled.reshape(nblocks, BLK, width).astype(jnp.float32)
    coverage = jnp.zeros((owners.shape[0], BLK, width), jnp.float32)
    for exon in range(SPAN):
        coverage = coverage + pblocks[exon_blocks[:, exon]]
    order = jnp.arange(owners.shape[0], dtype=jnp.int32)
    same = owners[:, None] == owners[None, :]
    rank = jnp.sum((same & (order[:, None] < order[None, :])).astype(jnp.int32), axis=0).astype(jnp.int32)
    target = coverage_obs[owners, rank]
    splice = jnp.tanh(coverage - target).astype(jnp.bfloat16)
    gained = jnp.zeros((nblocks, BLK, width), jnp.float32)
    for exon in range(SPAN):
        gained = gained.at[exon_blocks[:, exon]].add(splice.astype(jnp.float32))
    pooled_grad = out_grad.astype(jnp.float32) + gained.reshape(total_rows // 2, width)
    pre_grad = (jnp.repeat(pooled_grad, 2, axis=0) * 0.5 * slope).astype(jnp.bfloat16)
    grad_pad = jnp.pad(pre_grad, ((2, 2), (0, 0)))
    total = jnp.zeros((total_rows, width), jnp.float32)
    for tap in range(KW):
        total = total + jnp.dot(grad_pad[4 - tap:4 - tap + total_rows], conv_w[:, tap, :], preferred_element_type=jnp.float32)
    in_grad = total.astype(jnp.bfloat16)
    x_pad = jnp.pad(x_saved, ((2, 2), (0, 0)))

    def add_shard(shard, acc):
        start = (shard * L_DEV).astype(jnp.int32)
        rows = lax.dynamic_slice_in_dim(pre_grad, start, L_DEV, 0)
        window = lax.dynamic_slice_in_dim(x_pad, start, L_DEV + 4, 0)
        terms = [jnp.dot(rows.T, window[tap:tap + L_DEV], preferred_element_type=jnp.float32) for tap in range(KW)]
        part = lax.optimization_barrier(jnp.stack(terms, axis=1).astype(jnp.bfloat16))
        return acc + part.astype(jnp.float32)

    summed = lax.fori_loop(0, N_SEQ, add_shard, jnp.zeros((width, KW, width), jnp.float32))
    return in_grad, summed.astype(jnp.bfloat16)
```

```python
import functools

import jax
import jax.numpy as jnp
from jax import lax
from jax.experimental import pallas as pl
from jax.experimental.pallas import tpu as pltpu
from jax.sharding import PartitionSpec as P

PAD = 16
MIB = 1024 * 1024


def swap(block, axis, flip):
    count = lax.axis_size(axis)
    return lax.ppermute(block, axis, [(i, i ^ flip) for i in range(count)])


def shift(block, axis, step, first=0):
    count = lax.axis_size(axis)
    if step > 0:
        pairs = [(i, i + 1) for i in range(first, count - 1)]
    else:
        pairs = [(i + 1, i) for i in range(count - 1 - first)]
    return lax.ppermute(block, axis, pairs)


def gelu_pair(value):
    normal_cdf = 0.5 * (1.0 + jax.scipy.special.erf(value * 0.7071067811865476))
    density = jnp.exp(-0.5 * value * value) * 0.3989422804014327
    return (value * normal_cdf, normal_cdf + value * density)


def pad_offsets(values):
    return jnp.stack([jnp.asarray(v, jnp.int32) for v in values])


def input_kernel(taps, tile, offs, *refs, pieces):
    parts, (low, high, weights, out, wide, wbuf, sems) = refs[:pieces], refs[pieces:]
    rows = parts[0].shape[0]
    half = taps // 2
    copies = []
    base = 0
    for e in range(pieces):
        span = parts[e].shape[1]
        src = weights.at[:, pl.ds(pl.multiple_of(offs[e], 16), span), :]
        copy = pltpu.make_async_copy(src, wbuf.at[:, pl.ds(base, span), :], sems.at[e])
        copy.start()
        copies.append(copy)
        base += span
    base = 0
    for e in range(pieces):
        span = parts[e].shape[1]
        wide[pl.ds(0, PAD), pl.ds(base, span)] = low[:, pl.ds(base, span)]
        wide[pl.ds(PAD, rows), pl.ds(base, span)] = parts[e][...]
        wide[pl.ds(PAD + rows, PAD), pl.ds(base, span)] = high[:, pl.ds(base, span)]
        base += span
    for copy in copies:
        copy.wait()

    def body(step, carry):
        start = pl.multiple_of(step * tile, tile)
        block = wide[pl.ds(start, tile + 2 * PAD), :]
        total = None
        for tap in range(taps):
            term = jnp.dot(block, wbuf[tap], preferred_element_type=jnp.float32)
            first = PAD + half - tap
            term = term[first : first + tile]
            total = term if total is None else total + term
        out[pl.ds(start, tile), :] = total.astype(out.dtype)
        return carry

    lax.fori_loop(0, rows // tile, body, 0)


def input_gradient(parts, low, high, weights, offs):
    taps, chans, width = weights.shape
    rows = parts[0].shape[0]
    tile = min(256, rows)
    vmem = pl.BlockSpec(memory_space=pltpu.VMEM)
    return pl.pallas_call(
        functools.partial(input_kernel, taps, tile, pieces=len(parts)),
        out_shape=jax.ShapeDtypeStruct((rows, width), jnp.bfloat16),
        in_specs=[pl.BlockSpec(memory_space=pltpu.SMEM)]
        + [vmem] * (len(parts) + 2)
        + [pl.BlockSpec(memory_space=pl.ANY)],
        out_specs=vmem,
        scratch_shapes=[
            pltpu.VMEM((rows + 2 * PAD, chans), jnp.bfloat16),
            pltpu.VMEM((taps, chans, width), jnp.bfloat16),
            pltpu.SemaphoreType.DMA((len(parts),)),
        ],
        cost_estimate=pl.CostEstimate(
            flops=2 * rows * chans * width * taps,
            bytes_accessed=2 * (rows * chans + taps * chans * width + rows * width),
            transcendentals=0,
        ),
        compiler_params=pltpu.CompilerParams(vmem_limit_bytes=32 * MIB),
    )(offs, *parts, low, high, weights)


def weight_kernel(taps, tile, rows, offs, *refs, nx, ng):
    xs, gs = refs[:nx], refs[nx : nx + ng]
    out, xbuf, gbuf, acc, sems = refs[nx + ng :]
    half = taps // 2

    def copy(at):
        if at < nx:
            src, dst, extra = xs[at], xbuf, PAD
        else:
            src, dst, extra = gs[at - nx], gbuf, 0
        row = pl.multiple_of(offs[at] + extra, 16)
        return pltpu.make_async_copy(src, dst.at[pl.ds(row, src.shape[0]), :], sems.at[at])

    for at in range(nx + ng):

        @pl.when(offs[at] >= 0)
        def _():
            copy(at).start()

    zeros = jnp.zeros((PAD, xbuf.shape[1]), xbuf.dtype)
    xbuf[pl.ds(0, PAD), :] = zeros
    xbuf[pl.ds(PAD + rows, PAD), :] = zeros
    acc[...] = jnp.zeros_like(acc)
    for at in range(nx + ng):

        @pl.when(offs[at] >= 0)
        def _():
            copy(at).wait()

    def body(step, carry):
        start = pl.multiple_of(step * tile, tile)
        grad = gbuf[pl.ds(start, tile), :].T
        block = xbuf[pl.ds(start, tile + 2 * PAD), :].astype(jnp.float32)
        for tap in range(taps):
            first = PAD - half + tap
            moved = block[first : first + tile].astype(jnp.bfloat16)
            acc[tap] += jnp.dot(grad, moved, preferred_element_type=jnp.float32)
        return carry

    lax.fori_loop(0, rows // tile, body, 0)
    out[...] = acc[...].astype(out.dtype)


def weight_gradient(xs, gs, offs, taps, rows):
    width, chunk = xs[0].shape[1], gs[0].shape[1]
    tile = min(512, rows)
    some = pl.BlockSpec(memory_space=pl.ANY)
    return pl.pallas_call(
        functools.partial(weight_kernel, taps, tile, rows, nx=len(xs), ng=len(gs)),
        out_shape=jax.ShapeDtypeStruct((taps, chunk, width), jnp.bfloat16),
        in_specs=[pl.BlockSpec(memory_space=pltpu.SMEM)] + [some] * (len(xs) + len(gs)),
        out_specs=pl.BlockSpec(memory_space=pltpu.VMEM),
        scratch_shapes=[
            pltpu.VMEM((rows + 2 * PAD, width), jnp.bfloat16),
            pltpu.VMEM((rows, chunk), jnp.bfloat16),
            pltpu.VMEM((taps, chunk, width), jnp.float32),
            pltpu.SemaphoreType.DMA((len(xs) + len(gs),)),
        ],
        cost_estimate=pl.CostEstimate(
            flops=2 * rows * chunk * width * taps,
            bytes_accessed=2 * rows * (chunk + width),
            transcendentals=0,
        ),
        compiler_params=pltpu.CompilerParams(vmem_limit_bytes=40 * MIB),
    )(offs, *xs, *gs)


def local(x_saved, pre_act, out_grad, conv_w, coverage_obs, owners, exon_blocks):
    rows = x_saved.shape[0]
    width = x_saved.shape[1]
    taps = conv_w.shape[1]
    nseq = lax.axis_size("seq")
    nch = lax.axis_size("ch")
    mine = lax.axis_index("seq")
    place = lax.axis_index("ch")
    chunk = conv_w.shape[0] // nseq
    most = coverage_obs.shape[1]
    block = coverage_obs.shape[2]
    nblocks = rows // 2 // block
    counts = owners.shape[0]
    direct = nseq == nch and nseq <= 4 and chunk == width and width % 128 == 0

    if direct:
        xs, x_offs = [x_saved], [mine * rows]
        up = down = x_saved
        for hop in range(1, nseq):
            up = shift(up, "seq", 1, hop - 1)
            down = shift(down, "seq", -1, hop - 1)
            xs += [up, down]
            x_offs += [
                jnp.where(mine >= hop, (mine - hop) * rows, -1),
                jnp.where(mine + hop < nseq, (mine + hop) * rows, -1),
            ]
    else:
        xs, x_offs = [lax.all_gather(x_saved, "seq", axis=0, tiled=True)], [0]

    act, slope = gelu_pair(pre_act.astype(jnp.float32))
    pooled = (0.5 * jnp.sum(act.reshape(rows // 2, 2, width), axis=1)).astype(jnp.bfloat16)
    order = jnp.arange(counts, dtype=jnp.int32)
    same = owners[:, None] == owners[None, :]
    rank = jnp.sum((same & (order[:, None] < order[None, :])).astype(jnp.int32), axis=0)
    dest = jnp.arange(nseq, dtype=jnp.int32)
    if direct:
        dest = dest ^ mine
    slots = jnp.arange(most, dtype=jnp.int32)
    route = (owners[None, None, :] == dest[:, None, None]) & (
        rank[None, None, :] == slots[None, :, None]
    )
    route = route.astype(jnp.float32).reshape(nseq * most, counts)
    on_mine = exon_blocks // nblocks == mine
    holds = jnp.any(on_mine, axis=1)
    local_block = jnp.sum(jnp.where(on_mine, exon_blocks % nblocks, 0), axis=1)
    select = (
        holds[:, None] & (local_block[:, None] == jnp.arange(nblocks, dtype=jnp.int32)[None, :])
    ).astype(jnp.float32)
    picker = jnp.dot(route, select, precision=lax.Precision.HIGHEST).astype(jnp.bfloat16)
    pieces = pooled.reshape(nblocks, block * width)
    outgoing = jnp.dot(picker, pieces, preferred_element_type=jnp.float32).astype(jnp.bfloat16)
    outgoing = outgoing.reshape(nseq, most, block, width)
    if direct:
        arrived = [outgoing[0]] + [swap(outgoing[d], "seq", d) for d in range(1, nseq)]
        coverage = functools.reduce(jnp.add, [a.astype(jnp.float32) for a in arrived])
    else:
        arrived = lax.all_to_all(outgoing, "seq", split_axis=0, concat_axis=0, tiled=True)
        coverage = jnp.sum(arrived.astype(jnp.float32), axis=0)
    splice = jnp.tanh(coverage - coverage_obs[0]).astype(jnp.bfloat16)
    if direct:
        returned = jnp.stack([splice] + [swap(splice, "seq", d) for d in range(1, nseq)])
    else:
        returned = lax.all_gather(splice, "seq", axis=0, tiled=False)
    returned = returned.reshape(nseq * most, block * width)
    gained = jnp.dot(picker.T, returned, preferred_element_type=jnp.float32).reshape(
        rows // 2, width
    )
    pooled_grad = out_grad.astype(jnp.float32) + gained
    pre_grad = (jnp.repeat(pooled_grad, 2, axis=0) * 0.5 * slope).astype(jnp.bfloat16)

    if direct:
        parts = [pre_grad]
        flip = nch // 2
        while flip:
            parts = parts + [swap(p, "ch", flip) for p in parts]
            flip //= 2
        tags = [0]
        flip = nch // 2
        while flip:
            tags = tags + [t | flip for t in tags]
            flip //= 2
        w_offs = [(place ^ t) * width for t in tags]
        quarter = rows // nch
        slices = [lax.dynamic_slice_in_dim(p, place * quarter, quarter, axis=0) for p in parts]

        def chosen(flipped, options):
            want = mine ^ flipped ^ place
            picked = options[0]
            for t, option in zip(tags[1:], options[1:]):
                picked = jnp.where(want == t, option, picked)
            return picked

        gs, g_offs = [chosen(0, parts)], [mine * rows]
        for d in range(1, nseq):
            got = [swap(chosen(d, slices), "seq", d)]
            flip = nch // 2
            while flip:
                got = got + [swap(p, "ch", flip) for p in got]
                flip //= 2
            gs += got
            g_offs += [(mine ^ d) * rows + (place ^ t) * quarter for t in tags]
    else:
        whole = lax.all_gather(pre_grad, "ch", axis=1, tiled=True)
        parts, w_offs = [whole], [0]
        blocks = whole.reshape(rows, nseq, chunk).transpose(1, 0, 2)
        gs = [lax.all_to_all(blocks, "seq", 0, 0, tiled=True).reshape(nseq * rows, chunk)]
        g_offs = [0]
    low = shift(jnp.concatenate([p[rows - PAD :] for p in parts], axis=1), "seq", 1)
    high = shift(jnp.concatenate([p[:PAD] for p in parts], axis=1), "seq", -1)

    weights = conv_w.transpose(1, 0, 2)
    in_grad = input_gradient(parts, low, high, weights, pad_offsets(w_offs))
    w_grad = weight_gradient(xs, gs, pad_offsets(x_offs + g_offs), taps, nseq * rows)
    return (in_grad, w_grad.transpose(1, 0, 2))


def solution(mesh):
    in_specs = (
        P(("grp", "seq"), "ch"),
        P(("grp", "seq"), "ch"),
        P(("grp", "seq"), "ch"),
        P(None, None, "ch"),
        P(("grp", "seq"), None, None, "ch"),
        P("grp"),
        P("grp", None),
    )
    out_specs = (P(("grp", "seq"), "ch"), P(("grp", "seq"), None, "ch"))
    return jax.shard_map(local, mesh=mesh, in_specs=in_specs, out_specs=out_specs, check_vma=False)
```

```python
import functools

import jax
import jax.numpy as jnp
from jax import lax
from jax.experimental import pallas as pl
from jax.experimental.pallas import tpu as pltpu
from jax.sharding import PartitionSpec as P

PAD = 16
MIB = 1024 * 1024
VMEM = pl.BlockSpec(memory_space=pltpu.VMEM)
SMEM = pl.BlockSpec(memory_space=pltpu.SMEM)
SOME = pl.BlockSpec(memory_space=pl.ANY)
HALF_ROOT = 0.7071067811865476
DENSITY = 0.3989422804014327
LANES = 128


def swap(block, axis, flip):
    count = lax.axis_size(axis)
    return lax.ppermute(block, axis, [(i, i ^ flip) for i in range(count)])


def shift(block, axis, step, first=0):
    count = lax.axis_size(axis)
    if step > 0:
        pairs = [(i, i + 1) for i in range(first, count - 1)]
    else:
        pairs = [(i + 1, i) for i in range(count - 1 - first)]
    return lax.ppermute(block, axis, pairs)


def after(values, others=()):
    return lax.optimization_barrier(tuple(values) + tuple(others))[: len(values)]


def input_kernel(*refs, taps, tile, pieces, origins):
    parts, (low, high, weights, out, wide, wbuf, sems) = refs[:pieces], refs[pieces:]
    rows = parts[0].shape[0]
    half = taps // 2
    copies = []
    base = 0
    for e, origin in enumerate(origins()):
        span = parts[e].shape[1]
        src = weights.at[:, pl.ds(pl.multiple_of(origin, 16), span), :]
        copy = pltpu.make_async_copy(src, wbuf.at[:, pl.ds(base, span), :], sems.at[e])
        copy.start()
        copies.append(copy)
        base += span
    base = 0
    for e in range(pieces):
        span = parts[e].shape[1]
        wide[pl.ds(0, PAD), pl.ds(base, span)] = low[:, pl.ds(base, span)]
        wide[pl.ds(PAD, rows), pl.ds(base, span)] = parts[e][...]
        wide[pl.ds(PAD + rows, PAD), pl.ds(base, span)] = high[:, pl.ds(base, span)]
        base += span
    for copy in copies:
        copy.wait()

    def body(step, carry):
        start = pl.multiple_of(step * tile, tile)
        block = wide[pl.ds(start, tile + 2 * PAD), :]
        total = None
        for tap in range(taps):
            term = jnp.dot(block, wbuf[tap], preferred_element_type=jnp.float32)
            first = PAD + half - tap
            term = term[first : first + tile]
            total = term if total is None else total + term
        out[pl.ds(start, tile), :] = total.astype(out.dtype)
        return carry

    lax.fori_loop(0, rows // tile, body, 0)


def input_gradient(parts, low, high, weights, origins):
    taps, chans, width = weights.shape
    rows = parts[0].shape[0]
    return pl.pallas_call(
        functools.partial(
            input_kernel, taps=taps, tile=min(256, rows), pieces=len(parts), origins=origins
        ),
        out_shape=jax.ShapeDtypeStruct((rows, width), jnp.bfloat16),
        in_specs=[VMEM] * (len(parts) + 2) + [SOME],
        out_specs=VMEM,
        scratch_shapes=[
            pltpu.VMEM((rows + 2 * PAD, chans), jnp.bfloat16),
            pltpu.VMEM((taps, chans, width), jnp.bfloat16),
            pltpu.SemaphoreType.DMA((len(parts),)),
        ],
        cost_estimate=pl.CostEstimate(
            flops=2 * rows * chans * width * taps,
            bytes_accessed=2 * (rows * chans + taps * chans * width + rows * width),
            transcendentals=0,
        ),
        compiler_params=pltpu.CompilerParams(vmem_limit_bytes=32 * MIB),
    )(*parts, low, high, weights)


def weight_kernel(*refs, taps, tile, rows, size, nx, ng, layout, first):
    xs, gs, rest = refs[:nx], refs[nx : nx + ng], refs[nx + ng :]
    if first:
        out, xbuf, gbuf, acc, sems = rest
    else:
        before, out, xbuf, gbuf, acc, sems = rest
    half = taps // 2
    x_rows, g_rows, starts = layout()
    zeros = jnp.zeros((PAD, xbuf.shape[1]), xbuf.dtype)
    xbuf[pl.ds(0, PAD), :] = zeros
    xbuf[pl.ds(PAD + rows, PAD), :] = zeros
    pieces = [(src, xbuf, row) for src, row in zip(xs, x_rows)]
    pieces += [(src, gbuf, row) for src, row in zip(gs, g_rows)]

    def copy(at):
        src, dst, row = pieces[at]
        row = row if isinstance(row, int) else pl.multiple_of(row, 16)
        return pltpu.make_async_copy(src, dst.at[pl.ds(row, src.shape[0]), :], sems.at[at])

    def each(act):
        for at in range(nx + ng):
            row = pieces[at][2]
            if isinstance(row, int):
                act(at)
            else:
                pl.when(row >= 0)(functools.partial(act, at))

    each(lambda at: copy(at).start())
    acc[...] = jnp.zeros_like(acc) if first else before[...]
    each(lambda at: copy(at).wait())

    for begin in starts:

        def body(step, carry):
            start = begin + step * tile
            start = pl.multiple_of(start, 16)
            grad = gbuf[pl.ds(start, tile), :].T
            block = xbuf[pl.ds(start, tile + 2 * PAD), :].astype(jnp.float32)
            for tap in range(taps):
                at = PAD - half + tap
                moved = block[at : at + tile].astype(jnp.bfloat16)
                acc[tap] += jnp.dot(grad, moved, preferred_element_type=jnp.float32)
            return carry

        lax.fori_loop(0, size // tile, body, 0)
    out[...] = acc[...].astype(out.dtype)


def weight_gradient(xs, gs, layout, size, work, taps, rows, before=None, last=True):
    width, chunk = xs[0].shape[1], gs[0].shape[1]
    return pl.pallas_call(
        functools.partial(
            weight_kernel,
            taps=taps,
            tile=min(512, size),
            rows=rows,
            size=size,
            nx=len(xs),
            ng=len(gs),
            layout=layout,
            first=before is None,
        ),
        out_shape=jax.ShapeDtypeStruct(
            (taps, chunk, width), jnp.bfloat16 if last else jnp.float32
        ),
        in_specs=[SOME] * (len(xs) + len(gs)) + [VMEM] * (before is not None),
        out_specs=VMEM,
        scratch_shapes=[
            pltpu.VMEM((rows + 2 * PAD, width), jnp.bfloat16),
            pltpu.VMEM((rows, chunk), jnp.bfloat16),
            pltpu.VMEM((taps, chunk, width), jnp.float32),
            pltpu.SemaphoreType.DMA((len(xs) + len(gs),)),
        ],
        cost_estimate=pl.CostEstimate(
            flops=2 * work * chunk * width * taps,
            bytes_accessed=2 * work * (chunk + width),
            transcendentals=0,
        ),
        compiler_params=pltpu.CompilerParams(vmem_limit_bytes=40 * MIB),
    )(*xs, *gs, *([] if before is None else [before]))


def merge_pairs(value, scratch):
    size = value.shape[0] // 2
    sums = []
    for at in range(value.shape[1] // LANES):
        scratch[at] = value[:, at * LANES : (at + 1) * LANES]
        even = scratch[at, pl.ds(0, size, stride=2), :]
        sums.append(even + scratch[at, pl.ds(1, size, stride=2), :])
    return jnp.concatenate(sums, axis=1)


def make_pairs(value, scratch):
    size = value.shape[0]
    rows = []
    for at in range(value.shape[1] // LANES):
        part = value[:, at * LANES : (at + 1) * LANES]
        scratch[at, pl.ds(0, size, stride=2), :] = part
        scratch[at, pl.ds(1, size, stride=2), :] = part
        rows.append(scratch[at])
    return jnp.concatenate(rows, axis=1)


def pair_scratch(rows, width):
    return pltpu.VMEM((width // LANES, rows, LANES), jnp.float32)


def each_exon(owners, exons, seen, nblocks, most, act):
    mine = lax.axis_index("seq")
    span, count = exons.shape
    for i in range(seen.shape[0]):
        seen[i] = 0

    def body(t, carry):
        owner = owners[t]
        slot = (owner ^ mine) * most + seen[owner]
        seen[owner] += 1
        for e in range(span):
            where = exons[e, t]

            @pl.when(where // nblocks == mine)
            def _():
                act(slot, where % nblocks)

        return carry

    lax.fori_loop(0, count, body, 0)


def front_kernel(owners, exons, pre_act, *refs, nblocks, most, size):
    outs, (slots, pair, seen) = refs[:-3], refs[-3:]
    slots[...] = jnp.zeros_like(slots)

    def act(slot, block):
        at = pl.ds(pl.multiple_of(block * (2 * size), 2 * size), 2 * size)
        value = pre_act[at, :].astype(jnp.float32)
        value = value * (0.5 * (1.0 + lax.erf(value * HALF_ROOT)))
        mean = 0.5 * merge_pairs(value, pair)
        slots[pl.ds(pl.multiple_of(slot * size, size), size), :] = mean

    each_exon(owners, exons, seen, nblocks, most, act)
    group = most * size
    for d, out in enumerate(outs):
        out[...] = slots[pl.ds(d * group, group), :].astype(out.dtype)


def front(owners, exons, pre_act, most, size, groups):
    rows, width = pre_act.shape
    return pl.pallas_call(
        functools.partial(
            front_kernel, nblocks=rows // 2 // size, most=most, size=size
        ),
        out_shape=[jax.ShapeDtypeStruct((most * size, width), jnp.bfloat16)] * groups,
        in_specs=[SMEM] * 2 + [VMEM],
        out_specs=[VMEM] * groups,
        scratch_shapes=[
            pltpu.VMEM((groups * most * size, width), jnp.float32),
            pair_scratch(2 * size, width),
            pltpu.SMEM((groups,), jnp.int32),
        ],
        cost_estimate=pl.CostEstimate(flops=10**10, bytes_accessed=40 * MIB, transcendentals=0),
        compiler_params=pltpu.CompilerParams(vmem_limit_bytes=32 * MIB),
    )(owners, exons, pre_act)


def plain_kernel(pre_act, out_grad, slope, plain, both):
    value = pre_act[...].astype(jnp.float32)
    normal = 0.5 * (1.0 + lax.erf(value * HALF_ROOT))
    slope[...] = normal + value * (jnp.exp(-0.5 * value * value) * DENSITY)
    pooled = make_pairs(out_grad[...].astype(jnp.float32) * 0.5, both)
    plain[...] = (pooled * slope[...]).astype(plain.dtype)


def plain_gradient(pre_act, out_grad):
    rows, width = pre_act.shape
    return pl.pallas_call(
        plain_kernel,
        out_shape=[
            jax.ShapeDtypeStruct((rows, width), jnp.float32),
            jax.ShapeDtypeStruct((rows, width), jnp.bfloat16),
        ],
        in_specs=[VMEM] * 2,
        out_specs=[VMEM] * 2,
        scratch_shapes=[pair_scratch(rows, width)],
        compiler_params=pltpu.CompilerParams(vmem_limit_bytes=32 * MIB),
    )(pre_act, out_grad)


def gain_kernel(owners, exons, out_grad, slope, plain, *refs, nblocks, most, size):
    splices, (grad, gain, held, both, seen) = refs[:-5], refs[-5:]
    gain[...] = out_grad[...].astype(jnp.float32)
    grad[...] = plain[...]
    base = 0
    for splice in splices:
        held[pl.ds(base, splice.shape[0]), :] = splice[...].astype(jnp.float32)
        base += splice.shape[0]

    def add(slot, block):
        at = pl.ds(pl.multiple_of(block * size, size), size)
        gain[at, :] += held[pl.ds(pl.multiple_of(slot * size, size), size), :]

    def renew(slot, block):
        pooled = 0.5 * gain[pl.ds(pl.multiple_of(block * size, size), size), :]
        pooled = make_pairs(pooled, both)
        at = pl.ds(pl.multiple_of(block * (2 * size), 2 * size), 2 * size)
        grad[at, :] = (pooled * slope[at, :]).astype(grad.dtype)

    each_exon(owners, exons, seen, nblocks, most, add)
    each_exon(owners, exons, seen, nblocks, most, renew)


def gained_gradient(owners, exons, out_grad, slope, plain, splices, most, size, groups):
    rows, width = slope.shape
    return pl.pallas_call(
        functools.partial(
            gain_kernel, nblocks=rows // 2 // size, most=most, size=size
        ),
        out_shape=jax.ShapeDtypeStruct((rows, width), jnp.bfloat16),
        in_specs=[SMEM] * 2 + [VMEM] * (3 + len(splices)),
        out_specs=VMEM,
        scratch_shapes=[
            pltpu.VMEM((rows // 2, width), jnp.float32),
            pltpu.VMEM((groups * most * size, width), jnp.float32),
            pair_scratch(2 * size, width),
            pltpu.SMEM((groups,), jnp.int32),
        ],
        compiler_params=pltpu.CompilerParams(vmem_limit_bytes=32 * MIB),
    )(owners, exons, out_grad, slope, plain, *splices)


def gathered_gradient(pre_act, out_grad, coverage_obs, owners, exon_blocks):
    rows, width = pre_act.shape
    nseq = lax.axis_size("seq")
    mine = lax.axis_index("seq")
    most, block = coverage_obs.shape[1:3]
    nblocks = rows // 2 // block
    counts = owners.shape[0]
    value = pre_act.astype(jnp.float32)
    normal = 0.5 * (1.0 + jax.scipy.special.erf(value * HALF_ROOT))
    slope = normal + value * jnp.exp(-0.5 * value * value) * DENSITY
    act = value * normal
    pooled = (0.5 * jnp.sum(act.reshape(rows // 2, 2, width), axis=1)).astype(jnp.bfloat16)
    order = jnp.arange(counts, dtype=jnp.int32)
    same = owners[:, None] == owners[None, :]
    rank = jnp.sum((same & (order[:, None] < order[None, :])).astype(jnp.int32), axis=0)
    dest = jnp.arange(nseq, dtype=jnp.int32)
    slots = jnp.arange(most, dtype=jnp.int32)
    route = (owners[None, None, :] == dest[:, None, None]) & (
        rank[None, None, :] == slots[None, :, None]
    )
    route = route.astype(jnp.float32).reshape(nseq * most, counts)
    on_mine = exon_blocks // nblocks == mine
    holds = jnp.any(on_mine, axis=1)
    local_block = jnp.sum(jnp.where(on_mine, exon_blocks % nblocks, 0), axis=1)
    select = (
        holds[:, None] & (local_block[:, None] == jnp.arange(nblocks, dtype=jnp.int32)[None, :])
    ).astype(jnp.float32)
    picker = jnp.dot(route, select, precision=lax.Precision.HIGHEST).astype(jnp.bfloat16)
    pieces = pooled.reshape(nblocks, block * width)
    outgoing = jnp.dot(picker, pieces, preferred_element_type=jnp.float32).astype(jnp.bfloat16)
    outgoing = outgoing.reshape(nseq, most, block, width)
    arrived = lax.all_to_all(outgoing, "seq", split_axis=0, concat_axis=0, tiled=True)
    coverage = jnp.sum(arrived.astype(jnp.float32), axis=0)
    splice = jnp.tanh(coverage - coverage_obs[0]).astype(jnp.bfloat16)
    returned = lax.all_gather(splice, "seq", axis=0).reshape(nseq * most, block * width)
    gained = jnp.dot(picker.T, returned, preferred_element_type=jnp.float32)
    pooled_grad = out_grad.astype(jnp.float32) + gained.reshape(rows // 2, width)
    return (jnp.repeat(pooled_grad, 2, axis=0) * 0.5 * slope).astype(jnp.bfloat16)


def local(x_saved, pre_act, out_grad, conv_w, coverage_obs, owners, exon_blocks):
    rows, width = x_saved.shape
    taps = conv_w.shape[1]
    nseq = lax.axis_size("seq")
    nch = lax.axis_size("ch")
    chunk = conv_w.shape[0] // nseq
    most = coverage_obs.shape[1]
    size = coverage_obs.shape[2]
    direct = nseq == nch == 4 and chunk == width and width % 128 == 0
    exons = exon_blocks.T
    weights = conv_w.transpose(1, 0, 2)
    target = coverage_obs[0].reshape(most * size, width)

    if not direct:
        pre_grad = gathered_gradient(pre_act, out_grad, coverage_obs, owners, exon_blocks)
        x_all = lax.all_gather(x_saved, "seq", axis=0, tiled=True)
        whole = lax.all_gather(pre_grad, "ch", axis=1, tiled=True)
        blocks = whole.reshape(rows, nseq, chunk).transpose(1, 0, 2)
        g_all = lax.all_to_all(blocks, "seq", 0, 0, tiled=True).reshape(nseq * rows, chunk)
        low = shift(whole[rows - PAD :], "seq", 1)
        high = shift(whole[:PAD], "seq", -1)
        in_grad = input_gradient([whole], low, high, weights, lambda: [0])
        total = nseq * rows
        w_grad = weight_gradient(
            [x_all], [g_all], lambda: ([PAD], [0], [0]), total, total, taps, total
        )
        return (in_grad, w_grad.transpose(1, 0, 2))

    outgoing = front(owners, exons, pre_act, most, size, nseq)
    arrived = [outgoing[0]] + [swap(outgoing[d], "seq", d) for d in range(1, nseq)]
    coverage = functools.reduce(jnp.add, [a.astype(jnp.float32) for a in arrived])
    slope, plain = plain_gradient(pre_act, out_grad)
    splice = jnp.tanh(coverage - target).astype(jnp.bfloat16)
    splices = [splice] + [swap(splice, "seq", d) for d in range(1, nseq)]
    pre_grad = gained_gradient(owners, exons, out_grad, slope, plain, splices, most, size, nseq)

    mine = lax.axis_index("seq")
    place = lax.axis_index("ch")
    up1, down1 = shift(x_saved, "seq", 1), shift(x_saved, "seq", -1)
    pre_grad, up1, down1 = after([pre_grad, up1, down1])

    far = swap(pre_grad, "ch", 2)
    near = swap(pre_grad, "ch", 1)
    up2, down2 = shift(up1, "seq", 1, 1), shift(down1, "seq", -1, 1)
    far, near, up2, down2 = after([far, near, up2, down2])
    parts = [pre_grad, near, far, swap(far, "ch", 1)]

    quarter = rows // nch

    def chosen(flipped, options):
        want = mine ^ flipped ^ place
        picked = options[0]
        for t in range(1, nch):
            picked = jnp.where(want == t, options[t], picked)
        return picked

    slices = [lax.dynamic_slice_in_dim(p, place * quarter, quarter, axis=0) for p in parts]
    got = [swap(chosen(d, slices), "seq", d) for d in range(1, nseq)]
    low = shift(jnp.concatenate([p[rows - PAD :] for p in parts], axis=1), "seq", 1)
    high = shift(jnp.concatenate([p[:PAD] for p in parts], axis=1), "seq", -1)

    def origins():
        return [(lax.axis_index("ch") ^ t) * width for t in range(nch)]

    in_grad = input_gradient(parts, low, high, weights, origins)
    crossing = after([jnp.concatenate(got), up2, down2], [in_grad])
    crossing, up2, down2 = crossing

    across = swap(crossing, "ch", 2)
    up3, down3 = shift(up2, "seq", 1, 2), shift(down2, "seq", -1, 2)
    partial = weight_gradient(
        [up1[rows - PAD :], x_saved, down1[:PAD]],
        [chosen(0, parts)],
        lambda: ([0, PAD, PAD + rows], [0], [0]),
        rows,
        rows,
        taps,
        rows,
        last=False,
    )
    across, partial = after([across, partial])
    beside = swap(crossing, "ch", 1)
    beyond = swap(across, "ch", 1)

    def layout():
        mine = lax.axis_index("seq")
        place = lax.axis_index("ch")
        x_rows = [PAD + mine * rows]
        for hop in range(1, nseq):
            low_at, high_at = mine - hop, mine + hop
            x_rows += [
                jnp.where(low_at >= 0, PAD + low_at * rows, -1),
                jnp.where(high_at < nseq, PAD + high_at * rows, -1),
            ]
        g_rows = []
        for tag in range(nch):
            g_rows += [(mine ^ d) * rows + (place ^ tag) * quarter for d in range(1, nseq)]
        return x_rows, g_rows, [(mine ^ d) * rows for d in range(1, nseq)]

    g_pieces = []
    for piece in (crossing, beside, across, beyond):
        g_pieces += [piece[d * quarter : (d + 1) * quarter] for d in range(nseq - 1)]
    w_grad = weight_gradient(
        [x_saved, up1, down1, up2, down2, up3, down3],
        g_pieces,
        layout,
        rows,
        (nseq - 1) * rows,
        taps,
        nseq * rows,
        before=partial,
    )
    return (in_grad, w_grad.transpose(1, 0, 2))


def solution(mesh):
    in_specs = (
        P(("grp", "seq"), "ch"),
        P(("grp", "seq"), "ch"),
        P(("grp", "seq"), "ch"),
        P(None, None, "ch"),
        P(("grp", "seq"), None, None, "ch"),
        P("grp"),
        P("grp", None),
    )
    out_specs = (P(("grp", "seq"), "ch"), P(("grp", "seq"), None, "ch"))
    return jax.shard_map(local, mesh=mesh, in_specs=in_specs, out_specs=out_specs, check_vma=False)
```

```python
import functools

import jax
import jax.numpy as jnp
from jax import lax
from jax.experimental import pallas as pl
from jax.experimental.pallas import tpu as pltpu
from jax.sharding import PartitionSpec as P

PAD = 16
MIB = 1024 * 1024
VMEM = pl.BlockSpec(memory_space=pltpu.VMEM)
SMEM = pl.BlockSpec(memory_space=pltpu.SMEM)
SOME = pl.BlockSpec(memory_space=pl.ANY)
HALF_ROOT = 0.7071067811865476
DENSITY = 0.3989422804014327
LANES = 128
LITTLE = pl.CostEstimate(flops=1000, bytes_accessed=1000, transcendentals=0)


def swap(block, axis, flip):
    count = lax.axis_size(axis)
    return lax.ppermute(block, axis, [(i, i ^ flip) for i in range(count)])


def shift(block, axis, step, first=0):
    count = lax.axis_size(axis)
    if step > 0:
        pairs = [(i, i + 1) for i in range(first, count - 1)]
    else:
        pairs = [(i + 1, i) for i in range(count - 1 - first)]
    return lax.ppermute(block, axis, pairs)


def after(values, others=()):
    return lax.optimization_barrier(tuple(values) + tuple(others))[: len(values)]


def input_kernel(*refs, taps, tile, pieces, origins):
    parts, (low, high, weights, out, wide, wbuf, sems) = refs[:pieces], refs[pieces:]
    rows = parts[0].shape[0]
    half = taps // 2
    copies = []
    base = 0
    for e, origin in enumerate(origins()):
        span = parts[e].shape[1]
        src = weights.at[:, pl.ds(pl.multiple_of(origin, 16), span), :]
        copy = pltpu.make_async_copy(src, wbuf.at[:, pl.ds(base, span), :], sems.at[e])
        copy.start()
        copies.append(copy)
        base += span
    base = 0
    for e in range(pieces):
        span = parts[e].shape[1]
        wide[pl.ds(0, PAD), pl.ds(base, span)] = low[:, pl.ds(base, span)]
        wide[pl.ds(PAD, rows), pl.ds(base, span)] = parts[e][...]
        wide[pl.ds(PAD + rows, PAD), pl.ds(base, span)] = high[:, pl.ds(base, span)]
        base += span
    for copy in copies:
        copy.wait()

    def body(step, carry):
        start = pl.multiple_of(step * tile, tile)
        block = wide[pl.ds(start, tile + 2 * PAD), :]
        total = None
        for tap in range(taps):
            term = jnp.dot(block, wbuf[tap], preferred_element_type=jnp.float32)
            first = PAD + half - tap
            term = term[first : first + tile]
            total = term if total is None else total + term
        out[pl.ds(start, tile), :] = total.astype(out.dtype)
        return carry

    lax.fori_loop(0, rows // tile, body, 0)


def input_gradient(parts, low, high, weights, origins):
    taps, chans, width = weights.shape
    rows = parts[0].shape[0]
    return pl.pallas_call(
        functools.partial(
            input_kernel, taps=taps, tile=min(256, rows), pieces=len(parts), origins=origins
        ),
        out_shape=jax.ShapeDtypeStruct((rows, width), jnp.bfloat16),
        in_specs=[VMEM] * (len(parts) + 2) + [SOME],
        out_specs=VMEM,
        scratch_shapes=[
            pltpu.VMEM((rows + 2 * PAD, chans), jnp.bfloat16),
            pltpu.VMEM((taps, chans, width), jnp.bfloat16),
            pltpu.SemaphoreType.DMA((len(parts),)),
        ],
        cost_estimate=LITTLE,
        compiler_params=pltpu.CompilerParams(vmem_limit_bytes=(20 if len(parts) > 1 else 32) * MIB),
    )(*parts, low, high, weights)


def weight_kernel(*refs, taps, tile, rows, size, nx, ng, layout, first):
    xs, gs, rest = refs[:nx], refs[nx : nx + ng], refs[nx + ng :]
    if first:
        out, xbuf, gbuf, acc, sems = rest
    else:
        before, out, xbuf, gbuf, acc, sems = rest
    half = taps // 2
    x_rows, g_rows, starts = layout()
    zeros = jnp.zeros((PAD, xbuf.shape[1]), xbuf.dtype)
    xbuf[pl.ds(0, PAD), :] = zeros
    xbuf[pl.ds(PAD + rows, PAD), :] = zeros
    pieces = [(src, xbuf, row) for src, row in zip(xs, x_rows)]
    pieces += [(src, gbuf, row) for src, row in zip(gs, g_rows)]

    def copy(at):
        src, dst, row = pieces[at]
        row = row if isinstance(row, int) else pl.multiple_of(row, 16)
        return pltpu.make_async_copy(src, dst.at[pl.ds(row, src.shape[0]), :], sems.at[at])

    def each(act):
        for at in range(nx + ng):
            row = pieces[at][2]
            if isinstance(row, int):
                act(at)
            else:
                pl.when(row >= 0)(functools.partial(act, at))

    each(lambda at: copy(at).start())
    acc[...] = jnp.zeros_like(acc) if first else before[...]
    each(lambda at: copy(at).wait())

    for begin in starts:

        def body(step, carry):
            start = begin + step * tile
            start = pl.multiple_of(start, 16)
            grad = gbuf[pl.ds(start, tile), :].T
            block = xbuf[pl.ds(start, tile + 2 * PAD), :].astype(jnp.float32)
            for tap in range(taps):
                at = PAD - half + tap
                moved = block[at : at + tile].astype(jnp.bfloat16)
                acc[tap] += jnp.dot(grad, moved, preferred_element_type=jnp.float32)
            return carry

        lax.fori_loop(0, size // tile, body, 0)
    out[...] = acc[...].astype(out.dtype)


def weight_gradient(xs, gs, layout, size, taps, rows, before=None, last=True, vmem=40):
    width, chunk = xs[0].shape[1], gs[0].shape[1]
    return pl.pallas_call(
        functools.partial(
            weight_kernel,
            taps=taps,
            tile=min(512, size),
            rows=rows,
            size=size,
            nx=len(xs),
            ng=len(gs),
            layout=layout,
            first=before is None,
        ),
        out_shape=jax.ShapeDtypeStruct(
            (taps, chunk, width), jnp.bfloat16 if last else jnp.float32
        ),
        in_specs=[SOME] * (len(xs) + len(gs)) + [VMEM] * (before is not None),
        out_specs=VMEM,
        scratch_shapes=[
            pltpu.VMEM((rows + 2 * PAD, width), jnp.bfloat16),
            pltpu.VMEM((rows, chunk), jnp.bfloat16),
            pltpu.VMEM((taps, chunk, width), jnp.float32),
            pltpu.SemaphoreType.DMA((len(xs) + len(gs),)),
        ],
        cost_estimate=LITTLE,
        compiler_params=pltpu.CompilerParams(vmem_limit_bytes=vmem * MIB),
    )(*xs, *gs, *([] if before is None else [before]))


def merge_pairs(value, scratch):
    size = value.shape[0] // 2
    sums = []
    for at in range(value.shape[1] // LANES):
        scratch[at] = value[:, at * LANES : (at + 1) * LANES]
        even = scratch[at, pl.ds(0, size, stride=2), :]
        sums.append(even + scratch[at, pl.ds(1, size, stride=2), :])
    return jnp.concatenate(sums, axis=1)


def make_pairs(value, scratch):
    size = value.shape[0]
    rows = []
    for at in range(value.shape[1] // LANES):
        part = value[:, at * LANES : (at + 1) * LANES]
        scratch[at, pl.ds(0, size, stride=2), :] = part
        scratch[at, pl.ds(1, size, stride=2), :] = part
        rows.append(scratch[at])
    return jnp.concatenate(rows, axis=1)


def pair_scratch(rows, width):
    return pltpu.VMEM((width // LANES, rows, LANES), jnp.float32)


def each_exon(owners, exons, seen, nblocks, most, act):
    mine = lax.axis_index("seq")
    span, count = exons.shape
    for i in range(seen.shape[0]):
        seen[i] = 0

    def body(t, carry):
        owner = owners[t]
        slot = (owner ^ mine) * most + seen[owner]
        seen[owner] += 1
        for e in range(span):
            where = exons[e, t]

            @pl.when(where // nblocks == mine)
            def _():
                act(slot, where % nblocks)

        return carry

    lax.fori_loop(0, count, body, 0)


def front_kernel(owners, exons, pre_act, *refs, nblocks, most, size):
    outs, (slots, pair, seen) = refs[:-3], refs[-3:]
    slots[...] = jnp.zeros_like(slots)

    def act(slot, block):
        at = pl.ds(pl.multiple_of(block * (2 * size), 2 * size), 2 * size)
        value = pre_act[at, :].astype(jnp.float32)
        value = value * (0.5 * (1.0 + lax.erf(value * HALF_ROOT)))
        mean = 0.5 * merge_pairs(value, pair)
        slots[pl.ds(pl.multiple_of(slot * size, size), size), :] = mean

    each_exon(owners, exons, seen, nblocks, most, act)
    group = most * size
    for d, out in enumerate(outs):
        out[...] = slots[pl.ds(d * group, group), :].astype(out.dtype)


def front(owners, exons, pre_act, most, size, groups):
    rows, width = pre_act.shape
    return pl.pallas_call(
        functools.partial(
            front_kernel, nblocks=rows // 2 // size, most=most, size=size
        ),
        out_shape=[jax.ShapeDtypeStruct((most * size, width), jnp.bfloat16)] * groups,
        in_specs=[SMEM] * 2 + [VMEM],
        out_specs=[VMEM] * groups,
        scratch_shapes=[
            pltpu.VMEM((groups * most * size, width), jnp.float32),
            pair_scratch(2 * size, width),
            pltpu.SMEM((groups,), jnp.int32),
        ],
        cost_estimate=LITTLE,
        compiler_params=pltpu.CompilerParams(vmem_limit_bytes=16 * MIB),
    )(owners, exons, pre_act)


def plain_kernel(pre_act, out_grad, slope, plain, both):
    value = pre_act[...].astype(jnp.float32)
    normal = 0.5 * (1.0 + lax.erf(value * HALF_ROOT))
    slope[...] = normal + value * (jnp.exp(-0.5 * value * value) * DENSITY)
    pooled = make_pairs(out_grad[...].astype(jnp.float32) * 0.5, both)
    plain[...] = (pooled * slope[...]).astype(plain.dtype)


def plain_gradient(pre_act, out_grad):
    rows, width = pre_act.shape
    return pl.pallas_call(
        plain_kernel,
        out_shape=[
            jax.ShapeDtypeStruct((rows, width), jnp.float32),
            jax.ShapeDtypeStruct((rows, width), jnp.bfloat16),
        ],
        in_specs=[VMEM] * 2,
        out_specs=[VMEM] * 2,
        scratch_shapes=[pair_scratch(rows, width)],
        cost_estimate=LITTLE,
        compiler_params=pltpu.CompilerParams(vmem_limit_bytes=16 * MIB),
    )(pre_act, out_grad)


def gain_kernel(owners, exons, out_grad, slope, plain, *refs, nblocks, most, size):
    splices, (grad, gain, held, both, seen) = refs[:-5], refs[-5:]
    gain[...] = out_grad[...].astype(jnp.float32)
    grad[...] = plain[...]
    base = 0
    for splice in splices:
        held[pl.ds(base, splice.shape[0]), :] = splice[...].astype(jnp.float32)
        base += splice.shape[0]

    def add(slot, block):
        at = pl.ds(pl.multiple_of(block * size, size), size)
        gain[at, :] += held[pl.ds(pl.multiple_of(slot * size, size), size), :]

    def renew(slot, block):
        pooled = 0.5 * gain[pl.ds(pl.multiple_of(block * size, size), size), :]
        pooled = make_pairs(pooled, both)
        at = pl.ds(pl.multiple_of(block * (2 * size), 2 * size), 2 * size)
        grad[at, :] = (pooled * slope[at, :]).astype(grad.dtype)

    each_exon(owners, exons, seen, nblocks, most, add)
    each_exon(owners, exons, seen, nblocks, most, renew)


def gained_gradient(owners, exons, out_grad, slope, plain, splices, most, size, groups):
    rows, width = slope.shape
    return pl.pallas_call(
        functools.partial(
            gain_kernel, nblocks=rows // 2 // size, most=most, size=size
        ),
        out_shape=jax.ShapeDtypeStruct((rows, width), jnp.bfloat16),
        in_specs=[SMEM] * 2 + [VMEM] * (3 + len(splices)),
        out_specs=VMEM,
        scratch_shapes=[
            pltpu.VMEM((rows // 2, width), jnp.float32),
            pltpu.VMEM((groups * most * size, width), jnp.float32),
            pair_scratch(2 * size, width),
            pltpu.SMEM((groups,), jnp.int32),
        ],
        compiler_params=pltpu.CompilerParams(vmem_limit_bytes=16 * MIB),
    )(owners, exons, out_grad, slope, plain, *splices)


def gathered_gradient(pre_act, out_grad, coverage_obs, owners, exon_blocks):
    rows, width = pre_act.shape
    nseq = lax.axis_size("seq")
    mine = lax.axis_index("seq")
    most, block = coverage_obs.shape[1:3]
    nblocks = rows // 2 // block
    counts = owners.shape[0]
    value = pre_act.astype(jnp.float32)
    normal = 0.5 * (1.0 + jax.scipy.special.erf(value * HALF_ROOT))
    slope = normal + value * jnp.exp(-0.5 * value * value) * DENSITY
    act = value * normal
    pooled = (0.5 * jnp.sum(act.reshape(rows // 2, 2, width), axis=1)).astype(jnp.bfloat16)
    order = jnp.arange(counts, dtype=jnp.int32)
    same = owners[:, None] == owners[None, :]
    rank = jnp.sum((same & (order[:, None] < order[None, :])).astype(jnp.int32), axis=0)
    dest = jnp.arange(nseq, dtype=jnp.int32)
    slots = jnp.arange(most, dtype=jnp.int32)
    route = (owners[None, None, :] == dest[:, None, None]) & (
        rank[None, None, :] == slots[None, :, None]
    )
    route = route.astype(jnp.float32).reshape(nseq * most, counts)
    on_mine = exon_blocks // nblocks == mine
    holds = jnp.any(on_mine, axis=1)
    local_block = jnp.sum(jnp.where(on_mine, exon_blocks % nblocks, 0), axis=1)
    select = (
        holds[:, None] & (local_block[:, None] == jnp.arange(nblocks, dtype=jnp.int32)[None, :])
    ).astype(jnp.float32)
    picker = jnp.dot(route, select, precision=lax.Precision.HIGHEST).astype(jnp.bfloat16)
    pieces = pooled.reshape(nblocks, block * width)
    outgoing = jnp.dot(picker, pieces, preferred_element_type=jnp.float32).astype(jnp.bfloat16)
    outgoing = outgoing.reshape(nseq, most, block, width)
    arrived = lax.all_to_all(outgoing, "seq", split_axis=0, concat_axis=0, tiled=True)
    coverage = jnp.sum(arrived.astype(jnp.float32), axis=0)
    splice = jnp.tanh(coverage - coverage_obs[0]).astype(jnp.bfloat16)
    returned = lax.all_gather(splice, "seq", axis=0).reshape(nseq * most, block * width)
    gained = jnp.dot(picker.T, returned, preferred_element_type=jnp.float32)
    pooled_grad = out_grad.astype(jnp.float32) + gained.reshape(rows // 2, width)
    return (jnp.repeat(pooled_grad, 2, axis=0) * 0.5 * slope).astype(jnp.bfloat16)


def local(x_saved, pre_act, out_grad, conv_w, coverage_obs, owners, exon_blocks):
    rows, width = x_saved.shape
    taps = conv_w.shape[1]
    nseq = lax.axis_size("seq")
    nch = lax.axis_size("ch")
    chunk = conv_w.shape[0] // nseq
    most = coverage_obs.shape[1]
    size = coverage_obs.shape[2]
    direct = nseq == nch == 4 and chunk == width and width % 128 == 0
    exons = exon_blocks.T
    weights = conv_w.transpose(1, 0, 2)
    target = coverage_obs[0].reshape(most * size, width)

    if not direct:
        pre_grad = gathered_gradient(pre_act, out_grad, coverage_obs, owners, exon_blocks)
        x_all = lax.all_gather(x_saved, "seq", axis=0, tiled=True)
        whole = lax.all_gather(pre_grad, "ch", axis=1, tiled=True)
        blocks = whole.reshape(rows, nseq, chunk).transpose(1, 0, 2)
        g_all = lax.all_to_all(blocks, "seq", 0, 0, tiled=True).reshape(nseq * rows, chunk)
        low = shift(whole[rows - PAD :], "seq", 1)
        high = shift(whole[:PAD], "seq", -1)
        in_grad = input_gradient([whole], low, high, weights, lambda: [0])
        total = nseq * rows
        w_grad = weight_gradient(
            [x_all], [g_all], lambda: ([PAD], [0], [0]), total, taps, total
        )
        return (in_grad, w_grad.transpose(1, 0, 2))

    mine = lax.axis_index("seq")
    place = lax.axis_index("ch")
    outgoing = front(owners, exons, pre_act, most, size, nseq)
    slope, plain = plain_gradient(*after([pre_act, out_grad], outgoing))
    (source,) = after([x_saved], [plain])
    up1, down1 = shift(source, "seq", 1), shift(source, "seq", -1)
    arrived = [outgoing[0]] + [swap(outgoing[d], "seq", d) for d in range(1, nseq)]
    coverage = functools.reduce(jnp.add, [a.astype(jnp.float32) for a in arrived])
    splice = jnp.tanh(coverage - target).astype(jnp.bfloat16)
    splices = [splice] + [swap(splice, "seq", d) for d in range(1, nseq)]
    pre_grad = gained_gradient(owners, exons, out_grad, slope, plain, splices, most, size, nseq)
    pre_grad, up1, down1 = after([pre_grad, up1, down1])

    far = swap(pre_grad, "ch", 2)
    near = swap(pre_grad, "ch", 1)
    up2, down2 = shift(up1, "seq", 1, 1), shift(down1, "seq", -1, 1)
    far, near, up2, down2 = after([far, near, up2, down2])
    parts = after([pre_grad, near, far, swap(far, "ch", 1)])

    quarter = rows // nch
    half = taps // 2

    def chosen(flipped, options):
        want = mine ^ flipped ^ place
        picked = options[0]
        for t in range(1, nch):
            picked = jnp.where(want == t, options[t], picked)
        return picked

    slices = [lax.dynamic_slice_in_dim(p, place * quarter, quarter, axis=0) for p in parts]
    heads = jnp.concatenate([p[:half] for p in parts])
    tails = jnp.concatenate([p[rows - half :] for p in parts])
    spare = jnp.zeros((-len(heads) % PAD, width), jnp.bfloat16)
    sent = [chosen(d, slices) for d in range(1, nseq)]
    for d in (1, 3):
        edge = jnp.where((mine ^ d) > mine, tails, heads)
        sent[d - 1] = jnp.concatenate([sent[d - 1], edge, spare])
    *sent, up2, down2 = after([*sent, up2, down2])
    got = [swap(block, "seq", d) for d, block in zip(range(1, nseq), sent)]
    up3, down3 = shift(up2, "seq", 1, 2), shift(down2, "seq", -1, 2)

    partial = weight_gradient(
        [up1[rows - PAD :], x_saved, down1[:PAD]],
        [chosen(0, parts)],
        lambda: ([0, PAD, PAD + rows], [0], [0]),
        rows,
        taps,
        rows,
        last=False,
        vmem=20,
    )
    *got, partial = after([*got, partial])

    crossing = jnp.concatenate([block[:quarter] for block in got])
    across = swap(crossing, "ch", 2)
    beside = swap(crossing, "ch", 1)
    edges = [got[d - 1][quarter : quarter + len(heads)] for d in (1, 3)]
    edges = [jnp.concatenate(jnp.split(e, nch), axis=1) for e in edges]
    nothing = jnp.zeros_like(edges[0])
    low = jnp.where(mine % 2 == 1, edges[0], jnp.where(mine == 2, edges[1], nothing))
    high = jnp.where(mine % 2 == 0, edges[0], jnp.where(mine == 1, edges[1], nothing))
    low = jnp.pad(low, ((PAD - half, 0), (0, 0)))
    high = jnp.pad(high, ((0, PAD - half), (0, 0)))

    def origins():
        return [(lax.axis_index("ch") ^ t) * width for t in range(nch)]

    in_grad = input_gradient(parts, low, high, weights, origins)
    across, in_grad, up3, down3 = after([across, in_grad, up3, down3])
    beyond = swap(across, "ch", 1)

    def layout():
        mine = lax.axis_index("seq")
        place = lax.axis_index("ch")
        x_rows = [PAD + mine * rows]
        for hop in range(1, nseq):
            low_at, high_at = mine - hop, mine + hop
            x_rows += [
                jnp.where(low_at >= 0, PAD + low_at * rows, -1),
                jnp.where(high_at < nseq, PAD + high_at * rows, -1),
            ]
        g_rows = []
        for tag in range(nch):
            g_rows += [(mine ^ d) * rows + (place ^ tag) * quarter for d in range(1, nseq)]
        return x_rows, g_rows, [(mine ^ d) * rows for d in range(1, nseq)]

    g_pieces = []
    for piece in (crossing, beside, across, beyond):
        g_pieces += [piece[d * quarter : (d + 1) * quarter] for d in range(nseq - 1)]
    w_grad = weight_gradient(
        [x_saved, up1, down1, up2, down2, up3, down3],
        g_pieces,
        layout,
        rows,
        taps,
        nseq * rows,
        before=partial,
        vmem=24,
    )
    return (in_grad, w_grad.transpose(1, 0, 2))


def solution(mesh):
    in_specs = (
        P(("grp", "seq"), "ch"),
        P(("grp", "seq"), "ch"),
        P(("grp", "seq"), "ch"),
        P(None, None, "ch"),
        P(("grp", "seq"), None, None, "ch"),
        P("grp"),
        P("grp", None),
    )
    out_specs = (P(("grp", "seq"), "ch"), P(("grp", "seq"), None, "ch"))
    return jax.shard_map(local, mesh=mesh, in_specs=in_specs, out_specs=out_specs, check_vma=False)
```

```python
import functools

import jax
import jax.numpy as jnp
from jax import lax
from jax.experimental import pallas as pl
from jax.experimental.pallas import tpu as pltpu
from jax.sharding import PartitionSpec as P

PAD = 16
MIB = 1024 * 1024
VMEM = pl.BlockSpec(memory_space=pltpu.VMEM)
SMEM = pl.BlockSpec(memory_space=pltpu.SMEM)
SOME = pl.BlockSpec(memory_space=pl.ANY)
HALF_ROOT = 0.7071067811865476
DENSITY = 0.3989422804014327
LANES = 128
LITTLE = pl.CostEstimate(flops=1000, bytes_accessed=1000, transcendentals=0)


def swap(block, axis, flip):
    count = lax.axis_size(axis)
    return lax.ppermute(block, axis, [(i, i ^ flip) for i in range(count)])


def shift(block, axis, step, first=0):
    count = lax.axis_size(axis)
    if step > 0:
        pairs = [(i, i + 1) for i in range(first, count - 1)]
    else:
        pairs = [(i + 1, i) for i in range(count - 1 - first)]
    return lax.ppermute(block, axis, pairs)


def after(values, others=()):
    return lax.optimization_barrier(tuple(values) + tuple(others))[: len(values)]


def input_kernel(part, low, high, weights, out, block):
    taps = weights.shape[0]
    rows = part.shape[0]
    half = taps // 2
    block[pl.ds(0, PAD), :] = low[...]
    block[pl.ds(PAD, rows), :] = part[...]
    block[pl.ds(PAD + rows, PAD), :] = high[...]
    tile = min(256, rows)

    def body(step, carry):
        start = pl.multiple_of(step * tile, tile)
        rows_in = block[pl.ds(start, tile + 2 * PAD), :]
        total = None
        for tap in range(taps):
            term = jnp.dot(rows_in, weights[tap], preferred_element_type=jnp.float32)
            first = PAD + half - tap
            term = term[first : first + tile]
            total = term if total is None else total + term
        out[pl.ds(start, tile), :] = total.astype(out.dtype)
        return carry

    lax.fori_loop(0, rows // tile, body, 0)


def input_gradient(part, low, high, weights):
    taps, chans, width = weights.shape
    rows = part.shape[0]
    return pl.pallas_call(
        input_kernel,
        out_shape=jax.ShapeDtypeStruct((rows, width), jnp.bfloat16),
        in_specs=[VMEM] * 4,
        out_specs=VMEM,
        scratch_shapes=[pltpu.VMEM((rows + 2 * PAD, chans), jnp.bfloat16)],
        compiler_params=pltpu.CompilerParams(vmem_limit_bytes=32 * MIB),
    )(part, low, high, weights)


def pieces_kernel(*refs, taps, tile, pieces):
    parts, (low, high, weights, out, block) = refs[:pieces], refs[pieces:]
    rows = parts[0].shape[0]
    width = out.shape[1]
    half = taps // 2
    base = 0
    for part in parts:
        span = pl.ds(base, part.shape[1])
        block[pl.ds(0, PAD), span] = low[:, span]
        block[pl.ds(PAD, rows), span] = part[...]
        block[pl.ds(PAD + rows, PAD), span] = high[:, span]
        base += part.shape[1]

    def body(step, carry):
        start = pl.multiple_of(step * tile, tile)
        terms = jnp.dot(
            block[pl.ds(start, tile + 2 * PAD), :],
            weights[...],
            preferred_element_type=jnp.float32,
        )
        total = None
        for tap in range(taps):
            first = PAD + half - tap
            term = terms[first : first + tile, tap * width : (tap + 1) * width]
            total = term if total is None else total + term
        out[pl.ds(start, tile), :] = total.astype(out.dtype)
        return carry

    lax.fori_loop(0, rows // tile, body, 0)


def pieces_gradient(parts, low, high, weights, taps):
    chans = weights.shape[0]
    width = weights.shape[1] // taps
    rows = parts[0].shape[0]
    return pl.pallas_call(
        functools.partial(pieces_kernel, taps=taps, tile=min(512, rows), pieces=len(parts)),
        out_shape=jax.ShapeDtypeStruct((rows, width), jnp.bfloat16),
        in_specs=[VMEM] * (len(parts) + 3),
        out_specs=VMEM,
        scratch_shapes=[pltpu.VMEM((rows + 2 * PAD, chans), jnp.bfloat16)],
        cost_estimate=LITTLE,
        compiler_params=pltpu.CompilerParams(vmem_limit_bytes=24 * MIB),
    )(*parts, low, high, weights)


def weight_kernel(*refs, taps, tile, rows, size, nx, ng, layout, first, last, origins):
    xs, gs, rest = refs[:nx], refs[nx : nx + ng], list(refs[nx + ng :])
    before = None if first else rest.pop(0)
    weights = rest.pop(0) if origins else None
    out = rest.pop(0)
    laid = rest.pop(0) if origins else None
    xbuf, gbuf, acc, sems = rest
    width = xbuf.shape[1]
    half = taps // 2
    x_rows, g_rows, starts = layout()
    zeros = jnp.zeros((PAD, width), xbuf.dtype)
    xbuf[pl.ds(0, PAD), :] = zeros
    xbuf[pl.ds(PAD + rows, PAD), :] = zeros
    pieces = [(src, xbuf, row) for src, row in zip(xs, x_rows)]
    pieces += [(src, gbuf, row) for src, row in zip(gs, g_rows)]

    def copy(at):
        src, dst, row = pieces[at]
        row = row if isinstance(row, int) else pl.multiple_of(row, 16)
        return pltpu.make_async_copy(src, dst.at[pl.ds(row, src.shape[0]), :], sems.at[at])

    def each(act):
        for at in range(nx + ng):
            row = pieces[at][2]
            if isinstance(row, int):
                act(at)
            else:
                pl.when(row >= 0)(functools.partial(act, at))

    each(lambda at: copy(at).start())
    moves = []
    if origins:
        where = origins()
        span = weights.shape[1] // len(where)
        for e, origin in enumerate(where):
            for tap in range(taps):
                moves.append(
                    pltpu.make_async_copy(
                        weights.at[tap, pl.ds(pl.multiple_of(origin, 16), span), :],
                        laid.at[pl.ds(e * span, span), pl.ds(tap * width, width)],
                        sems.at[nx + ng + len(moves)],
                    )
                )
        for move in moves:
            move.start()
    acc[...] = jnp.zeros_like(acc) if first else before[...]
    each(lambda at: copy(at).wait())

    for begin in starts:

        def body(step, carry):
            start = pl.multiple_of(begin + step * tile, 16)
            grad = gbuf[pl.ds(start, tile), :].T
            block = xbuf[pl.ds(start, tile + 2 * PAD), :].astype(jnp.float32)
            moved = []
            for tap in range(taps):
                at = PAD - half + tap
                moved.append(block[at : at + tile].astype(jnp.bfloat16))
            if width % LANES:
                for tap in range(taps):
                    acc[tap] += jnp.dot(grad, moved[tap], preferred_element_type=jnp.float32)
            else:
                moved = jnp.concatenate(moved, axis=1)
                acc[...] += jnp.dot(grad, moved, preferred_element_type=jnp.float32)
            return carry

        lax.fori_loop(0, size // tile, body, 0)
    if last and width % LANES == 0:
        for tap in range(taps):
            out[tap] = acc[:, tap * width : (tap + 1) * width].astype(out.dtype)
    else:
        out[...] = acc[...].astype(out.dtype)
    for move in moves:
        move.wait()


def weight_gradient(
    xs, gs, layout, size, taps, rows, before=None, last=True, vmem=40, weights=None, origins=None
):
    width, chunk = xs[0].shape[1], gs[0].shape[1]
    split = (taps, chunk, width)
    joined = split if width % LANES else (chunk, taps * width)
    out_shape = [
        jax.ShapeDtypeStruct(split, jnp.bfloat16)
        if last
        else jax.ShapeDtypeStruct(joined, jnp.float32)
    ]
    moves = 0
    if origins:
        moves = taps * 4
        out_shape.append(
            jax.ShapeDtypeStruct((weights.shape[1], taps * width), weights.dtype)
        )
    return pl.pallas_call(
        functools.partial(
            weight_kernel,
            taps=taps,
            tile=min(1024, size) if width % LANES == 0 else min(512, size),
            rows=rows,
            size=size,
            nx=len(xs),
            ng=len(gs),
            layout=layout,
            first=before is None,
            last=last,
            origins=origins,
        ),
        out_shape=out_shape,
        in_specs=[SOME] * (len(xs) + len(gs))
        + [VMEM] * (before is not None)
        + [SOME] * (weights is not None),
        out_specs=[VMEM] * len(out_shape),
        scratch_shapes=[
            pltpu.VMEM((rows + 2 * PAD, width), jnp.bfloat16),
            pltpu.VMEM((rows, chunk), jnp.bfloat16),
            pltpu.VMEM(joined, jnp.float32),
            pltpu.SemaphoreType.DMA((len(xs) + len(gs) + moves,)),
        ],
        cost_estimate=LITTLE,
        compiler_params=pltpu.CompilerParams(vmem_limit_bytes=vmem * MIB),
    )(
        *xs,
        *gs,
        *([] if before is None else [before]),
        *([] if weights is None else [weights]),
    )


def merge_pairs(value, scratch):
    size = value.shape[0] // 2
    sums = []
    for at in range(value.shape[1] // LANES):
        scratch[at] = value[:, at * LANES : (at + 1) * LANES]
        even = scratch[at, pl.ds(0, size, stride=2), :]
        sums.append(even + scratch[at, pl.ds(1, size, stride=2), :])
    return jnp.concatenate(sums, axis=1)


def make_pairs(value, scratch):
    size = value.shape[0]
    rows = []
    for at in range(value.shape[1] // LANES):
        part = value[:, at * LANES : (at + 1) * LANES]
        scratch[at, pl.ds(0, size, stride=2), :] = part
        scratch[at, pl.ds(1, size, stride=2), :] = part
        rows.append(scratch[at])
    return jnp.concatenate(rows, axis=1)


def pair_scratch(rows, width):
    return pltpu.VMEM((width // LANES, rows, LANES), jnp.float32)


def each_exon(owners, exons, seen, nblocks, most, act):
    mine = lax.axis_index("seq")
    span, count = exons.shape
    for i in range(seen.shape[0]):
        seen[i] = 0

    def body(t, carry):
        owner = owners[t]
        slot = (owner ^ mine) * most + seen[owner]
        seen[owner] += 1
        for e in range(span):
            where = exons[e, t]

            @pl.when(where // nblocks == mine)
            def _():
                act(slot, where % nblocks)

        return carry

    lax.fori_loop(0, count, body, 0)


def front_kernel(owners, exons, pre_act, *refs, nblocks, most, size):
    outs, (slots, pair, seen) = refs[:-3], refs[-3:]
    slots[...] = jnp.zeros_like(slots)

    def act(slot, block):
        at = pl.ds(pl.multiple_of(block * (2 * size), 2 * size), 2 * size)
        value = pre_act[at, :].astype(jnp.float32)
        value = value * (0.5 * (1.0 + lax.erf(value * HALF_ROOT)))
        mean = 0.5 * merge_pairs(value, pair)
        slots[pl.ds(pl.multiple_of(slot * size, size), size), :] = mean

    each_exon(owners, exons, seen, nblocks, most, act)
    group = most * size
    for d, out in enumerate(outs):
        out[...] = slots[pl.ds(d * group, group), :].astype(out.dtype)


def front(owners, exons, pre_act, most, size, groups):
    rows, width = pre_act.shape
    return pl.pallas_call(
        functools.partial(
            front_kernel, nblocks=rows // 2 // size, most=most, size=size
        ),
        out_shape=[jax.ShapeDtypeStruct((most * size, width), jnp.bfloat16)] * groups,
        in_specs=[SMEM] * 2 + [VMEM],
        out_specs=[VMEM] * groups,
        scratch_shapes=[
            pltpu.VMEM((groups * most * size, width), jnp.float32),
            pair_scratch(2 * size, width),
            pltpu.SMEM((groups,), jnp.int32),
        ],
        cost_estimate=LITTLE,
        compiler_params=pltpu.CompilerParams(vmem_limit_bytes=16 * MIB),
    )(owners, exons, pre_act)


def plain_kernel(pre_act, out_grad, slope, plain, both):
    value = pre_act[...].astype(jnp.float32)
    normal = 0.5 * (1.0 + lax.erf(value * HALF_ROOT))
    slope[...] = normal + value * (jnp.exp(-0.5 * value * value) * DENSITY)
    pooled = make_pairs(out_grad[...].astype(jnp.float32) * 0.5, both)
    plain[...] = (pooled * slope[...]).astype(plain.dtype)


def plain_gradient(pre_act, out_grad):
    rows, width = pre_act.shape
    return pl.pallas_call(
        plain_kernel,
        out_shape=[
            jax.ShapeDtypeStruct((rows, width), jnp.float32),
            jax.ShapeDtypeStruct((rows, width), jnp.bfloat16),
        ],
        in_specs=[VMEM] * 2,
        out_specs=[VMEM] * 2,
        scratch_shapes=[pair_scratch(rows, width)],
        cost_estimate=LITTLE,
        compiler_params=pltpu.CompilerParams(vmem_limit_bytes=16 * MIB),
    )(pre_act, out_grad)


def gain_kernel(owners, exons, out_grad, slope, plain, *refs, nblocks, most, size):
    splices, (grad, gain, held, both, seen) = refs[:-5], refs[-5:]
    gain[...] = out_grad[...].astype(jnp.float32)
    grad[...] = plain[...]
    base = 0
    for splice in splices:
        held[pl.ds(base, splice.shape[0]), :] = splice[...].astype(jnp.float32)
        base += splice.shape[0]

    def add(slot, block):
        at = pl.ds(pl.multiple_of(block * size, size), size)
        gain[at, :] += held[pl.ds(pl.multiple_of(slot * size, size), size), :]

    def renew(slot, block):
        pooled = 0.5 * gain[pl.ds(pl.multiple_of(block * size, size), size), :]
        pooled = make_pairs(pooled, both)
        at = pl.ds(pl.multiple_of(block * (2 * size), 2 * size), 2 * size)
        grad[at, :] = (pooled * slope[at, :]).astype(grad.dtype)

    each_exon(owners, exons, seen, nblocks, most, add)
    each_exon(owners, exons, seen, nblocks, most, renew)


def gained_gradient(owners, exons, out_grad, slope, plain, splices, most, size, groups):
    rows, width = slope.shape
    return pl.pallas_call(
        functools.partial(
            gain_kernel, nblocks=rows // 2 // size, most=most, size=size
        ),
        out_shape=jax.ShapeDtypeStruct((rows, width), jnp.bfloat16),
        in_specs=[SMEM] * 2 + [VMEM] * (3 + len(splices)),
        out_specs=VMEM,
        scratch_shapes=[
            pltpu.VMEM((rows // 2, width), jnp.float32),
            pltpu.VMEM((groups * most * size, width), jnp.float32),
            pair_scratch(2 * size, width),
            pltpu.SMEM((groups,), jnp.int32),
        ],
        compiler_params=pltpu.CompilerParams(vmem_limit_bytes=16 * MIB),
    )(owners, exons, out_grad, slope, plain, *splices)


def gathered_gradient(pre_act, out_grad, coverage_obs, owners, exon_blocks):
    rows, width = pre_act.shape
    nseq = lax.axis_size("seq")
    mine = lax.axis_index("seq")
    most, block = coverage_obs.shape[1:3]
    nblocks = rows // 2 // block
    counts = owners.shape[0]
    value = pre_act.astype(jnp.float32)
    normal = 0.5 * (1.0 + jax.scipy.special.erf(value * HALF_ROOT))
    slope = normal + value * jnp.exp(-0.5 * value * value) * DENSITY
    act = value * normal
    pooled = (0.5 * jnp.sum(act.reshape(rows // 2, 2, width), axis=1)).astype(jnp.bfloat16)
    order = jnp.arange(counts, dtype=jnp.int32)
    same = owners[:, None] == owners[None, :]
    rank = jnp.sum((same & (order[:, None] < order[None, :])).astype(jnp.int32), axis=0)
    dest = jnp.arange(nseq, dtype=jnp.int32)
    slots = jnp.arange(most, dtype=jnp.int32)
    route = (owners[None, None, :] == dest[:, None, None]) & (
        rank[None, None, :] == slots[None, :, None]
    )
    route = route.astype(jnp.float32).reshape(nseq * most, counts)
    on_mine = exon_blocks // nblocks == mine
    holds = jnp.any(on_mine, axis=1)
    local_block = jnp.sum(jnp.where(on_mine, exon_blocks % nblocks, 0), axis=1)
    select = (
        holds[:, None] & (local_block[:, None] == jnp.arange(nblocks, dtype=jnp.int32)[None, :])
    ).astype(jnp.float32)
    picker = jnp.dot(route, select, precision=lax.Precision.HIGHEST).astype(jnp.bfloat16)
    pieces = pooled.reshape(nblocks, block * width)
    outgoing = jnp.dot(picker, pieces, preferred_element_type=jnp.float32).astype(jnp.bfloat16)
    outgoing = outgoing.reshape(nseq, most, block, width)
    arrived = lax.all_to_all(outgoing, "seq", split_axis=0, concat_axis=0, tiled=True)
    coverage = jnp.sum(arrived.astype(jnp.float32), axis=0)
    splice = jnp.tanh(coverage - coverage_obs[0]).astype(jnp.bfloat16)
    returned = lax.all_gather(splice, "seq", axis=0).reshape(nseq * most, block * width)
    gained = jnp.dot(picker.T, returned, preferred_element_type=jnp.float32)
    pooled_grad = out_grad.astype(jnp.float32) + gained.reshape(rows // 2, width)
    return (jnp.repeat(pooled_grad, 2, axis=0) * 0.5 * slope).astype(jnp.bfloat16)


def local(x_saved, pre_act, out_grad, conv_w, coverage_obs, owners, exon_blocks):
    rows, width = x_saved.shape
    taps = conv_w.shape[1]
    nseq = lax.axis_size("seq")
    nch = lax.axis_size("ch")
    chunk = conv_w.shape[0] // nseq
    most = coverage_obs.shape[1]
    size = coverage_obs.shape[2]
    direct = nseq == nch == 4 and chunk == width and width % 128 == 0
    exons = exon_blocks.T
    weights = conv_w.transpose(1, 0, 2)
    target = coverage_obs[0].reshape(most * size, width)

    if not direct:
        pre_grad = gathered_gradient(pre_act, out_grad, coverage_obs, owners, exon_blocks)
        x_all = lax.all_gather(x_saved, "seq", axis=0, tiled=True)
        whole = lax.all_gather(pre_grad, "ch", axis=1, tiled=True)
        blocks = whole.reshape(rows, nseq, chunk).transpose(1, 0, 2)
        g_all = lax.all_to_all(blocks, "seq", 0, 0, tiled=True).reshape(nseq * rows, chunk)
        low = shift(whole[rows - PAD :], "seq", 1)
        high = shift(whole[:PAD], "seq", -1)
        in_grad = input_gradient(whole, low, high, weights)
        total = nseq * rows
        (w_grad,) = weight_gradient(
            [x_all], [g_all], lambda: ([PAD], [0], [0]), total, taps, total
        )
        return (in_grad, w_grad.transpose(1, 0, 2))

    mine = lax.axis_index("seq")
    place = lax.axis_index("ch")
    outgoing = front(owners, exons, pre_act, most, size, nseq)
    slope, plain = plain_gradient(*after([pre_act, out_grad], outgoing))
    arrived = [outgoing[0]] + [swap(outgoing[d], "seq", d) for d in range(1, nseq)]
    coverage = functools.reduce(jnp.add, [a.astype(jnp.float32) for a in arrived])
    splice = jnp.tanh(coverage - target).astype(jnp.bfloat16)
    splices = [splice] + [swap(splice, "seq", d) for d in range(1, nseq)]
    pre_grad = gained_gradient(owners, exons, out_grad, slope, plain, splices, most, size, nseq)
    (source,) = after([x_saved], splices[1:])
    up1, down1 = shift(source, "seq", 1), shift(source, "seq", -1)

    far = swap(pre_grad, "ch", 2)
    near = swap(pre_grad, "ch", 1)
    up2, down2 = shift(up1, "seq", 1, 1), shift(down1, "seq", -1, 1)
    far, near, up2, down2 = after([far, near, up2, down2])
    parts = after([pre_grad, near, far, swap(far, "ch", 1)])

    quarter = rows // nch
    half = taps // 2

    def chosen(flipped, options):
        want = mine ^ flipped ^ place
        picked = options[0]
        for t in range(1, nch):
            picked = jnp.where(want == t, options[t], picked)
        return picked

    slices = [lax.dynamic_slice_in_dim(p, place * quarter, quarter, axis=0) for p in parts]
    heads = jnp.concatenate([p[:half] for p in parts])
    tails = jnp.concatenate([p[rows - half :] for p in parts])
    spare = jnp.zeros((-len(heads) % PAD, width), jnp.bfloat16)
    sent = [chosen(d, slices) for d in range(1, nseq)]
    for d in (1, 3):
        edge = jnp.where((mine ^ d) > mine, tails, heads)
        sent[d - 1] = jnp.concatenate([sent[d - 1], edge, spare])
    *sent, up2, down2 = after([*sent, up2, down2])
    got = [swap(block, "seq", d) for d, block in zip(range(1, nseq), sent)]
    up3, down3 = shift(up2, "seq", 1, 2), shift(down2, "seq", -1, 2)

    def origins():
        return [(lax.axis_index("ch") ^ t) * width for t in range(nch)]

    partial, laid = weight_gradient(
        [up1[rows - PAD :], x_saved, down1[:PAD]],
        [chosen(0, parts)],
        lambda: ([0, PAD, PAD + rows], [0], [0]),
        rows,
        taps,
        rows,
        last=False,
        vmem=24,
        weights=weights,
        origins=origins,
    )
    *got, partial = after([*got, partial])

    crossing = jnp.concatenate([block[:quarter] for block in got])
    across = swap(crossing, "ch", 2)
    beside = swap(crossing, "ch", 1)
    edges = [got[d - 1][quarter : quarter + len(heads)] for d in (1, 3)]
    edges = [jnp.concatenate(jnp.split(e, nch), axis=1) for e in edges]
    nothing = jnp.zeros_like(edges[0])
    low = jnp.where(mine % 2 == 1, edges[0], jnp.where(mine == 2, edges[1], nothing))
    high = jnp.where(mine % 2 == 0, edges[0], jnp.where(mine == 1, edges[1], nothing))
    low = jnp.pad(low, ((PAD - half, 0), (0, 0)))
    high = jnp.pad(high, ((0, PAD - half), (0, 0)))

    in_grad = pieces_gradient(parts, low, high, laid, taps)
    across, in_grad, up3, down3 = after([across, in_grad, up3, down3])
    beyond = swap(across, "ch", 1)

    def layout():
        mine = lax.axis_index("seq")
        place = lax.axis_index("ch")
        x_rows = [PAD + mine * rows]
        for hop in range(1, nseq):
            low_at, high_at = mine - hop, mine + hop
            x_rows += [
                jnp.where(low_at >= 0, PAD + low_at * rows, -1),
                jnp.where(high_at < nseq, PAD + high_at * rows, -1),
            ]
        g_rows = []
        for tag in range(nch):
            g_rows += [(mine ^ d) * rows + (place ^ tag) * quarter for d in range(1, nseq)]
        return x_rows, g_rows, [(mine ^ d) * rows for d in range(1, nseq)]

    g_pieces = []
    for piece in (crossing, beside, across, beyond):
        g_pieces += [piece[d * quarter : (d + 1) * quarter] for d in range(nseq - 1)]
    (w_grad,) = weight_gradient(
        [x_saved, up1, down1, up2, down2, up3, down3],
        g_pieces,
        layout,
        rows,
        taps,
        nseq * rows,
        before=partial,
        vmem=32,
    )
    return (in_grad, w_grad.transpose(1, 0, 2))


def solution(mesh):
    in_specs = (
        P(("grp", "seq"), "ch"),
        P(("grp", "seq"), "ch"),
        P(("grp", "seq"), "ch"),
        P(None, None, "ch"),
        P(("grp", "seq"), None, None, "ch"),
        P("grp"),
        P("grp", None),
    )
    out_specs = (P(("grp", "seq"), "ch"), P(("grp", "seq"), None, "ch"))
    return jax.shard_map(local, mesh=mesh, in_specs=in_specs, out_specs=out_specs, check_vma=False)
```

```python
import functools

import jax
import jax.numpy as jnp
from jax import lax
from jax.experimental import pallas as pl
from jax.experimental.pallas import tpu as pltpu
from jax.sharding import PartitionSpec as P

PAD = 16
MIB = 1024 * 1024
VMEM = pl.BlockSpec(memory_space=pltpu.VMEM)
SMEM = pl.BlockSpec(memory_space=pltpu.SMEM)
SOME = pl.BlockSpec(memory_space=pl.ANY)
HALF_ROOT = 0.7071067811865476
DENSITY = 0.3989422804014327
LANES = 128
LITTLE = pl.CostEstimate(flops=1000, bytes_accessed=1000, transcendentals=0)


def swap(block, axis, flip):
    count = lax.axis_size(axis)
    return lax.ppermute(block, axis, [(i, i ^ flip) for i in range(count)])


def shift(block, axis, step, first=0):
    count = lax.axis_size(axis)
    if step > 0:
        pairs = [(i, i + 1) for i in range(first, count - 1)]
    else:
        pairs = [(i + 1, i) for i in range(count - 1 - first)]
    return lax.ppermute(block, axis, pairs)


def after(values, others=()):
    return lax.optimization_barrier(tuple(values) + tuple(others))[: len(values)]


def input_kernel(part, low, high, weights, out, block):
    taps = weights.shape[0]
    rows = part.shape[0]
    half = taps // 2
    block[pl.ds(0, PAD), :] = low[...]
    block[pl.ds(PAD, rows), :] = part[...]
    block[pl.ds(PAD + rows, PAD), :] = high[...]
    tile = min(256, rows)

    def body(step, carry):
        start = pl.multiple_of(step * tile, tile)
        rows_in = block[pl.ds(start, tile + 2 * PAD), :]
        total = None
        for tap in range(taps):
            term = jnp.dot(rows_in, weights[tap], preferred_element_type=jnp.float32)
            first = PAD + half - tap
            term = term[first : first + tile]
            total = term if total is None else total + term
        out[pl.ds(start, tile), :] = total.astype(out.dtype)
        return carry

    lax.fori_loop(0, rows // tile, body, 0)


def input_gradient(part, low, high, weights):
    taps, chans, width = weights.shape
    rows = part.shape[0]
    return pl.pallas_call(
        input_kernel,
        out_shape=jax.ShapeDtypeStruct((rows, width), jnp.bfloat16),
        in_specs=[VMEM] * 4,
        out_specs=VMEM,
        scratch_shapes=[pltpu.VMEM((rows + 2 * PAD, chans), jnp.bfloat16)],
        compiler_params=pltpu.CompilerParams(vmem_limit_bytes=32 * MIB),
    )(part, low, high, weights)


def pieces_kernel(*refs, taps, pieces, middle):
    parts, rest = refs[:pieces], refs[pieces:]
    if middle:
        weights, out, block = rest
    else:
        low, high, center, weights, out, block = rest
    rows = parts[0].shape[0]
    width = weights.shape[1] // taps
    half = taps // 2
    quarter = rows // 4
    kept = [(0, rows)] if middle else [(0, quarter + PAD), (rows - quarter - PAD, quarter + PAD)]
    base = 0
    for part in parts:
        span = pl.ds(base, part.shape[1])
        for begin, count in kept:
            block[pl.ds(PAD + begin, count), span] = part[pl.ds(begin, count), :]
        if not middle:
            block[pl.ds(0, PAD), span] = low[:, span]
            block[pl.ds(PAD + rows, PAD), span] = high[:, span]
        base += part.shape[1]

    def tile(start, count):
        terms = jnp.dot(
            block[pl.ds(start, count + 2 * PAD), :],
            weights[...],
            preferred_element_type=jnp.float32,
        )
        total = None
        for tap in range(taps):
            first = PAD + half - tap
            term = terms[first : first + count, tap * width : (tap + 1) * width]
            total = term if total is None else total + term
        return total.astype(out.dtype)

    if middle:
        out[...] = tile(quarter, 2 * quarter)
    else:
        out[pl.ds(0, quarter), :] = tile(0, quarter)
        out[pl.ds(quarter, 2 * quarter), :] = center[...]
        out[pl.ds(3 * quarter, quarter), :] = tile(3 * quarter, quarter)


def pieces_gradient(parts, weights, taps, rest=()):
    chans = weights.shape[0]
    width = weights.shape[1] // taps
    rows = parts[0].shape[0]
    middle = not rest
    return pl.pallas_call(
        functools.partial(pieces_kernel, taps=taps, pieces=len(parts), middle=middle),
        out_shape=jax.ShapeDtypeStruct((rows // 2 if middle else rows, width), jnp.bfloat16),
        in_specs=[VMEM] * (len(parts) + len(rest) + 1),
        out_specs=VMEM,
        scratch_shapes=[pltpu.VMEM((rows + 2 * PAD, chans), jnp.bfloat16)],
        cost_estimate=LITTLE,
        compiler_params=pltpu.CompilerParams(vmem_limit_bytes=24 * MIB),
    )(*parts, *rest, weights)


def weight_kernel(*refs, taps, tile, rows, size, nx, ng, layout, first, last, origins, span):
    xs, gs, rest = refs[:nx], refs[nx : nx + ng], list(refs[nx + ng :])
    before = None if first else rest.pop(0)
    weights = rest.pop(0) if origins else None
    out = rest.pop(0)
    laid = rest.pop(0) if origins else None
    xbuf, gbuf, acc, sems = rest
    width = xbuf.shape[1]
    half = taps // 2
    x_rows, g_rows, starts, blanks, seams = layout()
    zeros = jnp.zeros((PAD, width), xbuf.dtype)
    xbuf[pl.ds(0, PAD), :] = zeros
    xbuf[pl.ds(PAD + rows, PAD), :] = zeros
    for wanted, row in blanks:

        @pl.when(wanted)
        def _():
            xbuf[pl.ds(row, PAD), :] = zeros

    pieces = [(src, xbuf, row, src.shape[0]) for src, row in zip(xs, x_rows)]
    pieces += [(src, gbuf, row, span or src.shape[0]) for src, row in zip(gs, g_rows)]

    def copy(at):
        src, dst, row, count = pieces[at]
        row = row if isinstance(row, int) else pl.multiple_of(row, 16)
        return pltpu.make_async_copy(
            src.at[pl.ds(0, count), :], dst.at[pl.ds(row, count), :], sems.at[at]
        )

    def each(act):
        for at in range(nx + ng):
            row = pieces[at][2]
            if isinstance(row, int):
                act(at)
            else:
                pl.when(row >= 0)(functools.partial(act, at))

    each(lambda at: copy(at).start())
    moves = []
    if origins:
        where = origins()
        depth = weights.shape[1] // len(where)
        for e, origin in enumerate(where):
            for tap in range(taps):
                moves.append(
                    pltpu.make_async_copy(
                        weights.at[tap, pl.ds(pl.multiple_of(origin, 16), depth), :],
                        laid.at[pl.ds(e * depth, depth), pl.ds(tap * width, width)],
                        sems.at[nx + ng + len(moves)],
                    )
                )
        for move in moves:
            move.start()
    acc[...] = jnp.zeros_like(acc) if first else before[...]
    each(lambda at: copy(at).wait())

    def add(start, count, side=None):
        grad = gbuf[pl.ds(start, count), :].T
        block = xbuf[pl.ds(start, count + 2 * PAD), :].astype(jnp.float32)
        if side is not None:
            row = lax.broadcasted_iota(jnp.int32, block.shape, 0)
            block = jnp.where(row >= count + PAD if side > 0 else row < PAD, block, 0.0)
        moved = []
        for tap in range(taps):
            at = PAD - half + tap
            moved.append(block[at : at + count].astype(jnp.bfloat16))
        if width % LANES:
            for tap in range(taps):
                acc[tap] += jnp.dot(grad, moved[tap], preferred_element_type=jnp.float32)
        else:
            moved = jnp.concatenate(moved, axis=1)
            acc[...] += jnp.dot(grad, moved, preferred_element_type=jnp.float32)

    for begin in starts:

        def body(step, carry):
            add(pl.multiple_of(begin + step * tile, 16), tile)
            return carry

        lax.fori_loop(0, size // tile, body, 0)
    for wanted, row, side in seams:
        pl.when(wanted)(functools.partial(add, row, PAD, side))
    if last and width % LANES == 0:
        for tap in range(taps):
            out[tap] = acc[:, tap * width : (tap + 1) * width].astype(out.dtype)
    else:
        out[...] = acc[...].astype(out.dtype)
    for move in moves:
        move.wait()


def weight_gradient(
    xs, gs, layout, size, taps, rows, before=None, last=True, vmem=40, weights=None, origins=None, span=None
):
    width, chunk = xs[0].shape[1], gs[0].shape[1]
    split = (taps, chunk, width)
    joined = split if width % LANES else (chunk, taps * width)
    out_shape = [
        jax.ShapeDtypeStruct(split, jnp.bfloat16)
        if last
        else jax.ShapeDtypeStruct(joined, jnp.float32)
    ]
    moves = 0
    if origins:
        moves = taps * 4
        out_shape.append(
            jax.ShapeDtypeStruct((weights.shape[1], taps * width), weights.dtype)
        )
    return pl.pallas_call(
        functools.partial(
            weight_kernel,
            taps=taps,
            tile=min(1024, size) if width % LANES == 0 else min(512, size),
            rows=rows,
            size=size,
            nx=len(xs),
            ng=len(gs),
            layout=layout,
            first=before is None,
            last=last,
            origins=origins,
            span=span,
        ),
        out_shape=out_shape,
        in_specs=[SOME] * (len(xs) + len(gs))
        + [VMEM] * (before is not None)
        + [SOME] * (weights is not None),
        out_specs=[VMEM] * len(out_shape),
        scratch_shapes=[
            pltpu.VMEM((rows + 2 * PAD, width), jnp.bfloat16),
            pltpu.VMEM((rows, chunk), jnp.bfloat16),
            pltpu.VMEM(joined, jnp.float32),
            pltpu.SemaphoreType.DMA((len(xs) + len(gs) + moves,)),
        ],
        cost_estimate=LITTLE,
        compiler_params=pltpu.CompilerParams(vmem_limit_bytes=vmem * MIB),
    )(
        *xs,
        *gs,
        *([] if before is None else [before]),
        *([] if weights is None else [weights]),
    )


def merge_pairs(value, scratch):
    size = value.shape[0] // 2
    sums = []
    for at in range(value.shape[1] // LANES):
        scratch[at] = value[:, at * LANES : (at + 1) * LANES]
        even = scratch[at, pl.ds(0, size, stride=2), :]
        sums.append(even + scratch[at, pl.ds(1, size, stride=2), :])
    return jnp.concatenate(sums, axis=1)


def make_pairs(value, scratch):
    size = value.shape[0]
    rows = []
    for at in range(value.shape[1] // LANES):
        part = value[:, at * LANES : (at + 1) * LANES]
        scratch[at, pl.ds(0, size, stride=2), :] = part
        scratch[at, pl.ds(1, size, stride=2), :] = part
        rows.append(scratch[at])
    return jnp.concatenate(rows, axis=1)


def pair_scratch(rows, width):
    return pltpu.VMEM((width // LANES, rows, LANES), jnp.float32)


def each_exon(owners, exons, seen, nblocks, most, act):
    mine = lax.axis_index("seq")
    span, count = exons.shape
    for i in range(seen.shape[0]):
        seen[i] = 0

    def body(t, carry):
        owner = owners[t]
        slot = (owner ^ mine) * most + seen[owner]
        seen[owner] += 1
        for e in range(span):
            where = exons[e, t]

            @pl.when(where // nblocks == mine)
            def _():
                act(slot, where % nblocks)

        return carry

    lax.fori_loop(0, count, body, 0)


def front_kernel(owners, exons, pre_act, *refs, nblocks, most, size):
    outs, (slots, pair, seen) = refs[:-3], refs[-3:]
    slots[...] = jnp.zeros_like(slots)

    def act(slot, block):
        at = pl.ds(pl.multiple_of(block * (2 * size), 2 * size), 2 * size)
        value = pre_act[at, :].astype(jnp.float32)
        value = value * (0.5 * (1.0 + lax.erf(value * HALF_ROOT)))
        mean = 0.5 * merge_pairs(value, pair)
        slots[pl.ds(pl.multiple_of(slot * size, size), size), :] = mean

    each_exon(owners, exons, seen, nblocks, most, act)
    group = most * size
    for d, out in enumerate(outs):
        out[...] = slots[pl.ds(d * group, group), :].astype(out.dtype)


def front(owners, exons, pre_act, most, size, groups):
    rows, width = pre_act.shape
    return pl.pallas_call(
        functools.partial(
            front_kernel, nblocks=rows // 2 // size, most=most, size=size
        ),
        out_shape=[jax.ShapeDtypeStruct((most * size, width), jnp.bfloat16)] * groups,
        in_specs=[SMEM] * 2 + [VMEM],
        out_specs=[VMEM] * groups,
        scratch_shapes=[
            pltpu.VMEM((groups * most * size, width), jnp.float32),
            pair_scratch(2 * size, width),
            pltpu.SMEM((groups,), jnp.int32),
        ],
        cost_estimate=LITTLE,
        compiler_params=pltpu.CompilerParams(vmem_limit_bytes=16 * MIB),
    )(owners, exons, pre_act)


def plain_kernel(pre_act, out_grad, slope, plain, both):
    value = pre_act[...].astype(jnp.float32)
    normal = 0.5 * (1.0 + lax.erf(value * HALF_ROOT))
    slope[...] = normal + value * (jnp.exp(-0.5 * value * value) * DENSITY)
    pooled = make_pairs(out_grad[...].astype(jnp.float32) * 0.5, both)
    plain[...] = (pooled * slope[...]).astype(plain.dtype)


def plain_gradient(pre_act, out_grad):
    rows, width = pre_act.shape
    return pl.pallas_call(
        plain_kernel,
        out_shape=[
            jax.ShapeDtypeStruct((rows, width), jnp.float32),
            jax.ShapeDtypeStruct((rows, width), jnp.bfloat16),
        ],
        in_specs=[VMEM] * 2,
        out_specs=[VMEM] * 2,
        scratch_shapes=[pair_scratch(rows, width)],
        cost_estimate=LITTLE,
        compiler_params=pltpu.CompilerParams(vmem_limit_bytes=16 * MIB),
    )(pre_act, out_grad)


def gain_kernel(owners, exons, out_grad, slope, plain, *refs, nblocks, most, size):
    splices, (grad, gain, held, both, seen) = refs[:-5], refs[-5:]
    gain[...] = out_grad[...].astype(jnp.float32)
    grad[...] = plain[...]
    base = 0
    for splice in splices:
        held[pl.ds(base, splice.shape[0]), :] = splice[...].astype(jnp.float32)
        base += splice.shape[0]

    def add(slot, block):
        at = pl.ds(pl.multiple_of(block * size, size), size)
        gain[at, :] += held[pl.ds(pl.multiple_of(slot * size, size), size), :]

    def renew(slot, block):
        pooled = 0.5 * gain[pl.ds(pl.multiple_of(block * size, size), size), :]
        pooled = make_pairs(pooled, both)
        at = pl.ds(pl.multiple_of(block * (2 * size), 2 * size), 2 * size)
        grad[at, :] = (pooled * slope[at, :]).astype(grad.dtype)

    each_exon(owners, exons, seen, nblocks, most, add)
    each_exon(owners, exons, seen, nblocks, most, renew)


def gained_gradient(owners, exons, out_grad, slope, plain, splices, most, size, groups):
    rows, width = slope.shape
    return pl.pallas_call(
        functools.partial(
            gain_kernel, nblocks=rows // 2 // size, most=most, size=size
        ),
        out_shape=jax.ShapeDtypeStruct((rows, width), jnp.bfloat16),
        in_specs=[SMEM] * 2 + [VMEM] * (3 + len(splices)),
        out_specs=VMEM,
        scratch_shapes=[
            pltpu.VMEM((rows // 2, width), jnp.float32),
            pltpu.VMEM((groups * most * size, width), jnp.float32),
            pair_scratch(2 * size, width),
            pltpu.SMEM((groups,), jnp.int32),
        ],
        compiler_params=pltpu.CompilerParams(vmem_limit_bytes=16 * MIB),
    )(owners, exons, out_grad, slope, plain, *splices)


def gathered_gradient(pre_act, out_grad, coverage_obs, owners, exon_blocks):
    rows, width = pre_act.shape
    nseq = lax.axis_size("seq")
    mine = lax.axis_index("seq")
    most, block = coverage_obs.shape[1:3]
    nblocks = rows // 2 // block
    counts = owners.shape[0]
    value = pre_act.astype(jnp.float32)
    normal = 0.5 * (1.0 + jax.scipy.special.erf(value * HALF_ROOT))
    slope = normal + value * jnp.exp(-0.5 * value * value) * DENSITY
    act = value * normal
    pooled = (0.5 * jnp.sum(act.reshape(rows // 2, 2, width), axis=1)).astype(jnp.bfloat16)
    order = jnp.arange(counts, dtype=jnp.int32)
    same = owners[:, None] == owners[None, :]
    rank = jnp.sum((same & (order[:, None] < order[None, :])).astype(jnp.int32), axis=0)
    dest = jnp.arange(nseq, dtype=jnp.int32)
    slots = jnp.arange(most, dtype=jnp.int32)
    route = (owners[None, None, :] == dest[:, None, None]) & (
        rank[None, None, :] == slots[None, :, None]
    )
    route = route.astype(jnp.float32).reshape(nseq * most, counts)
    on_mine = exon_blocks // nblocks == mine
    holds = jnp.any(on_mine, axis=1)
    local_block = jnp.sum(jnp.where(on_mine, exon_blocks % nblocks, 0), axis=1)
    select = (
        holds[:, None] & (local_block[:, None] == jnp.arange(nblocks, dtype=jnp.int32)[None, :])
    ).astype(jnp.float32)
    picker = jnp.dot(route, select, precision=lax.Precision.HIGHEST).astype(jnp.bfloat16)
    pieces = pooled.reshape(nblocks, block * width)
    outgoing = jnp.dot(picker, pieces, preferred_element_type=jnp.float32).astype(jnp.bfloat16)
    outgoing = outgoing.reshape(nseq, most, block, width)
    arrived = lax.all_to_all(outgoing, "seq", split_axis=0, concat_axis=0, tiled=True)
    coverage = jnp.sum(arrived.astype(jnp.float32), axis=0)
    splice = jnp.tanh(coverage - coverage_obs[0]).astype(jnp.bfloat16)
    returned = lax.all_gather(splice, "seq", axis=0).reshape(nseq * most, block * width)
    gained = jnp.dot(picker.T, returned, preferred_element_type=jnp.float32)
    pooled_grad = out_grad.astype(jnp.float32) + gained.reshape(rows // 2, width)
    return (jnp.repeat(pooled_grad, 2, axis=0) * 0.5 * slope).astype(jnp.bfloat16)


def local(x_saved, pre_act, out_grad, conv_w, coverage_obs, owners, exon_blocks):
    rows, width = x_saved.shape
    taps = conv_w.shape[1]
    nseq = lax.axis_size("seq")
    nch = lax.axis_size("ch")
    chunk = conv_w.shape[0] // nseq
    most = coverage_obs.shape[1]
    size = coverage_obs.shape[2]
    direct = nseq == nch == 4 and chunk == width and width % 128 == 0
    exons = exon_blocks.T
    weights = conv_w.transpose(1, 0, 2)
    target = coverage_obs[0].reshape(most * size, width)

    if not direct:
        pre_grad = gathered_gradient(pre_act, out_grad, coverage_obs, owners, exon_blocks)
        x_all = lax.all_gather(x_saved, "seq", axis=0, tiled=True)
        whole = lax.all_gather(pre_grad, "ch", axis=1, tiled=True)
        blocks = whole.reshape(rows, nseq, chunk).transpose(1, 0, 2)
        g_all = lax.all_to_all(blocks, "seq", 0, 0, tiled=True).reshape(nseq * rows, chunk)
        low = shift(whole[rows - PAD :], "seq", 1)
        high = shift(whole[:PAD], "seq", -1)
        in_grad = input_gradient(whole, low, high, weights)
        total = nseq * rows
        (w_grad,) = weight_gradient(
            [x_all], [g_all], lambda: ([PAD], [0], [0], [], []), total, taps, total
        )
        return (in_grad, w_grad.transpose(1, 0, 2))

    mine = lax.axis_index("seq")
    place = lax.axis_index("ch")
    early = x_saved[: rows // 2]
    up_early, down_early = shift(early, "seq", 1), shift(early, "seq", -1)
    outgoing = front(owners, exons, pre_act, most, size, nseq)
    slope, plain = plain_gradient(pre_act, out_grad)
    arrived = [outgoing[0]] + [swap(outgoing[d], "seq", d) for d in range(1, nseq)]
    *arrived, up_early, down_early, slope, plain = after(
        [*arrived, up_early, down_early, slope, plain]
    )
    coverage = functools.reduce(jnp.add, [a.astype(jnp.float32) for a in arrived])
    splice = jnp.tanh(coverage - target).astype(jnp.bfloat16)
    splices = [splice] + [swap(splice, "seq", d) for d in range(1, nseq)]
    pre_grad = gained_gradient(owners, exons, out_grad, slope, plain, splices, most, size, nseq)
    (late,) = after([x_saved[rows // 2 :]], splices[1:])
    up1 = jnp.concatenate([up_early, shift(late, "seq", 1)])
    down1 = jnp.concatenate([down_early, shift(late, "seq", -1)])

    far = swap(pre_grad, "ch", 2)
    near = swap(pre_grad, "ch", 1)
    up2, down2 = shift(up1, "seq", 1, 1), shift(down1, "seq", -1, 1)
    far, near, up2, down2 = after([far, near, up2, down2])
    parts = after([pre_grad, near, far, swap(far, "ch", 1)])

    quarter = rows // nch
    half = taps // 2

    def chosen(flipped, options):
        want = mine ^ flipped ^ place
        picked = options[0]
        for t in range(1, nch):
            picked = jnp.where(want == t, options[t], picked)
        return picked

    slices = [lax.dynamic_slice_in_dim(p, place * quarter, quarter, axis=0) for p in parts]
    heads = jnp.concatenate([p[:half] for p in parts])
    tails = jnp.concatenate([p[rows - half :] for p in parts])
    spare = jnp.zeros((-len(heads) % PAD, width), jnp.bfloat16)
    sent = [chosen(d, slices) for d in range(1, nseq)]
    for d in (1, 3):
        edge = jnp.where((mine ^ d) > mine, tails, heads)
        sent[d - 1] = jnp.concatenate([sent[d - 1], edge, spare])
    *sent, up2, down2 = after([*sent, up2, down2])
    got = [swap(block, "seq", d) for d, block in zip(range(1, nseq), sent)]
    up3, down3 = shift(up2, "seq", 1, 2), shift(down2, "seq", -1, 2)

    def origins():
        return [(lax.axis_index("ch") ^ t) * width for t in range(nch)]

    partial, laid = weight_gradient(
        [up1[rows - PAD :], x_saved, down1[:PAD]],
        [chosen(0, parts)],
        lambda: ([0, PAD, PAD + rows], [0], [0], [], []),
        rows,
        taps,
        rows,
        last=False,
        vmem=24,
        weights=weights,
        origins=origins,
    )
    center = pieces_gradient(parts, laid, taps)
    first, partial, center = after([got[0], partial, center])
    got[0] = first

    across = [swap(block, "ch", 2) for block in got]
    beside = [swap(block, "ch", 1) for block in got]
    edges = [got[d - 1][quarter : quarter + len(heads)] for d in (1, 3)]
    edges = [jnp.concatenate(jnp.split(e, nch), axis=1) for e in edges]
    nothing = jnp.zeros_like(edges[0])
    low = jnp.where(mine % 2 == 1, edges[0], jnp.where(mine == 2, edges[1], nothing))
    high = jnp.where(mine % 2 == 0, edges[0], jnp.where(mine == 1, edges[1], nothing))
    low = jnp.pad(low, ((PAD - half, 0), (0, 0)))
    high = jnp.pad(high, ((0, PAD - half), (0, 0)))
    in_grad = pieces_gradient(parts, laid, taps, [low, high, center])
    *across, in_grad = after([*across, in_grad])
    beyond = [swap(block, "ch", 1) for block in across]

    seam = (nseq - 1) * rows

    def layout(hops, blocks, closing):
        mine = lax.axis_index("seq")
        place = lax.axis_index("ch")
        x_rows = [PAD + mine * rows]
        for hop in range(1, hops):
            low_at, high_at = mine - hop, mine + hop
            x_rows += [
                jnp.where(low_at >= 0, PAD + low_at * rows, -1),
                jnp.where(high_at < nseq, PAD + high_at * rows, -1),
            ]
        used = (2, 3) if closing else blocks
        g_rows = [
            (mine ^ d) * rows + (place ^ tag) * quarter for d in used for tag in range(nch)
        ]
        starts = [(mine ^ d) * rows for d in blocks]
        if closing:
            seams = [(mine == 0, seam - PAD, 1), (mine == nseq - 1, rows, -1)]
            return x_rows, g_rows, starts, [], seams
        return x_rows, g_rows, starts, [(mine == 0, PAD + seam), (mine == nseq - 1, rows)], []

    def sources(blocks):
        return [
            kind[d - 1] for d in blocks for kind in (got, beside, across, beyond)
        ]

    (partial,) = weight_gradient(
        [x_saved, up1, down1, up2, down2],
        sources((1, 2)),
        functools.partial(layout, 3, (1, 2), False),
        rows,
        taps,
        nseq * rows,
        before=partial,
        last=False,
        vmem=32,
        span=quarter,
    )
    (w_grad,) = weight_gradient(
        [x_saved, up1, down1, up2, down2, up3, down3],
        sources((2, 3)),
        functools.partial(layout, 4, (3,), True),
        rows,
        taps,
        nseq * rows,
        before=after([partial], [in_grad])[0],
        vmem=32,
        span=quarter,
    )
    return (in_grad, w_grad.transpose(1, 0, 2))


def solution(mesh):
    in_specs = (
        P(("grp", "seq"), "ch"),
        P(("grp", "seq"), "ch"),
        P(("grp", "seq"), "ch"),
        P(None, None, "ch"),
        P(("grp", "seq"), None, None, "ch"),
        P("grp"),
        P("grp", None),
    )
    out_specs = (P(("grp", "seq"), "ch"), P(("grp", "seq"), None, "ch"))
    return jax.shard_map(local, mesh=mesh, in_specs=in_specs, out_specs=out_specs, check_vma=False)
```

```python
import functools

import jax
import jax.numpy as jnp
from jax import lax
from jax.experimental import pallas as pl
from jax.experimental.pallas import tpu as pltpu
from jax.sharding import PartitionSpec as P

PAD = 16
MIB = 1024 * 1024
VMEM = pl.BlockSpec(memory_space=pltpu.VMEM)
SMEM = pl.BlockSpec(memory_space=pltpu.SMEM)
SOME = pl.BlockSpec(memory_space=pl.ANY)
HALF_ROOT = 0.7071067811865476
DENSITY = 0.3989422804014327
LANES = 128
GAINF = 1000
LITTLE = pl.CostEstimate(flops=1000, bytes_accessed=1000, transcendentals=0)


def swap(block, axis, flip):
    count = lax.axis_size(axis)
    return lax.ppermute(block, axis, [(i, i ^ flip) for i in range(count)])


def shift(block, axis, step, first=0):
    count = lax.axis_size(axis)
    if step > 0:
        pairs = [(i, i + 1) for i in range(first, count - 1)]
    else:
        pairs = [(i + 1, i) for i in range(count - 1 - first)]
    return lax.ppermute(block, axis, pairs)


def after(values, others=()):
    return lax.optimization_barrier(tuple(values) + tuple(others))[: len(values)]


def input_kernel(part, low, high, weights, out, block):
    taps = weights.shape[0]
    rows = part.shape[0]
    half = taps // 2
    block[pl.ds(0, PAD), :] = low[...]
    block[pl.ds(PAD, rows), :] = part[...]
    block[pl.ds(PAD + rows, PAD), :] = high[...]
    tile = min(256, rows)

    def body(step, carry):
        start = pl.multiple_of(step * tile, tile)
        rows_in = block[pl.ds(start, tile + 2 * PAD), :]
        total = None
        for tap in range(taps):
            term = jnp.dot(rows_in, weights[tap], preferred_element_type=jnp.float32)
            first = PAD + half - tap
            term = term[first : first + tile]
            total = term if total is None else total + term
        out[pl.ds(start, tile), :] = total.astype(out.dtype)
        return carry

    lax.fori_loop(0, rows // tile, body, 0)


def input_gradient(part, low, high, weights):
    taps, chans, width = weights.shape
    rows = part.shape[0]
    return pl.pallas_call(
        input_kernel,
        out_shape=jax.ShapeDtypeStruct((rows, width), jnp.bfloat16),
        in_specs=[VMEM] * 4,
        out_specs=VMEM,
        scratch_shapes=[pltpu.VMEM((rows + 2 * PAD, chans), jnp.bfloat16)],
        compiler_params=pltpu.CompilerParams(vmem_limit_bytes=32 * MIB),
    )(part, low, high, weights)


def pieces_kernel(*refs, taps, pieces, middle):
    parts, rest = refs[:pieces], refs[pieces:]
    if middle:
        weights, out, block = rest
    else:
        near_edge, far_edge, center, weights, out, block = rest
    rows = parts[0].shape[0]
    width = weights.shape[1] // taps
    half = taps // 2
    quarter = rows // 4
    kept = [(0, rows)] if middle else [(0, quarter + PAD), (rows - quarter - PAD, quarter + PAD)]
    base = 0
    for part in parts:
        span = pl.ds(base, part.shape[1])
        for begin, count in kept:
            block[pl.ds(PAD + begin, count), span] = part[pl.ds(begin, count), :]
        base += part.shape[1]
    if not middle:
        mine = lax.axis_index("seq")
        one = near_edge[pl.ds(quarter, PAD), :].astype(jnp.float32)
        other = far_edge[pl.ds(quarter, PAD), :].astype(jnp.float32)
        low = jnp.where(mine % 2 == 1, one, jnp.where(mine == 2, other, 0.0))
        high = jnp.where(mine % 2 == 0, one, jnp.where(mine == 1, other, 0.0))
        for at in range(pieces):
            span = pl.ds(at * part.shape[1], part.shape[1])
            lower = pltpu.roll(low, PAD - half - half * at, 0)
            upper = pltpu.roll(high, (PAD - half * at) % PAD, 0)
            block[pl.ds(0, PAD), span] = lower.astype(block.dtype)
            block[pl.ds(PAD + rows, PAD), span] = upper.astype(block.dtype)

    def tile(start, count):
        terms = jnp.dot(
            block[pl.ds(start, count + 2 * PAD), :],
            weights[...],
            preferred_element_type=jnp.float32,
        )
        total = None
        for tap in range(taps):
            first = PAD + half - tap
            term = terms[first : first + count, tap * width : (tap + 1) * width]
            total = term if total is None else total + term
        return total.astype(out.dtype)

    if middle:
        out[...] = tile(quarter, 2 * quarter)
    else:
        out[pl.ds(0, quarter), :] = tile(0, quarter)
        out[pl.ds(quarter, 2 * quarter), :] = center[...]
        out[pl.ds(3 * quarter, quarter), :] = tile(3 * quarter, quarter)


def pieces_gradient(parts, weights, taps, rest=()):
    chans = weights.shape[0]
    width = weights.shape[1] // taps
    rows = parts[0].shape[0]
    middle = not rest
    return pl.pallas_call(
        functools.partial(pieces_kernel, taps=taps, pieces=len(parts), middle=middle),
        out_shape=jax.ShapeDtypeStruct((rows // 2 if middle else rows, width), jnp.bfloat16),
        in_specs=[VMEM] * (len(parts) + len(rest) + 1),
        out_specs=VMEM,
        scratch_shapes=[pltpu.VMEM((rows + 2 * PAD, chans), jnp.bfloat16)],
        cost_estimate=LITTLE,
        compiler_params=pltpu.CompilerParams(vmem_limit_bytes=24 * MIB),
    )(*parts, *rest, weights)


def weight_kernel(*refs, taps, tile, rows, size, nx, ng, layout, first, last, origins, span):
    xs, gs, rest = refs[:nx], refs[nx : nx + ng], list(refs[nx + ng :])
    before = None if first else rest.pop(0)
    weights = rest.pop(0) if origins else None
    out = rest.pop(0)
    laid = rest.pop(0) if origins else None
    xbuf, gbuf, acc, sems = rest
    width = xbuf.shape[1]
    half = taps // 2
    x_rows, g_rows, starts, blanks, seams = layout()
    zeros = jnp.zeros((PAD, width), xbuf.dtype)
    xbuf[pl.ds(0, PAD), :] = zeros
    xbuf[pl.ds(PAD + rows, PAD), :] = zeros
    for wanted, row in blanks:

        @pl.when(wanted)
        def _():
            xbuf[pl.ds(row, PAD), :] = zeros

    pieces = [(src, xbuf, row, src.shape[0]) for src, row in zip(xs, x_rows)]
    pieces += [(src, gbuf, row, span or src.shape[0]) for src, row in zip(gs, g_rows)]

    def copy(at):
        src, dst, row, count = pieces[at]
        row = row if isinstance(row, int) else pl.multiple_of(row, 16)
        return pltpu.make_async_copy(
            src.at[pl.ds(0, count), :], dst.at[pl.ds(row, count), :], sems.at[at]
        )

    def each(act):
        for at in range(nx + ng):
            row = pieces[at][2]
            if isinstance(row, int):
                act(at)
            else:
                pl.when(row >= 0)(functools.partial(act, at))

    each(lambda at: copy(at).start())
    moves = []
    if origins:
        where = origins()
        depth = weights.shape[1] // len(where)
        for e, origin in enumerate(where):
            for tap in range(taps):
                moves.append(
                    pltpu.make_async_copy(
                        weights.at[tap, pl.ds(pl.multiple_of(origin, 16), depth), :],
                        laid.at[pl.ds(e * depth, depth), pl.ds(tap * width, width)],
                        sems.at[nx + ng + len(moves)],
                    )
                )
        for move in moves:
            move.start()
    acc[...] = jnp.zeros_like(acc) if first else before[...]
    each(lambda at: copy(at).wait())

    def add(start, count, side=None):
        grad = gbuf[pl.ds(start, count), :].T
        block = xbuf[pl.ds(start, count + 2 * PAD), :].astype(jnp.float32)
        if side is not None:
            row = lax.broadcasted_iota(jnp.int32, block.shape, 0)
            block = jnp.where(row >= count + PAD if side > 0 else row < PAD, block, 0.0)
        moved = []
        for tap in range(taps):
            at = PAD - half + tap
            moved.append(block[at : at + count].astype(jnp.bfloat16))
        if width % LANES:
            for tap in range(taps):
                acc[tap] += jnp.dot(grad, moved[tap], preferred_element_type=jnp.float32)
        else:
            moved = jnp.concatenate(moved, axis=1)
            acc[...] += jnp.dot(grad, moved, preferred_element_type=jnp.float32)

    for begin in starts:

        def body(step, carry):
            add(pl.multiple_of(begin + step * tile, 16), tile)
            return carry

        lax.fori_loop(0, size // tile, body, 0)
    for wanted, row, side in seams:
        pl.when(wanted)(functools.partial(add, row, PAD, side))
    if last and width % LANES == 0:
        for tap in range(taps):
            out[tap] = acc[:, tap * width : (tap + 1) * width].astype(out.dtype)
    else:
        out[...] = acc[...].astype(out.dtype)
    for move in moves:
        move.wait()


def weight_gradient(
    xs, gs, layout, size, taps, rows, before=None, last=True, vmem=40, weights=None, origins=None, span=None
):
    width, chunk = xs[0].shape[1], gs[0].shape[1]
    split = (taps, chunk, width)
    joined = split if width % LANES else (chunk, taps * width)
    out_shape = [
        jax.ShapeDtypeStruct(split, jnp.bfloat16)
        if last
        else jax.ShapeDtypeStruct(joined, jnp.float32)
    ]
    moves = 0
    if origins:
        moves = taps * 4
        out_shape.append(
            jax.ShapeDtypeStruct((weights.shape[1], taps * width), weights.dtype)
        )
    return pl.pallas_call(
        functools.partial(
            weight_kernel,
            taps=taps,
            tile=min(1024, size) if width % LANES == 0 else min(512, size),
            rows=rows,
            size=size,
            nx=len(xs),
            ng=len(gs),
            layout=layout,
            first=before is None,
            last=last,
            origins=origins,
            span=span,
        ),
        out_shape=out_shape,
        in_specs=[SOME] * (len(xs) + len(gs))
        + [VMEM] * (before is not None)
        + [SOME] * (weights is not None),
        out_specs=[VMEM] * len(out_shape),
        scratch_shapes=[
            pltpu.VMEM((rows + 2 * PAD, width), jnp.bfloat16),
            pltpu.VMEM((rows, chunk), jnp.bfloat16),
            pltpu.VMEM(joined, jnp.float32),
            pltpu.SemaphoreType.DMA((len(xs) + len(gs) + moves,)),
        ],
        cost_estimate=LITTLE,
        compiler_params=pltpu.CompilerParams(vmem_limit_bytes=vmem * MIB),
    )(
        *xs,
        *gs,
        *([] if before is None else [before]),
        *([] if weights is None else [weights]),
    )


def merge_pairs(value, scratch):
    size = value.shape[0] // 2
    sums = []
    for at in range(value.shape[1] // LANES):
        scratch[at] = value[:, at * LANES : (at + 1) * LANES]
        even = scratch[at, pl.ds(0, size, stride=2), :]
        sums.append(even + scratch[at, pl.ds(1, size, stride=2), :])
    return jnp.concatenate(sums, axis=1)


def make_pairs(value, scratch):
    size = value.shape[0]
    rows = []
    for at in range(value.shape[1] // LANES):
        part = value[:, at * LANES : (at + 1) * LANES]
        scratch[at, pl.ds(0, size, stride=2), :] = part
        scratch[at, pl.ds(1, size, stride=2), :] = part
        rows.append(scratch[at])
    return jnp.concatenate(rows, axis=1)


def pair_scratch(rows, width):
    return pltpu.VMEM((width // LANES, rows, LANES), jnp.float32)


def each_exon(owners, exons, seen, nblocks, most, act):
    mine = lax.axis_index("seq")
    span, count = exons.shape
    for i in range(seen.shape[0]):
        seen[i] = 0

    def body(t, carry):
        owner = owners[t]
        slot = (owner ^ mine) * most + seen[owner]
        seen[owner] += 1
        for e in range(span):
            where = exons[e, t]

            @pl.when(where // nblocks == mine)
            def _():
                act(t, slot, where % nblocks)

        return carry

    lax.fori_loop(0, count, body, 0)


def front_kernel(owners, exons, pre_act, *refs, nblocks, most, size):
    outs, (slots, pair, seen) = refs[:-3], refs[-3:]
    slots[...] = jnp.zeros_like(slots)

    def act(t, slot, block):
        at = pl.ds(pl.multiple_of(block * (2 * size), 2 * size), 2 * size)
        value = pre_act[at, :].astype(jnp.float32)
        value = value * (0.5 * (1.0 + lax.erf(value * HALF_ROOT)))
        mean = 0.5 * merge_pairs(value, pair)
        slots[pl.ds(pl.multiple_of(slot * size, size), size), :] = mean

    each_exon(owners, exons, seen, nblocks, most, act)
    group = most * size
    for d, out in enumerate(outs):
        out[...] = slots[pl.ds(d * group, group), :].astype(out.dtype)


def front(owners, exons, pre_act, most, size, groups):
    rows, width = pre_act.shape
    return pl.pallas_call(
        functools.partial(
            front_kernel, nblocks=rows // 2 // size, most=most, size=size
        ),
        out_shape=[jax.ShapeDtypeStruct((most * size, width), jnp.bfloat16)] * groups,
        in_specs=[SMEM] * 2 + [VMEM],
        out_specs=[VMEM] * groups,
        scratch_shapes=[
            pltpu.VMEM((groups * most * size, width), jnp.float32),
            pair_scratch(2 * size, width),
            pltpu.SMEM((groups,), jnp.int32),
        ],
        cost_estimate=LITTLE,
        compiler_params=pltpu.CompilerParams(vmem_limit_bytes=16 * MIB),
    )(owners, exons, pre_act)


def plain_kernel(pre_act, out_grad, slope, plain, both):
    value = pre_act[...].astype(jnp.float32)
    normal = 0.5 * (1.0 + lax.erf(value * HALF_ROOT))
    slope[...] = normal + value * (jnp.exp(-0.5 * value * value) * DENSITY)
    pooled = make_pairs(out_grad[...].astype(jnp.float32) * 0.5, both)
    plain[...] = (pooled * slope[...]).astype(plain.dtype)


def plain_gradient(pre_act, out_grad):
    rows, width = pre_act.shape
    return pl.pallas_call(
        plain_kernel,
        out_shape=[
            jax.ShapeDtypeStruct((rows, width), jnp.float32),
            jax.ShapeDtypeStruct((rows, width), jnp.bfloat16),
        ],
        in_specs=[VMEM] * 2,
        out_specs=[VMEM] * 2,
        scratch_shapes=[pair_scratch(rows, width)],
        cost_estimate=LITTLE,
        compiler_params=pltpu.CompilerParams(vmem_limit_bytes=16 * MIB),
    )(pre_act, out_grad)


def gain_kernel(owners, exons, out_grad, slope, *refs, nblocks, most, size):
    splices, (grad, gain, held, both, seen) = refs[:-5], refs[-5:]
    gain[...] = out_grad[...].astype(jnp.float32)
    base = 0
    for splice in splices:
        held[pl.ds(base, splice.shape[0]), :] = splice[...].astype(jnp.float32)
        base += splice.shape[0]

    def add(t, slot, block):
        at = pl.ds(pl.multiple_of(block * size, size), size)
        gain[at, :] += held[pl.ds(pl.multiple_of(slot * size, size), size), :]

    def final(block):
        pooled = 0.5 * gain[pl.ds(pl.multiple_of(block * size, size), size), :]
        at = pl.ds(pl.multiple_of(block * (2 * size), 2 * size), 2 * size)
        return make_pairs(pooled, both) * slope[at, :]

    def renew(t, slot, block):
        at = pl.ds(pl.multiple_of(t * (2 * size), 2 * size), 2 * size)
        grad[at, :] = final(block).astype(grad.dtype)

    each_exon(owners, exons, seen, nblocks, most, add)
    each_exon(owners, exons, seen, nblocks, most, renew)
    count = exons.shape[1]
    row = lax.broadcasted_iota(jnp.int32, (2 * size, grad.shape[1]), 0)
    for at, block, first in ((count, 0, 0), (count + 1, nblocks - 1, 2 * size - 2)):
        rows = final(block)
        rows = jnp.where(row % 2 == 0, rows[first : first + 1], rows[first + 1 : first + 2])
        grad[pl.ds(at * 2 * size, 2 * size), :] = rows.astype(grad.dtype)


def gained_rows(owners, exons, out_grad, slope, splices, most, size, groups):
    rows, width = slope.shape
    return pl.pallas_call(
        functools.partial(gain_kernel, nblocks=rows // 2 // size, most=most, size=size),
        out_shape=jax.ShapeDtypeStruct(((exons.shape[1] + 2) * 2 * size, width), jnp.bfloat16),
        in_specs=[SMEM] * 2 + [VMEM] * (2 + len(splices)),
        out_specs=VMEM,
        scratch_shapes=[
            pltpu.VMEM((rows // 2, width), jnp.float32),
            pltpu.VMEM((groups * most * size, width), jnp.float32),
            pair_scratch(2 * size, width),
            pltpu.SMEM((groups,), jnp.int32),
        ],
        cost_estimate=pl.CostEstimate(flops=GAINF, bytes_accessed=1000, transcendentals=0),
        compiler_params=pltpu.CompilerParams(vmem_limit_bytes=16 * MIB),
    )(owners, exons, out_grad, slope, *splices)


def mend_kernel(exons, *refs, pieces, nblocks, size):
    gained, parts, sent, own = (
        refs[pieces : 2 * pieces],
        refs[2 * pieces : 3 * pieces],
        refs[3 * pieces : -1],
        refs[-1],
    )
    mine = lax.axis_index("seq")
    place = lax.axis_index("ch")
    span, count = exons.shape
    rows = parts[0].shape[0]
    quarter = rows // pieces

    def body(t, carry):
        for e in range(span):
            where = exons[e, t]

            @pl.when(where // nblocks == mine)
            def _():
                to = pl.ds(pl.multiple_of(where % nblocks * (2 * size), 2 * size), 2 * size)
                at = pl.ds(pl.multiple_of(t * (2 * size), 2 * size), 2 * size)
                for part, new in zip(parts, gained):
                    part[to, :] = new[at, :]

        return carry

    lax.fori_loop(0, count, body, 0)
    row = lax.broadcasted_iota(jnp.int32, (PAD, own.shape[1]), 0)
    for d, out in enumerate(sent, 1):
        for tag, part in enumerate(parts):

            @pl.when(mine ^ d ^ place == tag)
            def _():
                at = pl.ds(pl.multiple_of(place * quarter, quarter), quarter)
                out[pl.ds(0, quarter), :] = part[at, :]

        if out.shape[0] > quarter:
            after_me = (mine ^ d) > mine
            edge = jnp.zeros(row.shape, jnp.float32)
            for tag, new in enumerate(gained):
                head = new[pl.ds(count * 2 * size, PAD), :].astype(jnp.float32)
                tail = new[pl.ds((count + 1) * 2 * size, PAD), :].astype(jnp.float32)
                edge = jnp.where(row // 2 == tag, jnp.where(after_me, tail, head), edge)
            out[pl.ds(quarter, PAD), :] = edge.astype(out.dtype)
    for tag, part in enumerate(parts):

        @pl.when(mine ^ place == tag)
        def _():
            own[...] = part[...]


def mend(exons, parts, gained, size):
    rows, width = parts[0].shape
    pieces = len(parts)
    whole = jax.ShapeDtypeStruct((rows, width), jnp.bfloat16)
    quarter = rows // pieces
    sent = [
        jax.ShapeDtypeStruct((quarter + (PAD if d in (1, 3) else 0), width), jnp.bfloat16)
        for d in range(1, pieces)
    ]
    outs = pl.pallas_call(
        functools.partial(mend_kernel, pieces=pieces, nblocks=rows // 2 // size, size=size),
        out_shape=[whole] * pieces + sent + [whole],
        in_specs=[SMEM] + [VMEM] * (2 * pieces),
        out_specs=[VMEM] * (pieces + len(sent) + 1),
        input_output_aliases={1 + at: at for at in range(pieces)},
        cost_estimate=LITTLE,
        compiler_params=pltpu.CompilerParams(vmem_limit_bytes=24 * MIB),
    )(exons, *parts, *gained)
    return outs[:pieces], outs[pieces:-1], outs[-1]


def gathered_gradient(pre_act, out_grad, coverage_obs, owners, exon_blocks):
    rows, width = pre_act.shape
    nseq = lax.axis_size("seq")
    mine = lax.axis_index("seq")
    most, block = coverage_obs.shape[1:3]
    nblocks = rows // 2 // block
    counts = owners.shape[0]
    value = pre_act.astype(jnp.float32)
    normal = 0.5 * (1.0 + jax.scipy.special.erf(value * HALF_ROOT))
    slope = normal + value * jnp.exp(-0.5 * value * value) * DENSITY
    act = value * normal
    pooled = (0.5 * jnp.sum(act.reshape(rows // 2, 2, width), axis=1)).astype(jnp.bfloat16)
    order = jnp.arange(counts, dtype=jnp.int32)
    same = owners[:, None] == owners[None, :]
    rank = jnp.sum((same & (order[:, None] < order[None, :])).astype(jnp.int32), axis=0)
    dest = jnp.arange(nseq, dtype=jnp.int32)
    slots = jnp.arange(most, dtype=jnp.int32)
    route = (owners[None, None, :] == dest[:, None, None]) & (
        rank[None, None, :] == slots[None, :, None]
    )
    route = route.astype(jnp.float32).reshape(nseq * most, counts)
    on_mine = exon_blocks // nblocks == mine
    holds = jnp.any(on_mine, axis=1)
    local_block = jnp.sum(jnp.where(on_mine, exon_blocks % nblocks, 0), axis=1)
    select = (
        holds[:, None] & (local_block[:, None] == jnp.arange(nblocks, dtype=jnp.int32)[None, :])
    ).astype(jnp.float32)
    picker = jnp.dot(route, select, precision=lax.Precision.HIGHEST).astype(jnp.bfloat16)
    pieces = pooled.reshape(nblocks, block * width)
    outgoing = jnp.dot(picker, pieces, preferred_element_type=jnp.float32).astype(jnp.bfloat16)
    outgoing = outgoing.reshape(nseq, most, block, width)
    arrived = lax.all_to_all(outgoing, "seq", split_axis=0, concat_axis=0, tiled=True)
    coverage = jnp.sum(arrived.astype(jnp.float32), axis=0)
    splice = jnp.tanh(coverage - coverage_obs[0]).astype(jnp.bfloat16)
    returned = lax.all_gather(splice, "seq", axis=0).reshape(nseq * most, block * width)
    gained = jnp.dot(picker.T, returned, preferred_element_type=jnp.float32)
    pooled_grad = out_grad.astype(jnp.float32) + gained.reshape(rows // 2, width)
    return (jnp.repeat(pooled_grad, 2, axis=0) * 0.5 * slope).astype(jnp.bfloat16)


def local(x_saved, pre_act, out_grad, conv_w, coverage_obs, owners, exon_blocks):
    rows, width = x_saved.shape
    taps = conv_w.shape[1]
    nseq = lax.axis_size("seq")
    nch = lax.axis_size("ch")
    chunk = conv_w.shape[0] // nseq
    most = coverage_obs.shape[1]
    size = coverage_obs.shape[2]
    direct = nseq == nch == 4 and chunk == width and width % 128 == 0
    exons = exon_blocks.T
    weights = conv_w.transpose(1, 0, 2)
    target = coverage_obs[0].reshape(most * size, width)

    if not direct:
        pre_grad = gathered_gradient(pre_act, out_grad, coverage_obs, owners, exon_blocks)
        x_all = lax.all_gather(x_saved, "seq", axis=0, tiled=True)
        whole = lax.all_gather(pre_grad, "ch", axis=1, tiled=True)
        blocks = whole.reshape(rows, nseq, chunk).transpose(1, 0, 2)
        g_all = lax.all_to_all(blocks, "seq", 0, 0, tiled=True).reshape(nseq * rows, chunk)
        low = shift(whole[rows - PAD :], "seq", 1)
        high = shift(whole[:PAD], "seq", -1)
        in_grad = input_gradient(whole, low, high, weights)
        total = nseq * rows
        (w_grad,) = weight_gradient(
            [x_all], [g_all], lambda: ([PAD], [0], [0], [], []), total, taps, total
        )
        return (in_grad, w_grad.transpose(1, 0, 2))

    outgoing = front(owners, exons, pre_act, most, size, nseq)
    slope, plain = plain_gradient(pre_act, out_grad)
    arrived = [outgoing[0]] + [swap(outgoing[d], "seq", d) for d in range(1, nseq)]
    (source,) = after([x_saved], outgoing)
    up1, down1 = shift(source, "seq", 1), shift(source, "seq", -1)
    *arrived, plain, slope = after([*arrived, plain, slope])
    far, near = swap(plain, "ch", 2), swap(plain, "ch", 1)
    coverage = functools.reduce(jnp.add, [a.astype(jnp.float32) for a in arrived])
    splice = jnp.tanh(coverage - target).astype(jnp.bfloat16)
    splices = [splice] + [swap(splice, "seq", d) for d in range(1, nseq)]
    gained = gained_rows(owners, exons, out_grad, slope, splices, most, size, nseq)
    gained, up1, down1 = after([gained, up1, down1])

    far_gained, near_gained = swap(gained, "ch", 2), swap(gained, "ch", 1)
    up2, down2 = shift(up1, "seq", 1, 1), shift(down1, "seq", -1, 1)
    beyond = swap(far, "ch", 1)
    gained = [gained, near_gained, far_gained, swap(far_gained, "ch", 1)]
    *gained, beyond, up2, down2 = after([*gained, beyond, up2, down2])

    quarter = rows // nch
    parts, sent, own = mend(exons, [plain, near, far, beyond], gained, size)
    *sent, up2, down2 = after([*sent, up2, down2])
    got = [swap(block, "seq", d) for d, block in zip(range(1, nseq), sent)]
    up3, down3 = shift(up2, "seq", 1, 2), shift(down2, "seq", -1, 2)

    def origins():
        return [(lax.axis_index("ch") ^ t) * width for t in range(nch)]

    partial, laid = weight_gradient(
        [up1[rows - PAD :], x_saved, down1[:PAD]],
        [own],
        lambda: ([0, PAD, PAD + rows], [0], [0], [], []),
        rows,
        taps,
        rows,
        last=False,
        vmem=24,
        weights=weights,
        origins=origins,
    )
    center = pieces_gradient(parts, laid, taps)
    *got, partial, center = after([*got, partial, center])

    crossing = jnp.concatenate([block[:quarter] for block in got])
    across = swap(crossing, "ch", 2)
    beside = swap(crossing, "ch", 1)
    in_grad = pieces_gradient(parts, laid, taps, [got[0], got[2], center])
    across, in_grad, up3, down3 = after([across, in_grad, up3, down3])
    beyond = swap(across, "ch", 1)

    def layout():
        mine = lax.axis_index("seq")
        place = lax.axis_index("ch")
        x_rows = [PAD + mine * rows]
        for hop in range(1, nseq):
            low_at, high_at = mine - hop, mine + hop
            x_rows += [
                jnp.where(low_at >= 0, PAD + low_at * rows, -1),
                jnp.where(high_at < nseq, PAD + high_at * rows, -1),
            ]
        g_rows = [
            (mine ^ d) * rows + (place ^ tag) * quarter
            for tag in range(nch)
            for d in range(1, nseq)
        ]
        return x_rows, g_rows, [(mine ^ d) * rows for d in range(1, nseq)], [], []

    g_pieces = []
    for piece in (crossing, beside, across, beyond):
        g_pieces += [piece[d * quarter : (d + 1) * quarter] for d in range(nseq - 1)]
    (w_grad,) = weight_gradient(
        [x_saved, up1, down1, up2, down2, up3, down3],
        g_pieces,
        layout,
        rows,
        taps,
        nseq * rows,
        before=partial,
        vmem=32,
    )
    return (in_grad, w_grad.transpose(1, 0, 2))


def solution(mesh):
    in_specs = (
        P(("grp", "seq"), "ch"),
        P(("grp", "seq"), "ch"),
        P(("grp", "seq"), "ch"),
        P(None, None, "ch"),
        P(("grp", "seq"), None, None, "ch"),
        P("grp"),
        P("grp", None),
    )
    out_specs = (P(("grp", "seq"), "ch"), P(("grp", "seq"), None, "ch"))
    return jax.shard_map(local, mesh=mesh, in_specs=in_specs, out_specs=out_specs, check_vma=False)
```

```python
import functools

import jax
import jax.numpy as jnp
from jax import lax
from jax.experimental import pallas as pl
from jax.experimental.pallas import tpu as pltpu
from jax.sharding import PartitionSpec as P

PAD = 16
MIB = 1024 * 1024
VMEM = pl.BlockSpec(memory_space=pltpu.VMEM)
SMEM = pl.BlockSpec(memory_space=pltpu.SMEM)
SOME = pl.BlockSpec(memory_space=pl.ANY)
HALF_ROOT = 0.7071067811865476
DENSITY = 0.3989422804014327
LANES = 128
LONG = pl.CostEstimate(flops=10**10, bytes_accessed=1000, transcendentals=0)
LITTLE = pl.CostEstimate(flops=1000, bytes_accessed=1000, transcendentals=0)


def swap(block, axis, flip):
    count = lax.axis_size(axis)
    return lax.ppermute(block, axis, [(i, i ^ flip) for i in range(count)])


def shift(block, axis, step, first=0):
    count = lax.axis_size(axis)
    if step > 0:
        pairs = [(i, i + 1) for i in range(first, count - 1)]
    else:
        pairs = [(i + 1, i) for i in range(count - 1 - first)]
    return lax.ppermute(block, axis, pairs)


def after(values, others=()):
    return lax.optimization_barrier(tuple(values) + tuple(others))[: len(values)]


def input_kernel(part, low, high, weights, out, block):
    taps = weights.shape[0]
    rows = part.shape[0]
    half = taps // 2
    block[pl.ds(0, PAD), :] = low[...]
    block[pl.ds(PAD, rows), :] = part[...]
    block[pl.ds(PAD + rows, PAD), :] = high[...]
    tile = min(256, rows)

    def body(step, carry):
        start = pl.multiple_of(step * tile, tile)
        rows_in = block[pl.ds(start, tile + 2 * PAD), :]
        total = None
        for tap in range(taps):
            term = jnp.dot(rows_in, weights[tap], preferred_element_type=jnp.float32)
            first = PAD + half - tap
            term = term[first : first + tile]
            total = term if total is None else total + term
        out[pl.ds(start, tile), :] = total.astype(out.dtype)
        return carry

    lax.fori_loop(0, rows // tile, body, 0)


def input_gradient(part, low, high, weights):
    taps, chans, width = weights.shape
    rows = part.shape[0]
    return pl.pallas_call(
        input_kernel,
        out_shape=jax.ShapeDtypeStruct((rows, width), jnp.bfloat16),
        in_specs=[VMEM] * 4,
        out_specs=VMEM,
        scratch_shapes=[pltpu.VMEM((rows + 2 * PAD, chans), jnp.bfloat16)],
        compiler_params=pltpu.CompilerParams(vmem_limit_bytes=32 * MIB),
    )(part, low, high, weights)


def pieces_kernel(*refs, taps, pieces, middle):
    parts, rest = refs[:pieces], refs[pieces:]
    if middle:
        weights, out, block = rest
    else:
        near_edge, far_edge, center, weights, out, block = rest
    rows = parts[0].shape[0]
    width = weights.shape[1] // taps
    half = taps // 2
    quarter = rows // 4
    kept = [(0, rows)] if middle else [(0, quarter + PAD), (rows - quarter - PAD, quarter + PAD)]
    base = 0
    for part in parts:
        span = pl.ds(base, part.shape[1])
        for begin, count in kept:
            block[pl.ds(PAD + begin, count), span] = part[pl.ds(begin, count), :]
        base += part.shape[1]
    if not middle:
        mine = lax.axis_index("seq")
        one = near_edge[pl.ds(quarter, PAD), :].astype(jnp.float32)
        other = far_edge[pl.ds(quarter, PAD), :].astype(jnp.float32)
        low = jnp.where(mine % 2 == 1, one, jnp.where(mine == 2, other, 0.0))
        high = jnp.where(mine % 2 == 0, one, jnp.where(mine == 1, other, 0.0))
        for at in range(pieces):
            span = pl.ds(at * part.shape[1], part.shape[1])
            lower = pltpu.roll(low, PAD - half - half * at, 0)
            upper = pltpu.roll(high, (PAD - half * at) % PAD, 0)
            block[pl.ds(0, PAD), span] = lower.astype(block.dtype)
            block[pl.ds(PAD + rows, PAD), span] = upper.astype(block.dtype)

    def tile(start, count):
        terms = jnp.dot(
            block[pl.ds(start, count + 2 * PAD), :],
            weights[...],
            preferred_element_type=jnp.float32,
        )
        total = None
        for tap in range(taps):
            first = PAD + half - tap
            term = terms[first : first + count, tap * width : (tap + 1) * width]
            total = term if total is None else total + term
        return total.astype(out.dtype)

    if middle:
        out[...] = tile(quarter, 2 * quarter)
    else:
        out[pl.ds(0, quarter), :] = tile(0, quarter)
        out[pl.ds(quarter, 2 * quarter), :] = center[...]
        out[pl.ds(3 * quarter, quarter), :] = tile(3 * quarter, quarter)


def pieces_gradient(parts, weights, taps, rest=()):
    chans = weights.shape[0]
    width = weights.shape[1] // taps
    rows = parts[0].shape[0]
    middle = not rest
    return pl.pallas_call(
        functools.partial(pieces_kernel, taps=taps, pieces=len(parts), middle=middle),
        out_shape=jax.ShapeDtypeStruct((rows // 2 if middle else rows, width), jnp.bfloat16),
        in_specs=[VMEM] * (len(parts) + len(rest) + 1),
        out_specs=VMEM,
        scratch_shapes=[pltpu.VMEM((rows + 2 * PAD, chans), jnp.bfloat16)],
        cost_estimate=LITTLE,
        compiler_params=pltpu.CompilerParams(vmem_limit_bytes=24 * MIB),
    )(*parts, *rest, weights)


def weight_kernel(*refs, taps, tile, rows, size, nx, ng, layout, first, last, origins, span, stages):
    xs, gs, rest = refs[:nx], refs[nx : nx + ng], list(refs[nx + ng :])
    before = None if first else rest.pop(0)
    weights = rest.pop(0) if origins else None
    out = rest.pop(0)
    laid = rest.pop(0) if origins else None
    xbuf, gbuf, acc, sems = rest
    width = xbuf.shape[1]
    half = taps // 2
    x_rows, g_rows, starts, blanks, seams = layout()
    zeros = jnp.zeros((PAD, width), xbuf.dtype)
    xbuf[pl.ds(0, PAD), :] = zeros
    xbuf[pl.ds(PAD + rows, PAD), :] = zeros
    for wanted, row in blanks:

        @pl.when(wanted)
        def _():
            xbuf[pl.ds(row, PAD), :] = zeros

    pieces = [(src, xbuf, row, src.shape[0]) for src, row in zip(xs, x_rows)]
    pieces += [(src, gbuf, row, span or src.shape[0]) for src, row in zip(gs, g_rows)]

    def copy(at):
        src, dst, row, count = pieces[at]
        row = row if isinstance(row, int) else pl.multiple_of(row, 16)
        return pltpu.make_async_copy(
            src.at[pl.ds(0, count), :], dst.at[pl.ds(row, count), :], sems.at[at]
        )

    def each(act, stage=None):
        for at in range(nx + ng):
            if stages and stage is not None and stages[at] != stage:
                continue
            row = pieces[at][2]
            if isinstance(row, int):
                act(at)
            else:
                pl.when(row >= 0)(functools.partial(act, at))

    each(lambda at: copy(at).start())
    moves = []
    if origins:
        where = origins()
        depth = weights.shape[1] // len(where)
        for e, origin in enumerate(where):
            for tap in range(taps):
                moves.append(
                    pltpu.make_async_copy(
                        weights.at[tap, pl.ds(pl.multiple_of(origin, 16), depth), :],
                        laid.at[pl.ds(e * depth, depth), pl.ds(tap * width, width)],
                        sems.at[nx + ng + len(moves)],
                    )
                )
        for move in moves:
            move.start()
    acc[...] = jnp.zeros_like(acc) if first else before[...]
    if not stages:
        each(lambda at: copy(at).wait())

    def add(start, count, side=None):
        grad = gbuf[pl.ds(start, count), :].T
        block = xbuf[pl.ds(start, count + 2 * PAD), :].astype(jnp.float32)
        if side is not None:
            row = lax.broadcasted_iota(jnp.int32, block.shape, 0)
            block = jnp.where(row >= count + PAD if side > 0 else row < PAD, block, 0.0)
        moved = []
        for tap in range(taps):
            at = PAD - half + tap
            moved.append(block[at : at + count].astype(jnp.bfloat16))
        if width % LANES:
            for tap in range(taps):
                acc[tap] += jnp.dot(grad, moved[tap], preferred_element_type=jnp.float32)
        else:
            moved = jnp.concatenate(moved, axis=1)
            acc[...] += jnp.dot(grad, moved, preferred_element_type=jnp.float32)

    for stage, begin in enumerate(starts):
        if stages:
            each(lambda at: copy(at).wait(), stage)

        def body(step, carry):
            add(pl.multiple_of(begin + step * tile, 16), tile)
            return carry

        lax.fori_loop(0, size // tile, body, 0)
    for wanted, row, side in seams:
        pl.when(wanted)(functools.partial(add, row, PAD, side))
    if last and width % LANES == 0:
        for tap in range(taps):
            out[tap] = acc[:, tap * width : (tap + 1) * width].astype(out.dtype)
    else:
        out[...] = acc[...].astype(out.dtype)
    for move in moves:
        move.wait()


def weight_gradient(
    xs, gs, layout, size, taps, rows, before=None, last=True, vmem=40, weights=None, origins=None, span=None,
    stages=None
):
    width, chunk = xs[0].shape[1], gs[0].shape[1]
    split = (taps, chunk, width)
    joined = split if width % LANES else (chunk, taps * width)
    out_shape = [
        jax.ShapeDtypeStruct(split, jnp.bfloat16)
        if last
        else jax.ShapeDtypeStruct(joined, jnp.float32)
    ]
    moves = 0
    if origins:
        moves = taps * 4
        out_shape.append(
            jax.ShapeDtypeStruct((weights.shape[1], taps * width), weights.dtype)
        )
    return pl.pallas_call(
        functools.partial(
            weight_kernel,
            taps=taps,
            tile=min(1024, size) if width % LANES == 0 else min(512, size),
            rows=rows,
            size=size,
            nx=len(xs),
            ng=len(gs),
            layout=layout,
            first=before is None,
            last=last,
            origins=origins,
            span=span,
            stages=stages,
        ),
        out_shape=out_shape,
        in_specs=[SOME] * (len(xs) + len(gs))
        + [VMEM] * (before is not None)
        + [SOME] * (weights is not None),
        out_specs=[VMEM] * len(out_shape),
        scratch_shapes=[
            pltpu.VMEM((rows + 2 * PAD, width), jnp.bfloat16),
            pltpu.VMEM((rows, chunk), jnp.bfloat16),
            pltpu.VMEM(joined, jnp.float32),
            pltpu.SemaphoreType.DMA((len(xs) + len(gs) + moves,)),
        ],
        cost_estimate=LITTLE,
        compiler_params=pltpu.CompilerParams(vmem_limit_bytes=vmem * MIB),
    )(
        *xs,
        *gs,
        *([] if before is None else [before]),
        *([] if weights is None else [weights]),
    )


def merge_pairs(value, scratch):
    size = value.shape[0] // 2
    sums = []
    for at in range(value.shape[1] // LANES):
        scratch[at] = value[:, at * LANES : (at + 1) * LANES]
        even = scratch[at, pl.ds(0, size, stride=2), :]
        sums.append(even + scratch[at, pl.ds(1, size, stride=2), :])
    return jnp.concatenate(sums, axis=1)


def make_pairs(value, scratch):
    size = value.shape[0]
    rows = []
    for at in range(value.shape[1] // LANES):
        part = value[:, at * LANES : (at + 1) * LANES]
        scratch[at, pl.ds(0, size, stride=2), :] = part
        scratch[at, pl.ds(1, size, stride=2), :] = part
        rows.append(scratch[at])
    return jnp.concatenate(rows, axis=1)


def pair_scratch(rows, width):
    return pltpu.VMEM((width // LANES, rows, LANES), jnp.float32)


def each_exon(owners, exons, seen, nblocks, most, act):
    mine = lax.axis_index("seq")
    span, count = exons.shape
    for i in range(seen.shape[0]):
        seen[i] = 0

    def body(t, carry):
        owner = owners[t]
        slot = (owner ^ mine) * most + seen[owner]
        seen[owner] += 1
        for e in range(span):
            where = exons[e, t]

            @pl.when(where // nblocks == mine)
            def _():
                act(t, slot, where % nblocks)

        return carry

    lax.fori_loop(0, count, body, 0)


def front_kernel(owners, exons, pre_act, *refs, nblocks, most, size):
    outs, (slots, pair, seen) = refs[:-3], refs[-3:]
    slots[...] = jnp.zeros_like(slots)

    def act(t, slot, block):
        at = pl.ds(pl.multiple_of(block * (2 * size), 2 * size), 2 * size)
        value = pre_act[at, :].astype(jnp.float32)
        value = value * (0.5 * (1.0 + lax.erf(value * HALF_ROOT)))
        mean = 0.5 * merge_pairs(value, pair)
        slots[pl.ds(pl.multiple_of(slot * size, size), size), :] = mean

    each_exon(owners, exons, seen, nblocks, most, act)
    group = most * size
    for d, out in enumerate(outs):
        out[...] = slots[pl.ds(d * group, group), :].astype(out.dtype)


def front(owners, exons, pre_act, most, size, groups):
    rows, width = pre_act.shape
    return pl.pallas_call(
        functools.partial(
            front_kernel, nblocks=rows // 2 // size, most=most, size=size
        ),
        out_shape=[jax.ShapeDtypeStruct((most * size, width), jnp.bfloat16)] * groups,
        in_specs=[SMEM] * 2 + [VMEM],
        out_specs=[VMEM] * groups,
        scratch_shapes=[
            pltpu.VMEM((groups * most * size, width), jnp.float32),
            pair_scratch(2 * size, width),
            pltpu.SMEM((groups,), jnp.int32),
        ],
        cost_estimate=LITTLE,
        compiler_params=pltpu.CompilerParams(vmem_limit_bytes=16 * MIB),
    )(owners, exons, pre_act)


def plain_kernel(pre_act, out_grad, slope, plain, both):
    value = pre_act[...].astype(jnp.float32)
    normal = 0.5 * (1.0 + lax.erf(value * HALF_ROOT))
    slope[...] = normal + value * (jnp.exp(-0.5 * value * value) * DENSITY)
    pooled = make_pairs(out_grad[...].astype(jnp.float32) * 0.5, both)
    plain[...] = (pooled * slope[...]).astype(plain.dtype)


def plain_gradient(pre_act, out_grad):
    rows, width = pre_act.shape
    return pl.pallas_call(
        plain_kernel,
        out_shape=[
            jax.ShapeDtypeStruct((rows, width), jnp.float32),
            jax.ShapeDtypeStruct((rows, width), jnp.bfloat16),
        ],
        in_specs=[VMEM] * 2,
        out_specs=[VMEM] * 2,
        scratch_shapes=[pair_scratch(rows, width)],
        cost_estimate=LITTLE,
        compiler_params=pltpu.CompilerParams(vmem_limit_bytes=16 * MIB),
    )(pre_act, out_grad)


def gain_kernel(owners, exons, out_grad, slope, *refs, nblocks, most, size):
    splices, (grad, gain, held, both, seen) = refs[:-5], refs[-5:]
    gain[...] = out_grad[...].astype(jnp.float32)
    base = 0
    for splice in splices:
        held[pl.ds(base, splice.shape[0]), :] = splice[...].astype(jnp.float32)
        base += splice.shape[0]

    def add(t, slot, block):
        at = pl.ds(pl.multiple_of(block * size, size), size)
        gain[at, :] += held[pl.ds(pl.multiple_of(slot * size, size), size), :]

    def final(block):
        pooled = 0.5 * gain[pl.ds(pl.multiple_of(block * size, size), size), :]
        at = pl.ds(pl.multiple_of(block * (2 * size), 2 * size), 2 * size)
        return make_pairs(pooled, both) * slope[at, :]

    def renew(t, slot, block):
        at = pl.ds(pl.multiple_of(t * (2 * size), 2 * size), 2 * size)
        grad[at, :] = final(block).astype(grad.dtype)

    each_exon(owners, exons, seen, nblocks, most, add)
    each_exon(owners, exons, seen, nblocks, most, renew)
    count = exons.shape[1]
    row = lax.broadcasted_iota(jnp.int32, (2 * size, grad.shape[1]), 0)
    for at, block, first in ((count, 0, 0), (count + 1, nblocks - 1, 2 * size - 2)):
        rows = final(block)
        rows = jnp.where(row % 2 == 0, rows[first : first + 1], rows[first + 1 : first + 2])
        grad[pl.ds(at * 2 * size, 2 * size), :] = rows.astype(grad.dtype)


def gained_rows(owners, exons, out_grad, slope, splices, most, size, groups):
    rows, width = slope.shape
    return pl.pallas_call(
        functools.partial(gain_kernel, nblocks=rows // 2 // size, most=most, size=size),
        out_shape=jax.ShapeDtypeStruct(((exons.shape[1] + 2) * 2 * size, width), jnp.bfloat16),
        in_specs=[SMEM] * 2 + [VMEM] * (2 + len(splices)),
        out_specs=VMEM,
        scratch_shapes=[
            pltpu.VMEM((rows // 2, width), jnp.float32),
            pltpu.VMEM((groups * most * size, width), jnp.float32),
            pair_scratch(2 * size, width),
            pltpu.SMEM((groups,), jnp.int32),
        ],
        cost_estimate=LONG,
        compiler_params=pltpu.CompilerParams(vmem_limit_bytes=16 * MIB),
    )(owners, exons, out_grad, slope, *splices)


def mend_kernel(exons, *refs, pieces, nblocks, size):
    gained, parts, sent, own = (
        refs[pieces : 2 * pieces],
        refs[2 * pieces : 3 * pieces],
        refs[3 * pieces : -1],
        refs[-1],
    )
    mine = lax.axis_index("seq")
    place = lax.axis_index("ch")
    span, count = exons.shape
    rows = parts[0].shape[0]
    quarter = rows // pieces

    def body(t, carry):
        for e in range(span):
            where = exons[e, t]

            @pl.when(where // nblocks == mine)
            def _():
                to = pl.ds(pl.multiple_of(where % nblocks * (2 * size), 2 * size), 2 * size)
                at = pl.ds(pl.multiple_of(t * (2 * size), 2 * size), 2 * size)
                for part, new in zip(parts, gained):
                    part[to, :] = new[at, :]

        return carry

    lax.fori_loop(0, count, body, 0)
    row = lax.broadcasted_iota(jnp.int32, (PAD, own.shape[1]), 0)
    for d, out in enumerate(sent, 1):
        for tag, part in enumerate(parts):

            @pl.when(mine ^ d ^ place == tag)
            def _():
                at = pl.ds(pl.multiple_of(place * quarter, quarter), quarter)
                out[pl.ds(0, quarter), :] = part[at, :]

        if out.shape[0] > quarter:
            after_me = (mine ^ d) > mine
            edge = jnp.zeros(row.shape, jnp.float32)
            for tag, new in enumerate(gained):
                head = new[pl.ds(count * 2 * size, PAD), :].astype(jnp.float32)
                tail = new[pl.ds((count + 1) * 2 * size, PAD), :].astype(jnp.float32)
                edge = jnp.where(row // 2 == tag, jnp.where(after_me, tail, head), edge)
            out[pl.ds(quarter, PAD), :] = edge.astype(out.dtype)
    for tag, part in enumerate(parts):

        @pl.when(mine ^ place == tag)
        def _():
            own[...] = part[...]


def mend(exons, parts, gained, size):
    rows, width = parts[0].shape
    pieces = len(parts)
    whole = jax.ShapeDtypeStruct((rows, width), jnp.bfloat16)
    quarter = rows // pieces
    sent = [
        jax.ShapeDtypeStruct((quarter + (PAD if d in (1, 3) else 0), width), jnp.bfloat16)
        for d in range(1, pieces)
    ]
    outs = pl.pallas_call(
        functools.partial(mend_kernel, pieces=pieces, nblocks=rows // 2 // size, size=size),
        out_shape=[whole] * pieces + sent + [whole],
        in_specs=[SMEM] + [VMEM] * (2 * pieces),
        out_specs=[VMEM] * (pieces + len(sent) + 1),
        input_output_aliases={1 + at: at for at in range(pieces)},
        cost_estimate=LITTLE,
        compiler_params=pltpu.CompilerParams(vmem_limit_bytes=24 * MIB),
    )(exons, *parts, *gained)
    return outs[:pieces], outs[pieces:-1], outs[-1]


def gathered_gradient(pre_act, out_grad, coverage_obs, owners, exon_blocks):
    rows, width = pre_act.shape
    nseq = lax.axis_size("seq")
    mine = lax.axis_index("seq")
    most, block = coverage_obs.shape[1:3]
    nblocks = rows // 2 // block
    counts = owners.shape[0]
    value = pre_act.astype(jnp.float32)
    normal = 0.5 * (1.0 + jax.scipy.special.erf(value * HALF_ROOT))
    slope = normal + value * jnp.exp(-0.5 * value * value) * DENSITY
    act = value * normal
    pooled = (0.5 * jnp.sum(act.reshape(rows // 2, 2, width), axis=1)).astype(jnp.bfloat16)
    order = jnp.arange(counts, dtype=jnp.int32)
    same = owners[:, None] == owners[None, :]
    rank = jnp.sum((same & (order[:, None] < order[None, :])).astype(jnp.int32), axis=0)
    dest = jnp.arange(nseq, dtype=jnp.int32)
    slots = jnp.arange(most, dtype=jnp.int32)
    route = (owners[None, None, :] == dest[:, None, None]) & (
        rank[None, None, :] == slots[None, :, None]
    )
    route = route.astype(jnp.float32).reshape(nseq * most, counts)
    on_mine = exon_blocks // nblocks == mine
    holds = jnp.any(on_mine, axis=1)
    local_block = jnp.sum(jnp.where(on_mine, exon_blocks % nblocks, 0), axis=1)
    select = (
        holds[:, None] & (local_block[:, None] == jnp.arange(nblocks, dtype=jnp.int32)[None, :])
    ).astype(jnp.float32)
    picker = jnp.dot(route, select, precision=lax.Precision.HIGHEST).astype(jnp.bfloat16)
    pieces = pooled.reshape(nblocks, block * width)
    outgoing = jnp.dot(picker, pieces, preferred_element_type=jnp.float32).astype(jnp.bfloat16)
    outgoing = outgoing.reshape(nseq, most, block, width)
    arrived = lax.all_to_all(outgoing, "seq", split_axis=0, concat_axis=0, tiled=True)
    coverage = jnp.sum(arrived.astype(jnp.float32), axis=0)
    splice = jnp.tanh(coverage - coverage_obs[0]).astype(jnp.bfloat16)
    returned = lax.all_gather(splice, "seq", axis=0).reshape(nseq * most, block * width)
    gained = jnp.dot(picker.T, returned, preferred_element_type=jnp.float32)
    pooled_grad = out_grad.astype(jnp.float32) + gained.reshape(rows // 2, width)
    return (jnp.repeat(pooled_grad, 2, axis=0) * 0.5 * slope).astype(jnp.bfloat16)


def local(x_saved, pre_act, out_grad, conv_w, coverage_obs, owners, exon_blocks):
    rows, width = x_saved.shape
    taps = conv_w.shape[1]
    nseq = lax.axis_size("seq")
    nch = lax.axis_size("ch")
    chunk = conv_w.shape[0] // nseq
    most = coverage_obs.shape[1]
    size = coverage_obs.shape[2]
    direct = nseq == nch == 4 and chunk == width and width % 128 == 0
    exons = exon_blocks.T
    weights = conv_w.transpose(1, 0, 2)
    target = coverage_obs[0].reshape(most * size, width)

    if not direct:
        pre_grad = gathered_gradient(pre_act, out_grad, coverage_obs, owners, exon_blocks)
        x_all = lax.all_gather(x_saved, "seq", axis=0, tiled=True)
        whole = lax.all_gather(pre_grad, "ch", axis=1, tiled=True)
        blocks = whole.reshape(rows, nseq, chunk).transpose(1, 0, 2)
        g_all = lax.all_to_all(blocks, "seq", 0, 0, tiled=True).reshape(nseq * rows, chunk)
        low = shift(whole[rows - PAD :], "seq", 1)
        high = shift(whole[:PAD], "seq", -1)
        in_grad = input_gradient(whole, low, high, weights)
        total = nseq * rows
        (w_grad,) = weight_gradient(
            [x_all], [g_all], lambda: ([PAD], [0], [0], [], []), total, taps, total
        )
        return (in_grad, w_grad.transpose(1, 0, 2))

    outgoing = front(owners, exons, pre_act, most, size, nseq)
    slope, plain = plain_gradient(pre_act, out_grad)
    arrived = [outgoing[0]] + [swap(outgoing[d], "seq", d) for d in range(1, nseq)]
    (source,) = after([x_saved], outgoing)
    up1, down1 = shift(source, "seq", 1), shift(source, "seq", -1)
    *arrived, plain, slope = after([*arrived, plain, slope])
    far, near = swap(plain, "ch", 2), swap(plain, "ch", 1)
    coverage = functools.reduce(jnp.add, [a.astype(jnp.float32) for a in arrived])
    splice = jnp.tanh(coverage - target).astype(jnp.bfloat16)
    beside = swap(splice, "seq", 1)
    both = swap(jnp.concatenate([splice, beside]), "seq", 2)
    both, up1, down1 = after([both, up1, down1])
    splices = [splice, beside, both]
    gained = gained_rows(owners, exons, out_grad, slope, splices, most, size, nseq)

    far_gained, near_gained = swap(gained, "ch", 2), swap(gained, "ch", 1)
    up2, down2 = shift(up1, "seq", 1, 1), shift(down1, "seq", -1, 1)
    beyond = swap(far, "ch", 1)
    gained = [gained, near_gained, far_gained, swap(far_gained, "ch", 1)]
    *gained, beyond, up2, down2 = after([*gained, beyond, up2, down2])

    quarter = rows // nch
    parts, sent, own = mend(exons, [plain, near, far, beyond], gained, size)
    *sent, up2, down2 = after([*sent, up2, down2])
    got = [swap(block, "seq", d) for d, block in zip(range(1, nseq), sent)]
    up3, down3 = shift(up2, "seq", 1, 2), shift(down2, "seq", -1, 2)

    def origins():
        return [(lax.axis_index("ch") ^ t) * width for t in range(nch)]

    partial, laid = weight_gradient(
        [up1[rows - PAD :], x_saved, down1[:PAD]],
        [own],
        lambda: ([0, PAD, PAD + rows], [0], [0], [], []),
        rows,
        taps,
        rows,
        last=False,
        vmem=24,
        weights=weights,
        origins=origins,
    )
    center = pieces_gradient(parts, laid, taps)
    *got, partial, center = after([*got, partial, center])

    crossing = jnp.concatenate([block[:quarter] for block in got])
    across = swap(crossing, "ch", 2)
    beside = swap(crossing, "ch", 1)
    in_grad = pieces_gradient(parts, laid, taps, [got[0], got[2], center])
    across, in_grad, up3, down3 = after([across, in_grad, up3, down3])
    beyond = swap(across, "ch", 1)

    def layout():
        mine = lax.axis_index("seq")
        place = lax.axis_index("ch")
        x_rows = [PAD + mine * rows]
        for hop in range(1, nseq):
            low_at, high_at = mine - hop, mine + hop
            x_rows += [
                jnp.where(low_at >= 0, PAD + low_at * rows, -1),
                jnp.where(high_at < nseq, PAD + high_at * rows, -1),
            ]
        g_rows = [
            (mine ^ d) * rows + (place ^ tag) * quarter
            for d in range(1, nseq)
            for tag in range(nch)
        ]
        return x_rows, g_rows, [(mine ^ d) * rows for d in range(1, nseq)], [], []

    g_pieces, stages = [], [0] * 5 + [1] * 2
    for d in range(nseq - 1):
        for piece in (crossing, beside, across, beyond):
            g_pieces.append(piece[d * quarter : (d + 1) * quarter])
            stages.append(d)
    (w_grad,) = weight_gradient(
        [x_saved, up1, down1, up2, down2, up3, down3],
        g_pieces,
        layout,
        rows,
        taps,
        nseq * rows,
        before=partial,
        vmem=32,
        stages=stages,
    )
    return (in_grad, w_grad.transpose(1, 0, 2))


def solution(mesh):
    in_specs = (
        P(("grp", "seq"), "ch"),
        P(("grp", "seq"), "ch"),
        P(("grp", "seq"), "ch"),
        P(None, None, "ch"),
        P(("grp", "seq"), None, None, "ch"),
        P("grp"),
        P("grp", None),
    )
    out_specs = (P(("grp", "seq"), "ch"), P(("grp", "seq"), None, "ch"))
    return jax.shard_map(local, mesh=mesh, in_specs=in_specs, out_specs=out_specs, check_vma=False)
```

```python
import functools

import jax
import jax.numpy as jnp
from jax import lax
from jax.experimental import pallas as pl
from jax.experimental.pallas import tpu as pltpu
from jax.sharding import PartitionSpec as P

PAD = 16
MIB = 1024 * 1024
VMEM = pl.BlockSpec(memory_space=pltpu.VMEM)
SMEM = pl.BlockSpec(memory_space=pltpu.SMEM)
SOME = pl.BlockSpec(memory_space=pl.ANY)
HALF_ROOT = 0.7071067811865476
DENSITY = 0.3989422804014327
LANES = 128
LONG = pl.CostEstimate(flops=10**10, bytes_accessed=1000, transcendentals=0)
LITTLE = pl.CostEstimate(flops=1000, bytes_accessed=1000, transcendentals=0)


def swap(block, axis, flip):
    count = lax.axis_size(axis)
    return lax.ppermute(block, axis, [(i, i ^ flip) for i in range(count)])


def shift(block, axis, step, first=0):
    count = lax.axis_size(axis)
    if step > 0:
        pairs = [(i, i + 1) for i in range(first, count - 1)]
    else:
        pairs = [(i + 1, i) for i in range(count - 1 - first)]
    return lax.ppermute(block, axis, pairs)


def after(values, others=()):
    return lax.optimization_barrier(tuple(values) + tuple(others))[: len(values)]


def input_kernel(part, low, high, weights, out, block):
    taps = weights.shape[0]
    rows = part.shape[0]
    half = taps // 2
    block[pl.ds(0, PAD), :] = low[...]
    block[pl.ds(PAD, rows), :] = part[...]
    block[pl.ds(PAD + rows, PAD), :] = high[...]
    tile = min(256, rows)

    def body(step, carry):
        start = pl.multiple_of(step * tile, tile)
        rows_in = block[pl.ds(start, tile + 2 * PAD), :]
        total = None
        for tap in range(taps):
            term = jnp.dot(rows_in, weights[tap], preferred_element_type=jnp.float32)
            first = PAD + half - tap
            term = term[first : first + tile]
            total = term if total is None else total + term
        out[pl.ds(start, tile), :] = total.astype(out.dtype)
        return carry

    lax.fori_loop(0, rows // tile, body, 0)


def input_gradient(part, low, high, weights):
    taps, chans, width = weights.shape
    rows = part.shape[0]
    return pl.pallas_call(
        input_kernel,
        out_shape=jax.ShapeDtypeStruct((rows, width), jnp.bfloat16),
        in_specs=[VMEM] * 4,
        out_specs=VMEM,
        scratch_shapes=[pltpu.VMEM((rows + 2 * PAD, chans), jnp.bfloat16)],
        compiler_params=pltpu.CompilerParams(vmem_limit_bytes=32 * MIB),
    )(part, low, high, weights)


def pieces_kernel(*refs, taps, pieces, middle):
    parts, rest = refs[:pieces], refs[pieces:]
    if middle:
        weights, out, block = rest
    else:
        near_edge, far_edge, center, weights, out, block = rest
    rows = parts[0].shape[0]
    width = weights.shape[1] // taps
    half = taps // 2
    quarter = rows // 4
    kept = [(0, rows)] if middle else [(0, quarter + PAD), (rows - quarter - PAD, quarter + PAD)]
    base = 0
    for part in parts:
        span = pl.ds(base, part.shape[1])
        for begin, count in kept:
            block[pl.ds(PAD + begin, count), span] = part[pl.ds(begin, count), :]
        base += part.shape[1]
    if not middle:
        mine = lax.axis_index("seq")
        one = near_edge[pl.ds(quarter, PAD), :].astype(jnp.float32)
        other = far_edge[pl.ds(quarter, PAD), :].astype(jnp.float32)
        low = jnp.where(mine % 2 == 1, one, jnp.where(mine == 2, other, 0.0))
        high = jnp.where(mine % 2 == 0, one, jnp.where(mine == 1, other, 0.0))
        for at in range(pieces):
            span = pl.ds(at * part.shape[1], part.shape[1])
            lower = pltpu.roll(low, PAD - half - half * at, 0)
            upper = pltpu.roll(high, (PAD - half * at) % PAD, 0)
            block[pl.ds(0, PAD), span] = lower.astype(block.dtype)
            block[pl.ds(PAD + rows, PAD), span] = upper.astype(block.dtype)

    def tile(start, count):
        terms = jnp.dot(
            block[pl.ds(start, count + 2 * PAD), :],
            weights[...],
            preferred_element_type=jnp.float32,
        )
        total = None
        for tap in range(taps):
            first = PAD + half - tap
            term = terms[first : first + count, tap * width : (tap + 1) * width]
            total = term if total is None else total + term
        return total.astype(out.dtype)

    if middle:
        out[...] = tile(quarter, 2 * quarter)
    else:
        out[pl.ds(0, quarter), :] = tile(0, quarter)
        out[pl.ds(quarter, 2 * quarter), :] = center[...]
        out[pl.ds(3 * quarter, quarter), :] = tile(3 * quarter, quarter)


def pieces_gradient(parts, weights, taps, rest=()):
    chans = weights.shape[0]
    width = weights.shape[1] // taps
    rows = parts[0].shape[0]
    middle = not rest
    return pl.pallas_call(
        functools.partial(pieces_kernel, taps=taps, pieces=len(parts), middle=middle),
        out_shape=jax.ShapeDtypeStruct((rows // 2 if middle else rows, width), jnp.bfloat16),
        in_specs=[VMEM] * (len(parts) + len(rest) + 1),
        out_specs=VMEM,
        scratch_shapes=[pltpu.VMEM((rows + 2 * PAD, chans), jnp.bfloat16)],
        cost_estimate=LITTLE,
        compiler_params=pltpu.CompilerParams(vmem_limit_bytes=24 * MIB),
    )(*parts, *rest, weights)


def weight_kernel(*refs, taps, tile, rows, size, nx, ng, layout, first, last, origins, span, stages):
    xs, gs, rest = refs[:nx], refs[nx : nx + ng], list(refs[nx + ng :])
    before = None if first else rest.pop(0)
    weights = rest.pop(0) if origins else None
    out = rest.pop(0)
    laid = rest.pop(0) if origins else None
    xbuf, gbuf, acc, sems = rest
    width = xbuf.shape[1]
    half = taps // 2
    x_rows, g_rows, starts, blanks, seams = layout()
    zeros = jnp.zeros((PAD, width), xbuf.dtype)
    xbuf[pl.ds(0, PAD), :] = zeros
    xbuf[pl.ds(PAD + rows, PAD), :] = zeros
    for wanted, row in blanks:

        @pl.when(wanted)
        def _():
            xbuf[pl.ds(row, PAD), :] = zeros

    pieces = [(src, xbuf, row, src.shape[0]) for src, row in zip(xs, x_rows)]
    pieces += [(src, gbuf, row, span or src.shape[0]) for src, row in zip(gs, g_rows)]

    def copy(at):
        src, dst, row, count = pieces[at]
        row = row if isinstance(row, int) else pl.multiple_of(row, 16)
        return pltpu.make_async_copy(
            src.at[pl.ds(0, count), :], dst.at[pl.ds(row, count), :], sems.at[at]
        )

    def each(act, stage=None):
        for at in range(nx + ng):
            if stages and stage is not None and stages[at] != stage:
                continue
            row = pieces[at][2]
            if isinstance(row, int):
                act(at)
            else:
                pl.when(row >= 0)(functools.partial(act, at))

    each(lambda at: copy(at).start())
    moves = []
    if origins:
        where = origins()
        depth = weights.shape[1] // len(where)
        for e, origin in enumerate(where):
            for tap in range(taps):
                moves.append(
                    pltpu.make_async_copy(
                        weights.at[tap, pl.ds(pl.multiple_of(origin, 16), depth), :],
                        laid.at[pl.ds(e * depth, depth), pl.ds(tap * width, width)],
                        sems.at[nx + ng + len(moves)],
                    )
                )
        for move in moves:
            move.start()
    acc[...] = jnp.zeros_like(acc) if first else before[...]
    if not stages:
        each(lambda at: copy(at).wait())

    def add(start, count, side=None):
        grad = gbuf[pl.ds(start, count), :].T
        block = xbuf[pl.ds(start, count + 2 * PAD), :].astype(jnp.float32)
        if side is not None:
            row = lax.broadcasted_iota(jnp.int32, block.shape, 0)
            block = jnp.where(row >= count + PAD if side > 0 else row < PAD, block, 0.0)
        moved = []
        for tap in range(taps):
            at = PAD - half + tap
            moved.append(block[at : at + count].astype(jnp.bfloat16))
        if width % LANES:
            for tap in range(taps):
                acc[tap] += jnp.dot(grad, moved[tap], preferred_element_type=jnp.float32)
        else:
            moved = jnp.concatenate(moved, axis=1)
            acc[...] += jnp.dot(grad, moved, preferred_element_type=jnp.float32)

    for stage, begin in enumerate(starts):
        if stages:
            each(lambda at: copy(at).wait(), stage)

        def body(step, carry):
            add(pl.multiple_of(begin + step * tile, 16), tile)
            return carry

        lax.fori_loop(0, size // tile, body, 0)
    for wanted, row, side in seams:
        pl.when(wanted)(functools.partial(add, row, PAD, side))
    if last and width % LANES == 0:
        for tap in range(taps):
            out[tap] = acc[:, tap * width : (tap + 1) * width].astype(out.dtype)
    else:
        out[...] = acc[...].astype(out.dtype)
    for move in moves:
        move.wait()


def weight_gradient(
    xs, gs, layout, size, taps, rows, before=None, last=True, vmem=40, weights=None, origins=None, span=None,
    stages=None
):
    width, chunk = xs[0].shape[1], gs[0].shape[1]
    split = (taps, chunk, width)
    joined = split if width % LANES else (chunk, taps * width)
    out_shape = [
        jax.ShapeDtypeStruct(split, jnp.bfloat16)
        if last
        else jax.ShapeDtypeStruct(joined, jnp.float32)
    ]
    moves = 0
    if origins:
        moves = taps * 4
        out_shape.append(
            jax.ShapeDtypeStruct((weights.shape[1], taps * width), weights.dtype)
        )
    return pl.pallas_call(
        functools.partial(
            weight_kernel,
            taps=taps,
            tile=min(1024, size) if width % LANES == 0 else min(512, size),
            rows=rows,
            size=size,
            nx=len(xs),
            ng=len(gs),
            layout=layout,
            first=before is None,
            last=last,
            origins=origins,
            span=span,
            stages=stages,
        ),
        out_shape=out_shape,
        in_specs=[SOME] * (len(xs) + len(gs))
        + [VMEM] * (before is not None)
        + [SOME] * (weights is not None),
        out_specs=[VMEM] * len(out_shape),
        scratch_shapes=[
            pltpu.VMEM((rows + 2 * PAD, width), jnp.bfloat16),
            pltpu.VMEM((rows, chunk), jnp.bfloat16),
            pltpu.VMEM(joined, jnp.float32),
            pltpu.SemaphoreType.DMA((len(xs) + len(gs) + moves,)),
        ],
        cost_estimate=LITTLE,
        compiler_params=pltpu.CompilerParams(vmem_limit_bytes=vmem * MIB),
    )(
        *xs,
        *gs,
        *([] if before is None else [before]),
        *([] if weights is None else [weights]),
    )


def merge_pairs(value, scratch):
    size = value.shape[0] // 2
    sums = []
    for at in range(value.shape[1] // LANES):
        scratch[at] = value[:, at * LANES : (at + 1) * LANES]
        even = scratch[at, pl.ds(0, size, stride=2), :]
        sums.append(even + scratch[at, pl.ds(1, size, stride=2), :])
    return jnp.concatenate(sums, axis=1)


def make_pairs(value, scratch):
    size = value.shape[0]
    rows = []
    for at in range(value.shape[1] // LANES):
        part = value[:, at * LANES : (at + 1) * LANES]
        scratch[at, pl.ds(0, size, stride=2), :] = part
        scratch[at, pl.ds(1, size, stride=2), :] = part
        rows.append(scratch[at])
    return jnp.concatenate(rows, axis=1)


def pair_scratch(rows, width):
    return pltpu.VMEM((width // LANES, rows, LANES), jnp.float32)


def each_exon(owners, exons, seen, nblocks, most, act):
    mine = lax.axis_index("seq")
    span, count = exons.shape
    for i in range(seen.shape[0]):
        seen[i] = 0

    def body(t, carry):
        owner = owners[t]
        slot = (owner ^ mine) * most + seen[owner]
        seen[owner] += 1
        for e in range(span):
            where = exons[e, t]

            @pl.when(where // nblocks == mine)
            def _():
                act(t, slot, where % nblocks)

        return carry

    lax.fori_loop(0, count, body, 0)


def front_kernel(owners, exons, pre_act, *refs, nblocks, most, size):
    outs, (slots, pair, seen) = refs[:-3], refs[-3:]
    slots[...] = jnp.zeros_like(slots)

    def act(t, slot, block):
        at = pl.ds(pl.multiple_of(block * (2 * size), 2 * size), 2 * size)
        value = pre_act[at, :].astype(jnp.float32)
        value = value * (0.5 * (1.0 + lax.erf(value * HALF_ROOT)))
        mean = 0.5 * merge_pairs(value, pair)
        slots[pl.ds(pl.multiple_of(slot * size, size), size), :] = mean

    each_exon(owners, exons, seen, nblocks, most, act)
    group = most * size
    for d, out in enumerate(outs):
        out[...] = slots[pl.ds(d * group, group), :].astype(out.dtype)


def front(owners, exons, pre_act, most, size, groups):
    rows, width = pre_act.shape
    return pl.pallas_call(
        functools.partial(
            front_kernel, nblocks=rows // 2 // size, most=most, size=size
        ),
        out_shape=[jax.ShapeDtypeStruct((most * size, width), jnp.bfloat16)] * groups,
        in_specs=[SMEM] * 2 + [VMEM],
        out_specs=[VMEM] * groups,
        scratch_shapes=[
            pltpu.VMEM((groups * most * size, width), jnp.float32),
            pair_scratch(2 * size, width),
            pltpu.SMEM((groups,), jnp.int32),
        ],
        cost_estimate=LITTLE,
        compiler_params=pltpu.CompilerParams(vmem_limit_bytes=16 * MIB),
    )(owners, exons, pre_act)


def plain_kernel(pre_act, out_grad, slope, plain, both):
    value = pre_act[...].astype(jnp.float32)
    normal = 0.5 * (1.0 + lax.erf(value * HALF_ROOT))
    slope[...] = normal + value * (jnp.exp(-0.5 * value * value) * DENSITY)
    pooled = make_pairs(out_grad[...].astype(jnp.float32) * 0.5, both)
    plain[...] = (pooled * slope[...]).astype(plain.dtype)


def plain_gradient(pre_act, out_grad):
    rows, width = pre_act.shape
    return pl.pallas_call(
        plain_kernel,
        out_shape=[
            jax.ShapeDtypeStruct((rows, width), jnp.float32),
            jax.ShapeDtypeStruct((rows, width), jnp.bfloat16),
        ],
        in_specs=[VMEM] * 2,
        out_specs=[VMEM] * 2,
        scratch_shapes=[pair_scratch(rows, width)],
        cost_estimate=LITTLE,
        compiler_params=pltpu.CompilerParams(vmem_limit_bytes=16 * MIB),
    )(pre_act, out_grad)


def gain_kernel(owners, exons, out_grad, slope, *refs, nblocks, most, size):
    splices, (grad, gain, held, both, seen) = refs[:-5], refs[-5:]
    gain[...] = out_grad[...].astype(jnp.float32)
    base = 0
    for splice in splices:
        held[pl.ds(base, splice.shape[0]), :] = splice[...].astype(jnp.float32)
        base += splice.shape[0]

    def add(t, slot, block):
        at = pl.ds(pl.multiple_of(block * size, size), size)
        gain[at, :] += held[pl.ds(pl.multiple_of(slot * size, size), size), :]

    def final(block):
        pooled = 0.5 * gain[pl.ds(pl.multiple_of(block * size, size), size), :]
        at = pl.ds(pl.multiple_of(block * (2 * size), 2 * size), 2 * size)
        return make_pairs(pooled, both) * slope[at, :]

    def renew(t, slot, block):
        at = pl.ds(pl.multiple_of(t * (2 * size), 2 * size), 2 * size)
        grad[at, :] = final(block).astype(grad.dtype)

    each_exon(owners, exons, seen, nblocks, most, add)
    each_exon(owners, exons, seen, nblocks, most, renew)
    count = exons.shape[1]
    row = lax.broadcasted_iota(jnp.int32, (2 * size, grad.shape[1]), 0)
    for at, block, first in ((count, 0, 0), (count + 1, nblocks - 1, 2 * size - 2)):
        rows = final(block)
        rows = jnp.where(row % 2 == 0, rows[first : first + 1], rows[first + 1 : first + 2])
        grad[pl.ds(at * 2 * size, 2 * size), :] = rows.astype(grad.dtype)


def gained_rows(owners, exons, out_grad, slope, splices, most, size, groups):
    rows, width = slope.shape
    return pl.pallas_call(
        functools.partial(gain_kernel, nblocks=rows // 2 // size, most=most, size=size),
        out_shape=jax.ShapeDtypeStruct(((exons.shape[1] + 2) * 2 * size, width), jnp.bfloat16),
        in_specs=[SMEM] * 2 + [VMEM] * (2 + len(splices)),
        out_specs=VMEM,
        scratch_shapes=[
            pltpu.VMEM((rows // 2, width), jnp.float32),
            pltpu.VMEM((groups * most * size, width), jnp.float32),
            pair_scratch(2 * size, width),
            pltpu.SMEM((groups,), jnp.int32),
        ],
        cost_estimate=LONG,
        compiler_params=pltpu.CompilerParams(vmem_limit_bytes=16 * MIB),
    )(owners, exons, out_grad, slope, *splices)


def mend_kernel(exons, *refs, pieces, nblocks, size):
    gained, parts, sent, own = (
        refs[pieces : 2 * pieces],
        refs[2 * pieces : 3 * pieces],
        refs[3 * pieces : -1],
        refs[-1],
    )
    mine = lax.axis_index("seq")
    place = lax.axis_index("ch")
    span, count = exons.shape
    rows = parts[0].shape[0]
    quarter = rows // pieces

    def body(t, carry):
        for e in range(span):
            where = exons[e, t]

            @pl.when(where // nblocks == mine)
            def _():
                to = pl.ds(pl.multiple_of(where % nblocks * (2 * size), 2 * size), 2 * size)
                at = pl.ds(pl.multiple_of(t * (2 * size), 2 * size), 2 * size)
                for part, new in zip(parts, gained):
                    part[to, :] = new[at, :]

        return carry

    lax.fori_loop(0, count, body, 0)
    row = lax.broadcasted_iota(jnp.int32, (PAD, own.shape[1]), 0)
    for d, out in enumerate(sent, 1):
        for tag, part in enumerate(parts):

            @pl.when(mine ^ d ^ place == tag)
            def _():
                at = pl.ds(pl.multiple_of(place * quarter, quarter), quarter)
                out[pl.ds(0, quarter), :] = part[at, :]

        if out.shape[0] > quarter:
            after_me = (mine ^ d) > mine
            edge = jnp.zeros(row.shape, jnp.float32)
            for tag, new in enumerate(gained):
                head = new[pl.ds(count * 2 * size, PAD), :].astype(jnp.float32)
                tail = new[pl.ds((count + 1) * 2 * size, PAD), :].astype(jnp.float32)
                edge = jnp.where(row // 2 == tag, jnp.where(after_me, tail, head), edge)
            out[pl.ds(quarter, PAD), :] = edge.astype(out.dtype)
    for tag, part in enumerate(parts):

        @pl.when(mine ^ place == tag)
        def _():
            own[...] = part[...]


def mend(exons, parts, gained, size):
    rows, width = parts[0].shape
    pieces = len(parts)
    whole = jax.ShapeDtypeStruct((rows, width), jnp.bfloat16)
    quarter = rows // pieces
    sent = [
        jax.ShapeDtypeStruct((quarter + (PAD if d in (1, 3) else 0), width), jnp.bfloat16)
        for d in range(1, pieces)
    ]
    outs = pl.pallas_call(
        functools.partial(mend_kernel, pieces=pieces, nblocks=rows // 2 // size, size=size),
        out_shape=[whole] * pieces + sent + [whole],
        in_specs=[SMEM] + [VMEM] * (2 * pieces),
        out_specs=[VMEM] * (pieces + len(sent) + 1),
        input_output_aliases={1 + at: at for at in range(pieces)},
        cost_estimate=LITTLE,
        compiler_params=pltpu.CompilerParams(vmem_limit_bytes=24 * MIB),
    )(exons, *parts, *gained)
    return outs[:pieces], outs[pieces:-1], outs[-1]


def gathered_gradient(pre_act, out_grad, coverage_obs, owners, exon_blocks):
    rows, width = pre_act.shape
    nseq = lax.axis_size("seq")
    mine = lax.axis_index("seq")
    most, block = coverage_obs.shape[1:3]
    nblocks = rows // 2 // block
    counts = owners.shape[0]
    value = pre_act.astype(jnp.float32)
    normal = 0.5 * (1.0 + jax.scipy.special.erf(value * HALF_ROOT))
    slope = normal + value * jnp.exp(-0.5 * value * value) * DENSITY
    act = value * normal
    pooled = (0.5 * jnp.sum(act.reshape(rows // 2, 2, width), axis=1)).astype(jnp.bfloat16)
    order = jnp.arange(counts, dtype=jnp.int32)
    same = owners[:, None] == owners[None, :]
    rank = jnp.sum((same & (order[:, None] < order[None, :])).astype(jnp.int32), axis=0)
    dest = jnp.arange(nseq, dtype=jnp.int32)
    slots = jnp.arange(most, dtype=jnp.int32)
    route = (owners[None, None, :] == dest[:, None, None]) & (
        rank[None, None, :] == slots[None, :, None]
    )
    route = route.astype(jnp.float32).reshape(nseq * most, counts)
    on_mine = exon_blocks // nblocks == mine
    holds = jnp.any(on_mine, axis=1)
    local_block = jnp.sum(jnp.where(on_mine, exon_blocks % nblocks, 0), axis=1)
    select = (
        holds[:, None] & (local_block[:, None] == jnp.arange(nblocks, dtype=jnp.int32)[None, :])
    ).astype(jnp.float32)
    picker = jnp.dot(route, select, precision=lax.Precision.HIGHEST).astype(jnp.bfloat16)
    pieces = pooled.reshape(nblocks, block * width)
    outgoing = jnp.dot(picker, pieces, preferred_element_type=jnp.float32).astype(jnp.bfloat16)
    outgoing = outgoing.reshape(nseq, most, block, width)
    arrived = lax.all_to_all(outgoing, "seq", split_axis=0, concat_axis=0, tiled=True)
    coverage = jnp.sum(arrived.astype(jnp.float32), axis=0)
    splice = jnp.tanh(coverage - coverage_obs[0]).astype(jnp.bfloat16)
    returned = lax.all_gather(splice, "seq", axis=0).reshape(nseq * most, block * width)
    gained = jnp.dot(picker.T, returned, preferred_element_type=jnp.float32)
    pooled_grad = out_grad.astype(jnp.float32) + gained.reshape(rows // 2, width)
    return (jnp.repeat(pooled_grad, 2, axis=0) * 0.5 * slope).astype(jnp.bfloat16)


def local(x_saved, pre_act, out_grad, conv_w, coverage_obs, owners, exon_blocks):
    rows, width = x_saved.shape
    taps = conv_w.shape[1]
    nseq = lax.axis_size("seq")
    nch = lax.axis_size("ch")
    chunk = conv_w.shape[0] // nseq
    most = coverage_obs.shape[1]
    size = coverage_obs.shape[2]
    direct = nseq == nch == 4 and chunk == width and width % 128 == 0
    exons = exon_blocks.T
    weights = conv_w.transpose(1, 0, 2)
    target = coverage_obs[0].reshape(most * size, width)

    if not direct:
        pre_grad = gathered_gradient(pre_act, out_grad, coverage_obs, owners, exon_blocks)
        x_all = lax.all_gather(x_saved, "seq", axis=0, tiled=True)
        whole = lax.all_gather(pre_grad, "ch", axis=1, tiled=True)
        blocks = whole.reshape(rows, nseq, chunk).transpose(1, 0, 2)
        g_all = lax.all_to_all(blocks, "seq", 0, 0, tiled=True).reshape(nseq * rows, chunk)
        low = shift(whole[rows - PAD :], "seq", 1)
        high = shift(whole[:PAD], "seq", -1)
        in_grad = input_gradient(whole, low, high, weights)
        total = nseq * rows
        (w_grad,) = weight_gradient(
            [x_all], [g_all], lambda: ([PAD], [0], [0], [], []), total, taps, total
        )
        return (in_grad, w_grad.transpose(1, 0, 2))

    outgoing = front(owners, exons, pre_act, most, size, nseq)
    slope, plain = plain_gradient(*after([pre_act, out_grad], outgoing))
    arrived = [outgoing[0]] + [swap(outgoing[d], "seq", d) for d in range(1, nseq)]
    far, near = swap(plain, "ch", 2), swap(plain, "ch", 1)
    *arrived, plain, slope = after([*arrived, plain, slope])
    coverage = functools.reduce(jnp.add, [a.astype(jnp.float32) for a in arrived])
    splice = jnp.tanh(coverage - target).astype(jnp.bfloat16)
    splices = [splice] + [swap(splice, "seq", d) for d in range(1, nseq)]
    (source,) = after([x_saved], [splice])
    up1, down1 = shift(source, "seq", 1), shift(source, "seq", -1)
    *splices, far, near = after([*splices, far, near])
    gained = gained_rows(owners, exons, out_grad, slope, splices, most, size, nseq)

    far_gained, near_gained = swap(gained, "ch", 2), swap(gained, "ch", 1)
    beyond = swap(far, "ch", 1)
    gained = [gained, near_gained, far_gained, swap(far_gained, "ch", 1)]
    *gained, beyond, up1, down1 = after([*gained, beyond, up1, down1])

    quarter = rows // nch
    parts, sent, own = mend(exons, [plain, near, far, beyond], gained, size)
    *sent, up1, down1 = after([*sent, up1, down1])
    got = [swap(block, "seq", d) for d, block in zip(range(1, nseq), sent)]
    up2, down2 = shift(up1, "seq", 1, 1), shift(down1, "seq", -1, 1)

    def origins():
        return [(lax.axis_index("ch") ^ t) * width for t in range(nch)]

    partial, laid = weight_gradient(
        [up1[rows - PAD :], x_saved, down1[:PAD]],
        [own],
        lambda: ([0, PAD, PAD + rows], [0], [0], [], []),
        rows,
        taps,
        rows,
        last=False,
        vmem=24,
        weights=weights,
        origins=origins,
    )
    center = pieces_gradient(parts, laid, taps)
    *got, partial, center = after([*got, partial, center])

    crossing = jnp.concatenate([block[:quarter] for block in got])
    across = swap(crossing, "ch", 2)
    beside = swap(crossing, "ch", 1)
    in_grad = pieces_gradient(parts, laid, taps, [got[0], got[2], center])
    across, in_grad = after([across, in_grad])
    beyond = swap(across, "ch", 1)
    up3, down3 = shift(up2, "seq", 1, 2), shift(down2, "seq", -1, 2)

    seam = (nseq - 1) * rows

    def layout(hops, blocks, closing):
        mine = lax.axis_index("seq")
        place = lax.axis_index("ch")
        x_rows = [PAD + mine * rows]
        for hop in range(1, hops):
            low_at, high_at = mine - hop, mine + hop
            x_rows += [
                jnp.where(low_at >= 0, PAD + low_at * rows, -1),
                jnp.where(high_at < nseq, PAD + high_at * rows, -1),
            ]
        used = (2, 3) if closing else blocks
        g_rows = [
            (mine ^ d) * rows + (place ^ tag) * quarter for d in used for tag in range(nch)
        ]
        starts = [(mine ^ d) * rows for d in blocks]
        if closing:
            seams = [(mine == 0, seam - PAD, 1), (mine == nseq - 1, rows, -1)]
            return x_rows, g_rows, starts, [], seams
        return x_rows, g_rows, starts, [(mine == 0, PAD + seam), (mine == nseq - 1, rows)], []

    def sources(blocks):
        return [
            kind[(d - 1) * quarter : d * quarter]
            for d in blocks
            for kind in (crossing, beside, across, beyond)
        ]

    (partial,) = weight_gradient(
        [x_saved, up1, down1, up2, down2],
        sources((1, 2)),
        functools.partial(layout, 3, (1, 2), False),
        rows,
        taps,
        nseq * rows,
        before=partial,
        last=False,
        vmem=32,
        stages=[0] * 9 + [1] * 4,
    )
    (w_grad,) = weight_gradient(
        [x_saved, up1, down1, up2, down2, up3, down3],
        sources((2, 3)),
        functools.partial(layout, 4, (3,), True),
        rows,
        taps,
        nseq * rows,
        before=after([partial], [in_grad])[0],
        vmem=32,
    )
    return (in_grad, w_grad.transpose(1, 0, 2))


def solution(mesh):
    in_specs = (
        P(("grp", "seq"), "ch"),
        P(("grp", "seq"), "ch"),
        P(("grp", "seq"), "ch"),
        P(None, None, "ch"),
        P(("grp", "seq"), None, None, "ch"),
        P("grp"),
        P("grp", None),
    )
    out_specs = (P(("grp", "seq"), "ch"), P(("grp", "seq"), None, "ch"))
    return jax.shard_map(local, mesh=mesh, in_specs=in_specs, out_specs=out_specs, check_vma=False)
```

```python
import functools

import jax
import jax.numpy as jnp
from jax import lax
from jax.experimental import pallas as pl
from jax.experimental.pallas import tpu as pltpu
from jax.sharding import PartitionSpec as P

PAD = 16
MIB = 1024 * 1024
VMEM = pl.BlockSpec(memory_space=pltpu.VMEM)
SMEM = pl.BlockSpec(memory_space=pltpu.SMEM)
SOME = pl.BlockSpec(memory_space=pl.ANY)
HALF_ROOT = 0.7071067811865476
DENSITY = 0.3989422804014327
LANES = 128
LONG = pl.CostEstimate(flops=5 * 10**9, bytes_accessed=1000, transcendentals=0)
LITTLE = pl.CostEstimate(flops=1000, bytes_accessed=1000, transcendentals=0)


def swap(block, axis, flip):
    count = lax.axis_size(axis)
    return lax.ppermute(block, axis, [(i, i ^ flip) for i in range(count)])


def shift(block, axis, step, first=0):
    count = lax.axis_size(axis)
    if step > 0:
        pairs = [(i, i + 1) for i in range(first, count - 1)]
    else:
        pairs = [(i + 1, i) for i in range(count - 1 - first)]
    return lax.ppermute(block, axis, pairs)


def after(values, others=()):
    return lax.optimization_barrier(tuple(values) + tuple(others))[: len(values)]


def input_kernel(part, low, high, weights, out, block):
    taps = weights.shape[0]
    rows = part.shape[0]
    half = taps // 2
    block[pl.ds(0, PAD), :] = low[...]
    block[pl.ds(PAD, rows), :] = part[...]
    block[pl.ds(PAD + rows, PAD), :] = high[...]
    tile = min(256, rows)

    def body(step, carry):
        start = pl.multiple_of(step * tile, tile)
        rows_in = block[pl.ds(start, tile + 2 * PAD), :]
        total = None
        for tap in range(taps):
            term = jnp.dot(rows_in, weights[tap], preferred_element_type=jnp.float32)
            first = PAD + half - tap
            term = term[first : first + tile]
            total = term if total is None else total + term
        out[pl.ds(start, tile), :] = total.astype(out.dtype)
        return carry

    lax.fori_loop(0, rows // tile, body, 0)


def input_gradient(part, low, high, weights):
    taps, chans, width = weights.shape
    rows = part.shape[0]
    return pl.pallas_call(
        input_kernel,
        out_shape=jax.ShapeDtypeStruct((rows, width), jnp.bfloat16),
        in_specs=[VMEM] * 4,
        out_specs=VMEM,
        scratch_shapes=[pltpu.VMEM((rows + 2 * PAD, chans), jnp.bfloat16)],
        compiler_params=pltpu.CompilerParams(vmem_limit_bytes=32 * MIB),
    )(part, low, high, weights)


def pieces_kernel(*refs, taps, pieces, middle):
    parts, rest = refs[:pieces], refs[pieces:]
    if middle:
        weights, out, block = rest
    else:
        near_edge, far_edge, center, weights, out, block = rest
    rows = parts[0].shape[0]
    width = weights.shape[1] // taps
    half = taps // 2
    quarter = rows // 4
    kept = [(0, rows)] if middle else [(0, quarter + PAD), (rows - quarter - PAD, quarter + PAD)]
    base = 0
    for part in parts:
        span = pl.ds(base, part.shape[1])
        for begin, count in kept:
            block[pl.ds(PAD + begin, count), span] = part[pl.ds(begin, count), :]
        base += part.shape[1]
    if not middle:
        mine = lax.axis_index("seq")
        one = near_edge[pl.ds(quarter, PAD), :].astype(jnp.float32)
        other = far_edge[pl.ds(quarter, PAD), :].astype(jnp.float32)
        low = jnp.where(mine % 2 == 1, one, jnp.where(mine == 2, other, 0.0))
        high = jnp.where(mine % 2 == 0, one, jnp.where(mine == 1, other, 0.0))
        for at in range(pieces):
            span = pl.ds(at * part.shape[1], part.shape[1])
            lower = pltpu.roll(low, PAD - half - half * at, 0)
            upper = pltpu.roll(high, (PAD - half * at) % PAD, 0)
            block[pl.ds(0, PAD), span] = lower.astype(block.dtype)
            block[pl.ds(PAD + rows, PAD), span] = upper.astype(block.dtype)

    def tile(start, count):
        terms = jnp.dot(
            block[pl.ds(start, count + 2 * PAD), :],
            weights[...],
            preferred_element_type=jnp.float32,
        )
        total = None
        for tap in range(taps):
            first = PAD + half - tap
            term = terms[first : first + count, tap * width : (tap + 1) * width]
            total = term if total is None else total + term
        return total.astype(out.dtype)

    if middle:
        out[...] = tile(quarter, 2 * quarter)
    else:
        out[pl.ds(0, quarter), :] = tile(0, quarter)
        out[pl.ds(quarter, 2 * quarter), :] = center[...]
        out[pl.ds(3 * quarter, quarter), :] = tile(3 * quarter, quarter)


def pieces_gradient(parts, weights, taps, rest=()):
    chans = weights.shape[0]
    width = weights.shape[1] // taps
    rows = parts[0].shape[0]
    middle = not rest
    return pl.pallas_call(
        functools.partial(pieces_kernel, taps=taps, pieces=len(parts), middle=middle),
        out_shape=jax.ShapeDtypeStruct((rows // 2 if middle else rows, width), jnp.bfloat16),
        in_specs=[VMEM] * (len(parts) + len(rest) + 1),
        out_specs=VMEM,
        scratch_shapes=[pltpu.VMEM((rows + 2 * PAD, chans), jnp.bfloat16)],
        cost_estimate=LITTLE,
        compiler_params=pltpu.CompilerParams(vmem_limit_bytes=24 * MIB),
    )(*parts, *rest, weights)


def weight_kernel(*refs, taps, tile, rows, size, nx, ng, layout, first, last, origins, span, stages):
    xs, gs, rest = refs[:nx], refs[nx : nx + ng], list(refs[nx + ng :])
    before = None if first else rest.pop(0)
    weights = rest.pop(0) if origins else None
    out = rest.pop(0)
    laid = rest.pop(0) if origins else None
    xbuf, gbuf, acc, sems = rest
    width = xbuf.shape[1]
    half = taps // 2
    x_rows, g_rows, starts, blanks, seams = layout()
    zeros = jnp.zeros((PAD, width), xbuf.dtype)
    xbuf[pl.ds(0, PAD), :] = zeros
    xbuf[pl.ds(PAD + rows, PAD), :] = zeros
    for wanted, row in blanks:

        @pl.when(wanted)
        def _():
            xbuf[pl.ds(row, PAD), :] = zeros

    pieces = [(src, xbuf, row, src.shape[0]) for src, row in zip(xs, x_rows)]
    pieces += [(src, gbuf, row, span or src.shape[0]) for src, row in zip(gs, g_rows)]

    def copy(at):
        src, dst, row, count = pieces[at]
        row = row if isinstance(row, int) else pl.multiple_of(row, 16)
        return pltpu.make_async_copy(
            src.at[pl.ds(0, count), :], dst.at[pl.ds(row, count), :], sems.at[at]
        )

    def each(act, stage=None):
        for at in range(nx + ng):
            if stages and stage is not None and stages[at] != stage:
                continue
            row = pieces[at][2]
            if isinstance(row, int):
                act(at)
            else:
                pl.when(row >= 0)(functools.partial(act, at))

    each(lambda at: copy(at).start())
    moves = []
    if origins:
        where = origins()
        depth = weights.shape[1] // len(where)
        for e, origin in enumerate(where):
            for tap in range(taps):
                moves.append(
                    pltpu.make_async_copy(
                        weights.at[tap, pl.ds(pl.multiple_of(origin, 16), depth), :],
                        laid.at[pl.ds(e * depth, depth), pl.ds(tap * width, width)],
                        sems.at[nx + ng + len(moves)],
                    )
                )
        for move in moves:
            move.start()
    acc[...] = jnp.zeros_like(acc) if first else before[...]
    if not stages:
        each(lambda at: copy(at).wait())

    def add(start, count, side=None):
        grad = gbuf[pl.ds(start, count), :].T
        block = xbuf[pl.ds(start, count + 2 * PAD), :].astype(jnp.float32)
        if side is not None:
            row = lax.broadcasted_iota(jnp.int32, block.shape, 0)
            block = jnp.where(row >= count + PAD if side > 0 else row < PAD, block, 0.0)
        moved = []
        for tap in range(taps):
            at = PAD - half + tap
            moved.append(block[at : at + count].astype(jnp.bfloat16))
        if width % LANES:
            for tap in range(taps):
                acc[tap] += jnp.dot(grad, moved[tap], preferred_element_type=jnp.float32)
        else:
            moved = jnp.concatenate(moved, axis=1)
            acc[...] += jnp.dot(grad, moved, preferred_element_type=jnp.float32)

    for stage, begin in enumerate(starts):
        if stages:
            each(lambda at: copy(at).wait(), stage)

        def body(step, carry):
            add(pl.multiple_of(begin + step * tile, 16), tile)
            return carry

        lax.fori_loop(0, size // tile, body, 0)
    for wanted, row, side in seams:
        pl.when(wanted)(functools.partial(add, row, PAD, side))
    if last and width % LANES == 0:
        for tap in range(taps):
            out[tap] = acc[:, tap * width : (tap + 1) * width].astype(out.dtype)
    else:
        out[...] = acc[...].astype(out.dtype)
    for move in moves:
        move.wait()


def weight_gradient(
    xs, gs, layout, size, taps, rows, before=None, last=True, vmem=40, weights=None, origins=None, span=None,
    stages=None
):
    width, chunk = xs[0].shape[1], gs[0].shape[1]
    split = (taps, chunk, width)
    joined = split if width % LANES else (chunk, taps * width)
    out_shape = [
        jax.ShapeDtypeStruct(split, jnp.bfloat16)
        if last
        else jax.ShapeDtypeStruct(joined, jnp.float32)
    ]
    moves = 0
    if origins:
        moves = taps * 4
        out_shape.append(
            jax.ShapeDtypeStruct((weights.shape[1], taps * width), weights.dtype)
        )
    return pl.pallas_call(
        functools.partial(
            weight_kernel,
            taps=taps,
            tile=min(1024, size) if width % LANES == 0 else min(512, size),
            rows=rows,
            size=size,
            nx=len(xs),
            ng=len(gs),
            layout=layout,
            first=before is None,
            last=last,
            origins=origins,
            span=span,
            stages=stages,
        ),
        out_shape=out_shape,
        in_specs=[SOME] * (len(xs) + len(gs))
        + [VMEM] * (before is not None)
        + [SOME] * (weights is not None),
        out_specs=[VMEM] * len(out_shape),
        scratch_shapes=[
            pltpu.VMEM((rows + 2 * PAD, width), jnp.bfloat16),
            pltpu.VMEM((rows, chunk), jnp.bfloat16),
            pltpu.VMEM(joined, jnp.float32),
            pltpu.SemaphoreType.DMA((len(xs) + len(gs) + moves,)),
        ],
        cost_estimate=LITTLE,
        compiler_params=pltpu.CompilerParams(vmem_limit_bytes=vmem * MIB),
    )(
        *xs,
        *gs,
        *([] if before is None else [before]),
        *([] if weights is None else [weights]),
    )


def merge_pairs(value, scratch):
    size = value.shape[0] // 2
    sums = []
    for at in range(value.shape[1] // LANES):
        scratch[at] = value[:, at * LANES : (at + 1) * LANES]
        even = scratch[at, pl.ds(0, size, stride=2), :]
        sums.append(even + scratch[at, pl.ds(1, size, stride=2), :])
    return jnp.concatenate(sums, axis=1)


def make_pairs(value, scratch):
    size = value.shape[0]
    rows = []
    for at in range(value.shape[1] // LANES):
        part = value[:, at * LANES : (at + 1) * LANES]
        scratch[at, pl.ds(0, size, stride=2), :] = part
        scratch[at, pl.ds(1, size, stride=2), :] = part
        rows.append(scratch[at])
    return jnp.concatenate(rows, axis=1)


def pair_scratch(rows, width):
    return pltpu.VMEM((width // LANES, rows, LANES), jnp.float32)


def each_exon(owners, exons, seen, nblocks, most, act):
    mine = lax.axis_index("seq")
    span, count = exons.shape
    for i in range(seen.shape[0]):
        seen[i] = 0

    def body(t, carry):
        owner = owners[t]
        slot = (owner ^ mine) * most + seen[owner]
        seen[owner] += 1
        for e in range(span):
            where = exons[e, t]

            @pl.when(where // nblocks == mine)
            def _():
                act(t, slot, where % nblocks)

        return carry

    lax.fori_loop(0, count, body, 0)


def front_kernel(owners, exons, pre_act, *refs, nblocks, most, size):
    outs, (slots, pair, seen) = refs[:-3], refs[-3:]
    slots[...] = jnp.zeros_like(slots)

    def act(t, slot, block):
        at = pl.ds(pl.multiple_of(block * (2 * size), 2 * size), 2 * size)
        value = pre_act[at, :].astype(jnp.float32)
        value = value * (0.5 * (1.0 + lax.erf(value * HALF_ROOT)))
        mean = 0.5 * merge_pairs(value, pair)
        slots[pl.ds(pl.multiple_of(slot * size, size), size), :] = mean

    each_exon(owners, exons, seen, nblocks, most, act)
    group = most * size
    for d, out in enumerate(outs):
        out[...] = slots[pl.ds(d * group, group), :].astype(out.dtype)


def front(owners, exons, pre_act, most, size, groups):
    rows, width = pre_act.shape
    return pl.pallas_call(
        functools.partial(
            front_kernel, nblocks=rows // 2 // size, most=most, size=size
        ),
        out_shape=[jax.ShapeDtypeStruct((most * size, width), jnp.bfloat16)] * groups,
        in_specs=[SMEM] * 2 + [VMEM],
        out_specs=[VMEM] * groups,
        scratch_shapes=[
            pltpu.VMEM((groups * most * size, width), jnp.float32),
            pair_scratch(2 * size, width),
            pltpu.SMEM((groups,), jnp.int32),
        ],
        cost_estimate=LITTLE,
        compiler_params=pltpu.CompilerParams(vmem_limit_bytes=16 * MIB),
    )(owners, exons, pre_act)


def plain_kernel(pre_act, out_grad, slope, plain, both):
    value = pre_act[...].astype(jnp.float32)
    normal = 0.5 * (1.0 + lax.erf(value * HALF_ROOT))
    slope[...] = normal + value * (jnp.exp(-0.5 * value * value) * DENSITY)
    pooled = make_pairs(out_grad[...].astype(jnp.float32) * 0.5, both)
    plain[...] = (pooled * slope[...]).astype(plain.dtype)


def plain_gradient(pre_act, out_grad):
    rows, width = pre_act.shape
    return pl.pallas_call(
        plain_kernel,
        out_shape=[
            jax.ShapeDtypeStruct((rows, width), jnp.float32),
            jax.ShapeDtypeStruct((rows, width), jnp.bfloat16),
        ],
        in_specs=[VMEM] * 2,
        out_specs=[VMEM] * 2,
        scratch_shapes=[pair_scratch(rows, width)],
        cost_estimate=LITTLE,
        compiler_params=pltpu.CompilerParams(vmem_limit_bytes=16 * MIB),
    )(pre_act, out_grad)


def gain_kernel(owners, exons, out_grad, slope, *refs, nblocks, most, size):
    splices, (grad, gain, held, both, seen) = refs[:-5], refs[-5:]
    gain[...] = out_grad[...].astype(jnp.float32)
    base = 0
    for splice in splices:
        held[pl.ds(base, splice.shape[0]), :] = splice[...].astype(jnp.float32)
        base += splice.shape[0]

    def add(t, slot, block):
        at = pl.ds(pl.multiple_of(block * size, size), size)
        gain[at, :] += held[pl.ds(pl.multiple_of(slot * size, size), size), :]

    def final(block):
        pooled = 0.5 * gain[pl.ds(pl.multiple_of(block * size, size), size), :]
        at = pl.ds(pl.multiple_of(block * (2 * size), 2 * size), 2 * size)
        return make_pairs(pooled, both) * slope[at, :]

    def renew(t, slot, block):
        at = pl.ds(pl.multiple_of(t * (2 * size), 2 * size), 2 * size)
        grad[at, :] = final(block).astype(grad.dtype)

    each_exon(owners, exons, seen, nblocks, most, add)
    each_exon(owners, exons, seen, nblocks, most, renew)
    count = exons.shape[1]
    row = lax.broadcasted_iota(jnp.int32, (2 * size, grad.shape[1]), 0)
    for at, block, first in ((count, 0, 0), (count + 1, nblocks - 1, 2 * size - 2)):
        rows = final(block)
        rows = jnp.where(row % 2 == 0, rows[first : first + 1], rows[first + 1 : first + 2])
        grad[pl.ds(at * 2 * size, 2 * size), :] = rows.astype(grad.dtype)


def gained_rows(owners, exons, out_grad, slope, splices, most, size, groups):
    rows, width = slope.shape
    return pl.pallas_call(
        functools.partial(gain_kernel, nblocks=rows // 2 // size, most=most, size=size),
        out_shape=jax.ShapeDtypeStruct(((exons.shape[1] + 2) * 2 * size, width), jnp.bfloat16),
        in_specs=[SMEM] * 2 + [VMEM] * (2 + len(splices)),
        out_specs=VMEM,
        scratch_shapes=[
            pltpu.VMEM((rows // 2, width), jnp.float32),
            pltpu.VMEM((groups * most * size, width), jnp.float32),
            pair_scratch(2 * size, width),
            pltpu.SMEM((groups,), jnp.int32),
        ],
        cost_estimate=LONG,
        compiler_params=pltpu.CompilerParams(vmem_limit_bytes=16 * MIB),
    )(owners, exons, out_grad, slope, *splices)


def mend_kernel(exons, *refs, pieces, nblocks, size):
    gained, parts, sent, own = (
        refs[pieces : 2 * pieces],
        refs[2 * pieces : 3 * pieces],
        refs[3 * pieces : -1],
        refs[-1],
    )
    mine = lax.axis_index("seq")
    place = lax.axis_index("ch")
    span, count = exons.shape
    rows = parts[0].shape[0]
    quarter = rows // pieces

    def body(t, carry):
        for e in range(span):
            where = exons[e, t]

            @pl.when(where // nblocks == mine)
            def _():
                to = pl.ds(pl.multiple_of(where % nblocks * (2 * size), 2 * size), 2 * size)
                at = pl.ds(pl.multiple_of(t * (2 * size), 2 * size), 2 * size)
                for part, new in zip(parts, gained):
                    part[to, :] = new[at, :]

        return carry

    lax.fori_loop(0, count, body, 0)
    row = lax.broadcasted_iota(jnp.int32, (PAD, own.shape[1]), 0)
    for d, out in enumerate(sent, 1):
        for tag, part in enumerate(parts):

            @pl.when(mine ^ d ^ place == tag)
            def _():
                at = pl.ds(pl.multiple_of(place * quarter, quarter), quarter)
                out[pl.ds(0, quarter), :] = part[at, :]

        if out.shape[0] > quarter:
            after_me = (mine ^ d) > mine
            edge = jnp.zeros(row.shape, jnp.float32)
            for tag, new in enumerate(gained):
                head = new[pl.ds(count * 2 * size, PAD), :].astype(jnp.float32)
                tail = new[pl.ds((count + 1) * 2 * size, PAD), :].astype(jnp.float32)
                edge = jnp.where(row // 2 == tag, jnp.where(after_me, tail, head), edge)
            out[pl.ds(quarter, PAD), :] = edge.astype(out.dtype)
    for tag, part in enumerate(parts):

        @pl.when(mine ^ place == tag)
        def _():
            own[...] = part[...]


def mend(exons, parts, gained, size):
    rows, width = parts[0].shape
    pieces = len(parts)
    whole = jax.ShapeDtypeStruct((rows, width), jnp.bfloat16)
    quarter = rows // pieces
    sent = [
        jax.ShapeDtypeStruct((quarter + (PAD if d in (1, 3) else 0), width), jnp.bfloat16)
        for d in range(1, pieces)
    ]
    outs = pl.pallas_call(
        functools.partial(mend_kernel, pieces=pieces, nblocks=rows // 2 // size, size=size),
        out_shape=[whole] * pieces + sent + [whole],
        in_specs=[SMEM] + [VMEM] * (2 * pieces),
        out_specs=[VMEM] * (pieces + len(sent) + 1),
        input_output_aliases={1 + at: at for at in range(pieces)},
        cost_estimate=LITTLE,
        compiler_params=pltpu.CompilerParams(vmem_limit_bytes=24 * MIB),
    )(exons, *parts, *gained)
    return outs[:pieces], outs[pieces:-1], outs[-1]


def gathered_gradient(pre_act, out_grad, coverage_obs, owners, exon_blocks):
    rows, width = pre_act.shape
    nseq = lax.axis_size("seq")
    mine = lax.axis_index("seq")
    most, block = coverage_obs.shape[1:3]
    nblocks = rows // 2 // block
    counts = owners.shape[0]
    value = pre_act.astype(jnp.float32)
    normal = 0.5 * (1.0 + jax.scipy.special.erf(value * HALF_ROOT))
    slope = normal + value * jnp.exp(-0.5 * value * value) * DENSITY
    act = value * normal
    pooled = (0.5 * jnp.sum(act.reshape(rows // 2, 2, width), axis=1)).astype(jnp.bfloat16)
    order = jnp.arange(counts, dtype=jnp.int32)
    same = owners[:, None] == owners[None, :]
    rank = jnp.sum((same & (order[:, None] < order[None, :])).astype(jnp.int32), axis=0)
    dest = jnp.arange(nseq, dtype=jnp.int32)
    slots = jnp.arange(most, dtype=jnp.int32)
    route = (owners[None, None, :] == dest[:, None, None]) & (
        rank[None, None, :] == slots[None, :, None]
    )
    route = route.astype(jnp.float32).reshape(nseq * most, counts)
    on_mine = exon_blocks // nblocks == mine
    holds = jnp.any(on_mine, axis=1)
    local_block = jnp.sum(jnp.where(on_mine, exon_blocks % nblocks, 0), axis=1)
    select = (
        holds[:, None] & (local_block[:, None] == jnp.arange(nblocks, dtype=jnp.int32)[None, :])
    ).astype(jnp.float32)
    picker = jnp.dot(route, select, precision=lax.Precision.HIGHEST).astype(jnp.bfloat16)
    pieces = pooled.reshape(nblocks, block * width)
    outgoing = jnp.dot(picker, pieces, preferred_element_type=jnp.float32).astype(jnp.bfloat16)
    outgoing = outgoing.reshape(nseq, most, block, width)
    arrived = lax.all_to_all(outgoing, "seq", split_axis=0, concat_axis=0, tiled=True)
    coverage = jnp.sum(arrived.astype(jnp.float32), axis=0)
    splice = jnp.tanh(coverage - coverage_obs[0]).astype(jnp.bfloat16)
    returned = lax.all_gather(splice, "seq", axis=0).reshape(nseq * most, block * width)
    gained = jnp.dot(picker.T, returned, preferred_element_type=jnp.float32)
    pooled_grad = out_grad.astype(jnp.float32) + gained.reshape(rows // 2, width)
    return (jnp.repeat(pooled_grad, 2, axis=0) * 0.5 * slope).astype(jnp.bfloat16)


def local(x_saved, pre_act, out_grad, conv_w, coverage_obs, owners, exon_blocks):
    rows, width = x_saved.shape
    taps = conv_w.shape[1]
    nseq = lax.axis_size("seq")
    nch = lax.axis_size("ch")
    chunk = conv_w.shape[0] // nseq
    most = coverage_obs.shape[1]
    size = coverage_obs.shape[2]
    direct = nseq == nch == 4 and chunk == width and width % 128 == 0
    exons = exon_blocks.T
    weights = conv_w.transpose(1, 0, 2)
    target = coverage_obs[0].reshape(most * size, width)

    if not direct:
        pre_grad = gathered_gradient(pre_act, out_grad, coverage_obs, owners, exon_blocks)
        x_all = lax.all_gather(x_saved, "seq", axis=0, tiled=True)
        whole = lax.all_gather(pre_grad, "ch", axis=1, tiled=True)
        blocks = whole.reshape(rows, nseq, chunk).transpose(1, 0, 2)
        g_all = lax.all_to_all(blocks, "seq", 0, 0, tiled=True).reshape(nseq * rows, chunk)
        low = shift(whole[rows - PAD :], "seq", 1)
        high = shift(whole[:PAD], "seq", -1)
        in_grad = input_gradient(whole, low, high, weights)
        total = nseq * rows
        (w_grad,) = weight_gradient(
            [x_all], [g_all], lambda: ([PAD], [0], [0], [], []), total, taps, total
        )
        return (in_grad, w_grad.transpose(1, 0, 2))

    outgoing = front(owners, exons, pre_act, most, size, nseq)
    slope, plain = plain_gradient(*after([pre_act, out_grad], outgoing))
    arrived = [outgoing[0]] + [swap(outgoing[d], "seq", d) for d in range(1, nseq)]
    (source,) = after([x_saved], outgoing)
    up1, down1 = shift(source, "seq", 1), shift(source, "seq", -1)
    far, near = swap(plain, "ch", 2), swap(plain, "ch", 1)
    *arrived, plain, slope, near = after([*arrived, plain, slope, near])
    coverage = functools.reduce(jnp.add, [a.astype(jnp.float32) for a in arrived])
    splice = jnp.tanh(coverage - target).astype(jnp.bfloat16)
    splices = [splice] + [swap(splice, "seq", d) for d in range(1, nseq)]
    *splices, far = after([*splices, far])
    gained = gained_rows(owners, exons, out_grad, slope, splices, most, size, nseq)
    gained, up1, down1 = after([gained, up1, down1])

    far_gained, near_gained = swap(gained, "ch", 2), swap(gained, "ch", 1)
    up2, down2 = shift(up1, "seq", 1, 1), shift(down1, "seq", -1, 1)
    beyond = swap(far, "ch", 1)
    gained = [gained, near_gained, far_gained, swap(far_gained, "ch", 1)]
    *gained, beyond, up2, down2 = after([*gained, beyond, up2, down2])

    quarter = rows // nch
    parts, sent, own = mend(exons, [plain, near, far, beyond], gained, size)
    *sent, up2, down2 = after([*sent, up2, down2])
    got = [swap(block, "seq", d) for d, block in zip(range(1, nseq), sent)]
    up3, down3 = shift(up2, "seq", 1, 2), shift(down2, "seq", -1, 2)

    def origins():
        return [(lax.axis_index("ch") ^ t) * width for t in range(nch)]

    partial, laid = weight_gradient(
        [up1[rows - PAD :], x_saved, down1[:PAD]],
        [own],
        lambda: ([0, PAD, PAD + rows], [0], [0], [], []),
        rows,
        taps,
        rows,
        last=False,
        vmem=24,
        weights=weights,
        origins=origins,
    )
    center = pieces_gradient(parts, laid, taps)
    *got, partial, center = after([*got, partial, center])

    crossing = jnp.concatenate([block[:quarter] for block in got])
    across = swap(crossing, "ch", 2)
    beside = swap(crossing, "ch", 1)
    in_grad = pieces_gradient(parts, laid, taps, [got[0], got[2], center])
    across, in_grad, up3, down3 = after([across, in_grad, up3, down3])
    beyond = swap(across, "ch", 1)

    def layout():
        mine = lax.axis_index("seq")
        place = lax.axis_index("ch")
        x_rows = [PAD + mine * rows]
        for hop in range(1, nseq):
            low_at, high_at = mine - hop, mine + hop
            x_rows += [
                jnp.where(low_at >= 0, PAD + low_at * rows, -1),
                jnp.where(high_at < nseq, PAD + high_at * rows, -1),
            ]
        g_rows = [
            (mine ^ d) * rows + (place ^ tag) * quarter
            for d in range(1, nseq)
            for tag in range(nch)
        ]
        return x_rows, g_rows, [(mine ^ d) * rows for d in range(1, nseq)], [], []

    g_pieces, stages = [], [0] * 5 + [1] * 2
    for d in range(nseq - 1):
        for piece in (crossing, beside, across, beyond):
            g_pieces.append(piece[d * quarter : (d + 1) * quarter])
            stages.append(d)
    (w_grad,) = weight_gradient(
        [x_saved, up1, down1, up2, down2, up3, down3],
        g_pieces,
        layout,
        rows,
        taps,
        nseq * rows,
        before=partial,
        vmem=32,
        stages=stages,
    )
    return (in_grad, w_grad.transpose(1, 0, 2))


def solution(mesh):
    in_specs = (
        P(("grp", "seq"), "ch"),
        P(("grp", "seq"), "ch"),
        P(("grp", "seq"), "ch"),
        P(None, None, "ch"),
        P(("grp", "seq"), None, None, "ch"),
        P("grp"),
        P("grp", None),
    )
    out_specs = (P(("grp", "seq"), "ch"), P(("grp", "seq"), None, "ch"))
    return jax.shard_map(local, mesh=mesh, in_specs=in_specs, out_specs=out_specs, check_vma=False)
```

```python
import functools

import jax
import jax.numpy as jnp
from jax import lax
from jax.experimental import pallas as pl
from jax.experimental.pallas import tpu as pltpu
from jax.sharding import PartitionSpec as P

PAD = 16
MIB = 1024 * 1024
VMEM = pl.BlockSpec(memory_space=pltpu.VMEM)
SMEM = pl.BlockSpec(memory_space=pltpu.SMEM)
SOME = pl.BlockSpec(memory_space=pl.ANY)
HALF_ROOT = 0.7071067811865476
DENSITY = 0.3989422804014327
LANES = 128
LONG = pl.CostEstimate(flops=4 * 10**9, bytes_accessed=1000, transcendentals=0)
LITTLE = pl.CostEstimate(flops=1000, bytes_accessed=1000, transcendentals=0)


def swap(block, axis, flip):
    count = lax.axis_size(axis)
    return lax.ppermute(block, axis, [(i, i ^ flip) for i in range(count)])


def shift(block, axis, step, first=0):
    count = lax.axis_size(axis)
    if step > 0:
        pairs = [(i, i + 1) for i in range(first, count - 1)]
    else:
        pairs = [(i + 1, i) for i in range(count - 1 - first)]
    return lax.ppermute(block, axis, pairs)


def after(values, others=()):
    return lax.optimization_barrier(tuple(values) + tuple(others))[: len(values)]


def input_kernel(part, low, high, weights, out, block):
    taps = weights.shape[0]
    rows = part.shape[0]
    half = taps // 2
    block[pl.ds(0, PAD), :] = low[...]
    block[pl.ds(PAD, rows), :] = part[...]
    block[pl.ds(PAD + rows, PAD), :] = high[...]
    tile = min(256, rows)

    def body(step, carry):
        start = pl.multiple_of(step * tile, tile)
        rows_in = block[pl.ds(start, tile + 2 * PAD), :]
        total = None
        for tap in range(taps):
            term = jnp.dot(rows_in, weights[tap], preferred_element_type=jnp.float32)
            first = PAD + half - tap
            term = term[first : first + tile]
            total = term if total is None else total + term
        out[pl.ds(start, tile), :] = total.astype(out.dtype)
        return carry

    lax.fori_loop(0, rows // tile, body, 0)


def input_gradient(part, low, high, weights):
    taps, chans, width = weights.shape
    rows = part.shape[0]
    return pl.pallas_call(
        input_kernel,
        out_shape=jax.ShapeDtypeStruct((rows, width), jnp.bfloat16),
        in_specs=[VMEM] * 4,
        out_specs=VMEM,
        scratch_shapes=[pltpu.VMEM((rows + 2 * PAD, chans), jnp.bfloat16)],
        compiler_params=pltpu.CompilerParams(vmem_limit_bytes=32 * MIB),
    )(part, low, high, weights)


def pieces_kernel(*refs, taps, pieces, middle):
    parts, rest = refs[:pieces], refs[pieces:]
    if middle:
        weights, out, block = rest
    else:
        near_edge, far_edge, center, weights, out, block = rest
    rows = parts[0].shape[0]
    width = weights.shape[1] // taps
    half = taps // 2
    quarter = rows // 4
    kept = [(0, rows)] if middle else [(0, quarter + PAD), (rows - quarter - PAD, quarter + PAD)]
    base = 0
    for part in parts:
        span = pl.ds(base, part.shape[1])
        for begin, count in kept:
            block[pl.ds(PAD + begin, count), span] = part[pl.ds(begin, count), :]
        base += part.shape[1]
    if not middle:
        mine = lax.axis_index("seq")
        one = near_edge[pl.ds(quarter, PAD), :].astype(jnp.float32)
        other = far_edge[pl.ds(quarter, PAD), :].astype(jnp.float32)
        low = jnp.where(mine % 2 == 1, one, jnp.where(mine == 2, other, 0.0))
        high = jnp.where(mine % 2 == 0, one, jnp.where(mine == 1, other, 0.0))
        for at in range(pieces):
            span = pl.ds(at * part.shape[1], part.shape[1])
            lower = pltpu.roll(low, PAD - half - half * at, 0)
            upper = pltpu.roll(high, (PAD - half * at) % PAD, 0)
            block[pl.ds(0, PAD), span] = lower.astype(block.dtype)
            block[pl.ds(PAD + rows, PAD), span] = upper.astype(block.dtype)

    def tile(start, count):
        terms = jnp.dot(
            block[pl.ds(start, count + 2 * PAD), :],
            weights[...],
            preferred_element_type=jnp.float32,
        )
        total = None
        for tap in range(taps):
            first = PAD + half - tap
            term = terms[first : first + count, tap * width : (tap + 1) * width]
            total = term if total is None else total + term
        return total.astype(out.dtype)

    if middle:
        out[...] = tile(quarter, 2 * quarter)
    else:
        out[pl.ds(0, quarter), :] = tile(0, quarter)
        out[pl.ds(quarter, 2 * quarter), :] = center[...]
        out[pl.ds(3 * quarter, quarter), :] = tile(3 * quarter, quarter)


def pieces_gradient(parts, weights, taps, rest=()):
    chans = weights.shape[0]
    width = weights.shape[1] // taps
    rows = parts[0].shape[0]
    middle = not rest
    return pl.pallas_call(
        functools.partial(pieces_kernel, taps=taps, pieces=len(parts), middle=middle),
        out_shape=jax.ShapeDtypeStruct((rows // 2 if middle else rows, width), jnp.bfloat16),
        in_specs=[VMEM] * (len(parts) + len(rest) + 1),
        out_specs=VMEM,
        scratch_shapes=[pltpu.VMEM((rows + 2 * PAD, chans), jnp.bfloat16)],
        cost_estimate=LITTLE,
        compiler_params=pltpu.CompilerParams(vmem_limit_bytes=24 * MIB),
    )(*parts, *rest, weights)


def weight_kernel(*refs, taps, tile, rows, size, nx, ng, layout, first, last, origins, span, stages):
    xs, gs, rest = refs[:nx], refs[nx : nx + ng], list(refs[nx + ng :])
    before = None if first else rest.pop(0)
    weights = rest.pop(0) if origins else None
    out = rest.pop(0)
    laid = rest.pop(0) if origins else None
    xbuf, gbuf, acc, sems = rest
    width = xbuf.shape[1]
    half = taps // 2
    x_rows, g_rows, starts, blanks, seams = layout()
    zeros = jnp.zeros((PAD, width), xbuf.dtype)
    xbuf[pl.ds(0, PAD), :] = zeros
    xbuf[pl.ds(PAD + rows, PAD), :] = zeros
    for wanted, row in blanks:

        @pl.when(wanted)
        def _():
            xbuf[pl.ds(row, PAD), :] = zeros

    pieces = [(src, xbuf, row, src.shape[0]) for src, row in zip(xs, x_rows)]
    pieces += [(src, gbuf, row, span or src.shape[0]) for src, row in zip(gs, g_rows)]

    def copy(at):
        src, dst, row, count = pieces[at]
        row = row if isinstance(row, int) else pl.multiple_of(row, 16)
        return pltpu.make_async_copy(
            src.at[pl.ds(0, count), :], dst.at[pl.ds(row, count), :], sems.at[at]
        )

    def each(act, stage=None):
        for at in range(nx + ng):
            if stages and stage is not None and stages[at] != stage:
                continue
            row = pieces[at][2]
            if isinstance(row, int):
                act(at)
            else:
                pl.when(row >= 0)(functools.partial(act, at))

    each(lambda at: copy(at).start())
    moves = []
    if origins:
        where = origins()
        depth = weights.shape[1] // len(where)
        for e, origin in enumerate(where):
            for tap in range(taps):
                moves.append(
                    pltpu.make_async_copy(
                        weights.at[tap, pl.ds(pl.multiple_of(origin, 16), depth), :],
                        laid.at[pl.ds(e * depth, depth), pl.ds(tap * width, width)],
                        sems.at[nx + ng + len(moves)],
                    )
                )
        for move in moves:
            move.start()
    acc[...] = jnp.zeros_like(acc) if first else before[...]
    if not stages:
        each(lambda at: copy(at).wait())

    def add(start, count, side=None):
        grad = gbuf[pl.ds(start, count), :].T
        block = xbuf[pl.ds(start, count + 2 * PAD), :].astype(jnp.float32)
        if side is not None:
            row = lax.broadcasted_iota(jnp.int32, block.shape, 0)
            block = jnp.where(row >= count + PAD if side > 0 else row < PAD, block, 0.0)
        moved = []
        for tap in range(taps):
            at = PAD - half + tap
            moved.append(block[at : at + count].astype(jnp.bfloat16))
        if width % LANES:
            for tap in range(taps):
                acc[tap] += jnp.dot(grad, moved[tap], preferred_element_type=jnp.float32)
        else:
            moved = jnp.concatenate(moved, axis=1)
            acc[...] += jnp.dot(grad, moved, preferred_element_type=jnp.float32)

    for stage, begin in enumerate(starts):
        if stages:
            each(lambda at: copy(at).wait(), stage)

        def body(step, carry):
            add(pl.multiple_of(begin + step * tile, 16), tile)
            return carry

        lax.fori_loop(0, size // tile, body, 0)
    for wanted, row, side in seams:
        pl.when(wanted)(functools.partial(add, row, PAD, side))
    if last and width % LANES == 0:
        for tap in range(taps):
            out[tap] = acc[:, tap * width : (tap + 1) * width].astype(out.dtype)
    else:
        out[...] = acc[...].astype(out.dtype)
    for move in moves:
        move.wait()


def weight_gradient(
    xs, gs, layout, size, taps, rows, before=None, last=True, vmem=40, weights=None, origins=None, span=None,
    stages=None
):
    width, chunk = xs[0].shape[1], gs[0].shape[1]
    split = (taps, chunk, width)
    joined = split if width % LANES else (chunk, taps * width)
    out_shape = [
        jax.ShapeDtypeStruct(split, jnp.bfloat16)
        if last
        else jax.ShapeDtypeStruct(joined, jnp.float32)
    ]
    moves = 0
    if origins:
        moves = taps * 4
        out_shape.append(
            jax.ShapeDtypeStruct((weights.shape[1], taps * width), weights.dtype)
        )
    return pl.pallas_call(
        functools.partial(
            weight_kernel,
            taps=taps,
            tile=min(1024, size) if width % LANES == 0 else min(512, size),
            rows=rows,
            size=size,
            nx=len(xs),
            ng=len(gs),
            layout=layout,
            first=before is None,
            last=last,
            origins=origins,
            span=span,
            stages=stages,
        ),
        out_shape=out_shape,
        in_specs=[SOME] * (len(xs) + len(gs))
        + [VMEM] * (before is not None)
        + [SOME] * (weights is not None),
        out_specs=[VMEM] * len(out_shape),
        scratch_shapes=[
            pltpu.VMEM((rows + 2 * PAD, width), jnp.bfloat16),
            pltpu.VMEM((rows, chunk), jnp.bfloat16),
            pltpu.VMEM(joined, jnp.float32),
            pltpu.SemaphoreType.DMA((len(xs) + len(gs) + moves,)),
        ],
        cost_estimate=LITTLE,
        compiler_params=pltpu.CompilerParams(vmem_limit_bytes=vmem * MIB),
    )(
        *xs,
        *gs,
        *([] if before is None else [before]),
        *([] if weights is None else [weights]),
    )


def merge_pairs(value, scratch):
    size = value.shape[0] // 2
    sums = []
    for at in range(value.shape[1] // LANES):
        scratch[at] = value[:, at * LANES : (at + 1) * LANES]
        even = scratch[at, pl.ds(0, size, stride=2), :]
        sums.append(even + scratch[at, pl.ds(1, size, stride=2), :])
    return jnp.concatenate(sums, axis=1)


def make_pairs(value, scratch):
    size = value.shape[0]
    rows = []
    for at in range(value.shape[1] // LANES):
        part = value[:, at * LANES : (at + 1) * LANES]
        scratch[at, pl.ds(0, size, stride=2), :] = part
        scratch[at, pl.ds(1, size, stride=2), :] = part
        rows.append(scratch[at])
    return jnp.concatenate(rows, axis=1)


def pair_scratch(rows, width):
    return pltpu.VMEM((width // LANES, rows, LANES), jnp.float32)


def each_exon(owners, exons, seen, nblocks, most, act):
    mine = lax.axis_index("seq")
    span, count = exons.shape
    for i in range(seen.shape[0]):
        seen[i] = 0

    def body(t, carry):
        owner = owners[t]
        slot = (owner ^ mine) * most + seen[owner]
        seen[owner] += 1
        for e in range(span):
            where = exons[e, t]

            @pl.when(where // nblocks == mine)
            def _():
                act(t, slot, where % nblocks)

        return carry

    lax.fori_loop(0, count, body, 0)


def front_kernel(owners, exons, pre_act, *refs, nblocks, most, size):
    outs, (slots, pair, seen) = refs[:-3], refs[-3:]
    slots[...] = jnp.zeros_like(slots)

    def act(t, slot, block):
        at = pl.ds(pl.multiple_of(block * (2 * size), 2 * size), 2 * size)
        value = pre_act[at, :].astype(jnp.float32)
        value = value * (0.5 * (1.0 + lax.erf(value * HALF_ROOT)))
        mean = 0.5 * merge_pairs(value, pair)
        slots[pl.ds(pl.multiple_of(slot * size, size), size), :] = mean

    each_exon(owners, exons, seen, nblocks, most, act)
    group = most * size
    for d, out in enumerate(outs):
        out[...] = slots[pl.ds(d * group, group), :].astype(out.dtype)


def front(owners, exons, pre_act, most, size, groups):
    rows, width = pre_act.shape
    return pl.pallas_call(
        functools.partial(
            front_kernel, nblocks=rows // 2 // size, most=most, size=size
        ),
        out_shape=[jax.ShapeDtypeStruct((most * size, width), jnp.bfloat16)] * groups,
        in_specs=[SMEM] * 2 + [VMEM],
        out_specs=[VMEM] * groups,
        scratch_shapes=[
            pltpu.VMEM((groups * most * size, width), jnp.float32),
            pair_scratch(2 * size, width),
            pltpu.SMEM((groups,), jnp.int32),
        ],
        cost_estimate=LITTLE,
        compiler_params=pltpu.CompilerParams(vmem_limit_bytes=16 * MIB),
    )(owners, exons, pre_act)


def plain_kernel(pre_act, out_grad, slope, plain, both):
    value = pre_act[...].astype(jnp.float32)
    normal = 0.5 * (1.0 + lax.erf(value * HALF_ROOT))
    slope[...] = normal + value * (jnp.exp(-0.5 * value * value) * DENSITY)
    pooled = make_pairs(out_grad[...].astype(jnp.float32) * 0.5, both)
    plain[...] = (pooled * slope[...]).astype(plain.dtype)


def plain_gradient(pre_act, out_grad):
    rows, width = pre_act.shape
    return pl.pallas_call(
        plain_kernel,
        out_shape=[
            jax.ShapeDtypeStruct((rows, width), jnp.float32),
            jax.ShapeDtypeStruct((rows, width), jnp.bfloat16),
        ],
        in_specs=[VMEM] * 2,
        out_specs=[VMEM] * 2,
        scratch_shapes=[pair_scratch(rows, width)],
        cost_estimate=LITTLE,
        compiler_params=pltpu.CompilerParams(vmem_limit_bytes=16 * MIB),
    )(pre_act, out_grad)


def gain_kernel(owners, exons, out_grad, slope, *refs, nblocks, most, size):
    splices, (grad, gain, held, both, seen) = refs[:-5], refs[-5:]
    gain[...] = out_grad[...].astype(jnp.float32)
    base = 0
    for splice in splices:
        held[pl.ds(base, splice.shape[0]), :] = splice[...].astype(jnp.float32)
        base += splice.shape[0]

    def add(t, slot, block):
        at = pl.ds(pl.multiple_of(block * size, size), size)
        gain[at, :] += held[pl.ds(pl.multiple_of(slot * size, size), size), :]

    def final(block):
        pooled = 0.5 * gain[pl.ds(pl.multiple_of(block * size, size), size), :]
        at = pl.ds(pl.multiple_of(block * (2 * size), 2 * size), 2 * size)
        return make_pairs(pooled, both) * slope[at, :]

    def renew(t, slot, block):
        at = pl.ds(pl.multiple_of(t * (2 * size), 2 * size), 2 * size)
        grad[at, :] = final(block).astype(grad.dtype)

    each_exon(owners, exons, seen, nblocks, most, add)
    each_exon(owners, exons, seen, nblocks, most, renew)
    count = exons.shape[1]
    row = lax.broadcasted_iota(jnp.int32, (2 * size, grad.shape[1]), 0)
    for at, block, first in ((count, 0, 0), (count + 1, nblocks - 1, 2 * size - 2)):
        rows = final(block)
        rows = jnp.where(row % 2 == 0, rows[first : first + 1], rows[first + 1 : first + 2])
        grad[pl.ds(at * 2 * size, 2 * size), :] = rows.astype(grad.dtype)


def gained_rows(owners, exons, out_grad, slope, splices, most, size, groups):
    rows, width = slope.shape
    return pl.pallas_call(
        functools.partial(gain_kernel, nblocks=rows // 2 // size, most=most, size=size),
        out_shape=jax.ShapeDtypeStruct(((exons.shape[1] + 2) * 2 * size, width), jnp.bfloat16),
        in_specs=[SMEM] * 2 + [VMEM] * (2 + len(splices)),
        out_specs=VMEM,
        scratch_shapes=[
            pltpu.VMEM((rows // 2, width), jnp.float32),
            pltpu.VMEM((groups * most * size, width), jnp.float32),
            pair_scratch(2 * size, width),
            pltpu.SMEM((groups,), jnp.int32),
        ],
        cost_estimate=LONG,
        compiler_params=pltpu.CompilerParams(vmem_limit_bytes=16 * MIB),
    )(owners, exons, out_grad, slope, *splices)


def mend_kernel(exons, *refs, pieces, nblocks, size):
    gained, parts, sent, own = (
        refs[pieces : 2 * pieces],
        refs[2 * pieces : 3 * pieces],
        refs[3 * pieces : -1],
        refs[-1],
    )
    mine = lax.axis_index("seq")
    place = lax.axis_index("ch")
    span, count = exons.shape
    rows = parts[0].shape[0]
    quarter = rows // pieces

    def body(t, carry):
        for e in range(span):
            where = exons[e, t]

            @pl.when(where // nblocks == mine)
            def _():
                to = pl.ds(pl.multiple_of(where % nblocks * (2 * size), 2 * size), 2 * size)
                at = pl.ds(pl.multiple_of(t * (2 * size), 2 * size), 2 * size)
                for part, new in zip(parts, gained):
                    part[to, :] = new[at, :]

        return carry

    lax.fori_loop(0, count, body, 0)
    row = lax.broadcasted_iota(jnp.int32, (PAD, own.shape[1]), 0)
    for d, out in enumerate(sent, 1):
        for tag, part in enumerate(parts):

            @pl.when(mine ^ d ^ place == tag)
            def _():
                at = pl.ds(pl.multiple_of(place * quarter, quarter), quarter)
                out[pl.ds(0, quarter), :] = part[at, :]

        if out.shape[0] > quarter:
            after_me = (mine ^ d) > mine
            edge = jnp.zeros(row.shape, jnp.float32)
            for tag, new in enumerate(gained):
                head = new[pl.ds(count * 2 * size, PAD), :].astype(jnp.float32)
                tail = new[pl.ds((count + 1) * 2 * size, PAD), :].astype(jnp.float32)
                edge = jnp.where(row // 2 == tag, jnp.where(after_me, tail, head), edge)
            out[pl.ds(quarter, PAD), :] = edge.astype(out.dtype)
    for tag, part in enumerate(parts):

        @pl.when(mine ^ place == tag)
        def _():
            own[...] = part[...]


def mend(exons, parts, gained, size):
    rows, width = parts[0].shape
    pieces = len(parts)
    whole = jax.ShapeDtypeStruct((rows, width), jnp.bfloat16)
    quarter = rows // pieces
    sent = [
        jax.ShapeDtypeStruct((quarter + (PAD if d in (1, 3) else 0), width), jnp.bfloat16)
        for d in range(1, pieces)
    ]
    outs = pl.pallas_call(
        functools.partial(mend_kernel, pieces=pieces, nblocks=rows // 2 // size, size=size),
        out_shape=[whole] * pieces + sent + [whole],
        in_specs=[SMEM] + [VMEM] * (2 * pieces),
        out_specs=[VMEM] * (pieces + len(sent) + 1),
        input_output_aliases={1 + at: at for at in range(pieces)},
        cost_estimate=LITTLE,
        compiler_params=pltpu.CompilerParams(vmem_limit_bytes=24 * MIB),
    )(exons, *parts, *gained)
    return outs[:pieces], outs[pieces:-1], outs[-1]


def gathered_gradient(pre_act, out_grad, coverage_obs, owners, exon_blocks):
    rows, width = pre_act.shape
    nseq = lax.axis_size("seq")
    mine = lax.axis_index("seq")
    most, block = coverage_obs.shape[1:3]
    nblocks = rows // 2 // block
    counts = owners.shape[0]
    value = pre_act.astype(jnp.float32)
    normal = 0.5 * (1.0 + jax.scipy.special.erf(value * HALF_ROOT))
    slope = normal + value * jnp.exp(-0.5 * value * value) * DENSITY
    act = value * normal
    pooled = (0.5 * jnp.sum(act.reshape(rows // 2, 2, width), axis=1)).astype(jnp.bfloat16)
    order = jnp.arange(counts, dtype=jnp.int32)
    same = owners[:, None] == owners[None, :]
    rank = jnp.sum((same & (order[:, None] < order[None, :])).astype(jnp.int32), axis=0)
    dest = jnp.arange(nseq, dtype=jnp.int32)
    slots = jnp.arange(most, dtype=jnp.int32)
    route = (owners[None, None, :] == dest[:, None, None]) & (
        rank[None, None, :] == slots[None, :, None]
    )
    route = route.astype(jnp.float32).reshape(nseq * most, counts)
    on_mine = exon_blocks // nblocks == mine
    holds = jnp.any(on_mine, axis=1)
    local_block = jnp.sum(jnp.where(on_mine, exon_blocks % nblocks, 0), axis=1)
    select = (
        holds[:, None] & (local_block[:, None] == jnp.arange(nblocks, dtype=jnp.int32)[None, :])
    ).astype(jnp.float32)
    picker = jnp.dot(route, select, precision=lax.Precision.HIGHEST).astype(jnp.bfloat16)
    pieces = pooled.reshape(nblocks, block * width)
    outgoing = jnp.dot(picker, pieces, preferred_element_type=jnp.float32).astype(jnp.bfloat16)
    outgoing = outgoing.reshape(nseq, most, block, width)
    arrived = lax.all_to_all(outgoing, "seq", split_axis=0, concat_axis=0, tiled=True)
    coverage = jnp.sum(arrived.astype(jnp.float32), axis=0)
    splice = jnp.tanh(coverage - coverage_obs[0]).astype(jnp.bfloat16)
    returned = lax.all_gather(splice, "seq", axis=0).reshape(nseq * most, block * width)
    gained = jnp.dot(picker.T, returned, preferred_element_type=jnp.float32)
    pooled_grad = out_grad.astype(jnp.float32) + gained.reshape(rows // 2, width)
    return (jnp.repeat(pooled_grad, 2, axis=0) * 0.5 * slope).astype(jnp.bfloat16)


def local(x_saved, pre_act, out_grad, conv_w, coverage_obs, owners, exon_blocks):
    rows, width = x_saved.shape
    taps = conv_w.shape[1]
    nseq = lax.axis_size("seq")
    nch = lax.axis_size("ch")
    chunk = conv_w.shape[0] // nseq
    most = coverage_obs.shape[1]
    size = coverage_obs.shape[2]
    direct = nseq == nch == 4 and chunk == width and width % 128 == 0
    exons = exon_blocks.T
    weights = conv_w.transpose(1, 0, 2)
    target = coverage_obs[0].reshape(most * size, width)

    if not direct:
        pre_grad = gathered_gradient(pre_act, out_grad, coverage_obs, owners, exon_blocks)
        x_all = lax.all_gather(x_saved, "seq", axis=0, tiled=True)
        whole = lax.all_gather(pre_grad, "ch", axis=1, tiled=True)
        blocks = whole.reshape(rows, nseq, chunk).transpose(1, 0, 2)
        g_all = lax.all_to_all(blocks, "seq", 0, 0, tiled=True).reshape(nseq * rows, chunk)
        low = shift(whole[rows - PAD :], "seq", 1)
        high = shift(whole[:PAD], "seq", -1)
        in_grad = input_gradient(whole, low, high, weights)
        total = nseq * rows
        (w_grad,) = weight_gradient(
            [x_all], [g_all], lambda: ([PAD], [0], [0], [], []), total, taps, total
        )
        return (in_grad, w_grad.transpose(1, 0, 2))

    outgoing = front(owners, exons, pre_act, most, size, nseq)
    slope, plain = plain_gradient(pre_act, out_grad)
    arrived = [outgoing[0]] + [swap(outgoing[d], "seq", d) for d in range(1, nseq)]
    (source,) = after([x_saved], outgoing)
    up1, down1 = shift(source, "seq", 1), shift(source, "seq", -1)
    *arrived, plain, slope = after([*arrived, plain, slope])
    far, near = swap(plain, "ch", 2), swap(plain, "ch", 1)
    coverage = functools.reduce(jnp.add, [a.astype(jnp.float32) for a in arrived])
    splice = jnp.tanh(coverage - target).astype(jnp.bfloat16)
    (last_splice,) = after([splice], [up1, down1])
    splices = [splice, swap(splice, "seq", 1), swap(splice, "seq", 2), swap(last_splice, "seq", 3)]
    gained = gained_rows(owners, exons, out_grad, slope, splices, most, size, nseq)

    far_gained, near_gained = swap(gained, "ch", 2), swap(gained, "ch", 1)
    up2, down2 = shift(up1, "seq", 1, 1), shift(down1, "seq", -1, 1)
    beyond = swap(far, "ch", 1)
    gained = [gained, near_gained, far_gained, swap(far_gained, "ch", 1)]
    *gained, beyond, up2, down2 = after([*gained, beyond, up2, down2])

    quarter = rows // nch
    parts, sent, own = mend(exons, [plain, near, far, beyond], gained, size)
    *sent, up2, down2 = after([*sent, up2, down2])
    got = [swap(block, "seq", d) for d, block in zip(range(1, nseq), sent)]
    up3, down3 = shift(up2, "seq", 1, 2), shift(down2, "seq", -1, 2)

    def origins():
        return [(lax.axis_index("ch") ^ t) * width for t in range(nch)]

    partial, laid = weight_gradient(
        [up1[rows - PAD :], x_saved, down1[:PAD]],
        [own],
        lambda: ([0, PAD, PAD + rows], [0], [0], [], []),
        rows,
        taps,
        rows,
        last=False,
        vmem=24,
        weights=weights,
        origins=origins,
    )
    center = pieces_gradient(parts, laid, taps)
    *got, partial, center = after([*got, partial, center])

    crossing = jnp.concatenate([block[:quarter] for block in got])
    across = swap(crossing, "ch", 2)
    beside = swap(crossing, "ch", 1)
    in_grad = pieces_gradient(parts, laid, taps, [got[0], got[2], center])
    across, in_grad, up3, down3 = after([across, in_grad, up3, down3])
    beyond = swap(across, "ch", 1)

    def layout():
        mine = lax.axis_index("seq")
        place = lax.axis_index("ch")
        x_rows = [PAD + mine * rows]
        for hop in range(1, nseq):
            low_at, high_at = mine - hop, mine + hop
            x_rows += [
                jnp.where(low_at >= 0, PAD + low_at * rows, -1),
                jnp.where(high_at < nseq, PAD + high_at * rows, -1),
            ]
        g_rows = [
            (mine ^ d) * rows + (place ^ tag) * quarter
            for d in range(1, nseq)
            for tag in range(nch)
        ]
        return x_rows, g_rows, [(mine ^ d) * rows for d in range(1, nseq)], [], []

    g_pieces, stages = [], [0] * 5 + [1] * 2
    for d in range(nseq - 1):
        for piece in (crossing, beside, across, beyond):
            g_pieces.append(piece[d * quarter : (d + 1) * quarter])
            stages.append(d)
    (w_grad,) = weight_gradient(
        [x_saved, up1, down1, up2, down2, up3, down3],
        g_pieces,
        layout,
        rows,
        taps,
        nseq * rows,
        before=partial,
        vmem=32,
        stages=stages,
    )
    return (in_grad, w_grad.transpose(1, 0, 2))


def solution(mesh):
    in_specs = (
        P(("grp", "seq"), "ch"),
        P(("grp", "seq"), "ch"),
        P(("grp", "seq"), "ch"),
        P(None, None, "ch"),
        P(("grp", "seq"), None, None, "ch"),
        P("grp"),
        P("grp", None),
    )
    out_specs = (P(("grp", "seq"), "ch"), P(("grp", "seq"), None, "ch"))
    return jax.shard_map(local, mesh=mesh, in_specs=in_specs, out_specs=out_specs, check_vma=False)
```

```python
import functools

import jax
import jax.numpy as jnp
from jax import lax
from jax.experimental import pallas as pl
from jax.experimental.pallas import tpu as pltpu
from jax.sharding import PartitionSpec as P

PAD = 16
MIB = 1024 * 1024
VMEM = pl.BlockSpec(memory_space=pltpu.VMEM)
SMEM = pl.BlockSpec(memory_space=pltpu.SMEM)
SOME = pl.BlockSpec(memory_space=pl.ANY)
HALF_ROOT = 0.7071067811865476
DENSITY = 0.3989422804014327
LANES = 128
LONG = pl.CostEstimate(flops=4 * 10**9, bytes_accessed=1000, transcendentals=0)
LITTLE = pl.CostEstimate(flops=1000, bytes_accessed=1000, transcendentals=0)


def swap(block, axis, flip):
    count = lax.axis_size(axis)
    return lax.ppermute(block, axis, [(i, i ^ flip) for i in range(count)])


def shift(block, axis, step, first=0):
    count = lax.axis_size(axis)
    if step > 0:
        pairs = [(i, i + 1) for i in range(first, count - 1)]
    else:
        pairs = [(i + 1, i) for i in range(count - 1 - first)]
    return lax.ppermute(block, axis, pairs)


def after(values, others=()):
    return lax.optimization_barrier(tuple(values) + tuple(others))[: len(values)]


def input_kernel(part, low, high, weights, out, block):
    taps = weights.shape[0]
    rows = part.shape[0]
    half = taps // 2
    block[pl.ds(0, PAD), :] = low[...]
    block[pl.ds(PAD, rows), :] = part[...]
    block[pl.ds(PAD + rows, PAD), :] = high[...]
    tile = min(256, rows)

    def body(step, carry):
        start = pl.multiple_of(step * tile, tile)
        rows_in = block[pl.ds(start, tile + 2 * PAD), :]
        total = None
        for tap in range(taps):
            term = jnp.dot(rows_in, weights[tap], preferred_element_type=jnp.float32)
            first = PAD + half - tap
            term = term[first : first + tile]
            total = term if total is None else total + term
        out[pl.ds(start, tile), :] = total.astype(out.dtype)
        return carry

    lax.fori_loop(0, rows // tile, body, 0)


def input_gradient(part, low, high, weights):
    taps, chans, width = weights.shape
    rows = part.shape[0]
    return pl.pallas_call(
        input_kernel,
        out_shape=jax.ShapeDtypeStruct((rows, width), jnp.bfloat16),
        in_specs=[VMEM] * 4,
        out_specs=VMEM,
        scratch_shapes=[pltpu.VMEM((rows + 2 * PAD, chans), jnp.bfloat16)],
        compiler_params=pltpu.CompilerParams(vmem_limit_bytes=32 * MIB),
    )(part, low, high, weights)


def pieces_kernel(*refs, taps, pieces, middle):
    parts, rest = refs[:pieces], refs[pieces:]
    if middle:
        weights, out, block = rest
    else:
        near_edge, far_edge, center, weights, out, block = rest
    rows = parts[0].shape[0]
    width = weights.shape[1] // taps
    half = taps // 2
    quarter = rows // 4
    kept = [(0, rows)] if middle else [(0, quarter + PAD), (rows - quarter - PAD, quarter + PAD)]
    base = 0
    for part in parts:
        span = pl.ds(base, part.shape[1])
        for begin, count in kept:
            block[pl.ds(PAD + begin, count), span] = part[pl.ds(begin, count), :]
        base += part.shape[1]
    if not middle:
        mine = lax.axis_index("seq")
        one = near_edge[pl.ds(quarter, PAD), :].astype(jnp.float32)
        other = far_edge[pl.ds(quarter, PAD), :].astype(jnp.float32)
        low = jnp.where(mine % 2 == 1, one, jnp.where(mine == 2, other, 0.0))
        high = jnp.where(mine % 2 == 0, one, jnp.where(mine == 1, other, 0.0))
        for at in range(pieces):
            span = pl.ds(at * part.shape[1], part.shape[1])
            lower = pltpu.roll(low, PAD - half - half * at, 0)
            upper = pltpu.roll(high, (PAD - half * at) % PAD, 0)
            block[pl.ds(0, PAD), span] = lower.astype(block.dtype)
            block[pl.ds(PAD + rows, PAD), span] = upper.astype(block.dtype)

    def tile(start, count):
        terms = jnp.dot(
            block[pl.ds(start, count + 2 * PAD), :],
            weights[...],
            preferred_element_type=jnp.float32,
        )
        total = None
        for tap in range(taps):
            first = PAD + half - tap
            term = terms[first : first + count, tap * width : (tap + 1) * width]
            total = term if total is None else total + term
        return total.astype(out.dtype)

    if middle:
        out[...] = tile(quarter, 2 * quarter)
    else:
        out[pl.ds(0, quarter), :] = tile(0, quarter)
        out[pl.ds(quarter, 2 * quarter), :] = center[...]
        out[pl.ds(3 * quarter, quarter), :] = tile(3 * quarter, quarter)


def pieces_gradient(parts, weights, taps, rest=()):
    chans = weights.shape[0]
    width = weights.shape[1] // taps
    rows = parts[0].shape[0]
    middle = not rest
    return pl.pallas_call(
        functools.partial(pieces_kernel, taps=taps, pieces=len(parts), middle=middle),
        out_shape=jax.ShapeDtypeStruct((rows // 2 if middle else rows, width), jnp.bfloat16),
        in_specs=[VMEM] * (len(parts) + len(rest) + 1),
        out_specs=VMEM,
        scratch_shapes=[pltpu.VMEM((rows + 2 * PAD, chans), jnp.bfloat16)],
        cost_estimate=LITTLE,
        compiler_params=pltpu.CompilerParams(vmem_limit_bytes=24 * MIB),
    )(*parts, *rest, weights)


def weight_kernel(*refs, taps, tile, rows, size, nx, ng, layout, first, last, origins, span, stages):
    xs, gs, rest = refs[:nx], refs[nx : nx + ng], list(refs[nx + ng :])
    before = None if first else rest.pop(0)
    weights = rest.pop(0) if origins else None
    out = rest.pop(0)
    laid = rest.pop(0) if origins else None
    xbuf, gbuf, acc, sems = rest
    width = xbuf.shape[1]
    half = taps // 2
    x_rows, g_rows, starts, blanks, seams = layout()
    zeros = jnp.zeros((PAD, width), xbuf.dtype)
    xbuf[pl.ds(0, PAD), :] = zeros
    xbuf[pl.ds(PAD + rows, PAD), :] = zeros
    for wanted, row in blanks:

        @pl.when(wanted)
        def _():
            xbuf[pl.ds(row, PAD), :] = zeros

    pieces = [(src, xbuf, row, src.shape[0]) for src, row in zip(xs, x_rows)]
    pieces += [(src, gbuf, row, span or src.shape[0]) for src, row in zip(gs, g_rows)]

    def copy(at):
        src, dst, row, count = pieces[at]
        row = row if isinstance(row, int) else pl.multiple_of(row, 16)
        return pltpu.make_async_copy(
            src.at[pl.ds(0, count), :], dst.at[pl.ds(row, count), :], sems.at[at]
        )

    def each(act, stage=None):
        for at in range(nx + ng):
            if stages and stage is not None and stages[at] != stage:
                continue
            row = pieces[at][2]
            if isinstance(row, int):
                act(at)
            else:
                pl.when(row >= 0)(functools.partial(act, at))

    each(lambda at: copy(at).start())
    moves = []
    if origins:
        where = origins()
        depth = weights.shape[1] // len(where)
        for e, origin in enumerate(where):
            for tap in range(taps):
                moves.append(
                    pltpu.make_async_copy(
                        weights.at[tap, pl.ds(pl.multiple_of(origin, 16), depth), :],
                        laid.at[pl.ds(e * depth, depth), pl.ds(tap * width, width)],
                        sems.at[nx + ng + len(moves)],
                    )
                )
        for move in moves:
            move.start()
    short = size == tile and not seams and width % LANES == 0
    if not short:
        acc[...] = jnp.zeros_like(acc) if first else before[...]
    if not stages:
        each(lambda at: copy(at).wait())

    def add(start, count, side=None, base=None, close=False):
        grad = gbuf[pl.ds(start, count), :].T
        block = xbuf[pl.ds(start, count + 2 * PAD), :].astype(jnp.float32)
        if side is not None:
            row = lax.broadcasted_iota(jnp.int32, block.shape, 0)
            block = jnp.where(row >= count + PAD if side > 0 else row < PAD, block, 0.0)
        moved = []
        for tap in range(taps):
            at = PAD - half + tap
            moved.append(block[at : at + count].astype(jnp.bfloat16))
        if width % LANES:
            for tap in range(taps):
                acc[tap] += jnp.dot(grad, moved[tap], preferred_element_type=jnp.float32)
        else:
            moved = jnp.concatenate(moved, axis=1)
            total = jnp.dot(grad, moved, preferred_element_type=jnp.float32)
            if base is not None:
                total = base[...] + total
            if not close:
                acc[...] = total
            elif last:
                for tap in range(taps):
                    out[tap] = total[:, tap * width : (tap + 1) * width].astype(out.dtype)
            else:
                out[...] = total

    for stage, begin in enumerate(starts):
        if stages:
            each(lambda at: copy(at).wait(), stage)

        if short:
            base = acc if stage else before
            add(pl.multiple_of(begin, 16), tile, None, base, stage == len(starts) - 1)
            continue

        def body(step, carry):
            add(pl.multiple_of(begin + step * tile, 16), tile, None, acc)
            return carry

        lax.fori_loop(0, size // tile, body, 0)
    for wanted, row, side in seams:
        pl.when(wanted)(functools.partial(add, row, PAD, side, acc))
    if short:
        pass
    elif last and width % LANES == 0:
        for tap in range(taps):
            out[tap] = acc[:, tap * width : (tap + 1) * width].astype(out.dtype)
    else:
        out[...] = acc[...].astype(out.dtype)
    for move in moves:
        move.wait()


def weight_gradient(
    xs, gs, layout, size, taps, rows, before=None, last=True, vmem=40, weights=None, origins=None, span=None,
    stages=None
):
    width, chunk = xs[0].shape[1], gs[0].shape[1]
    split = (taps, chunk, width)
    joined = split if width % LANES else (chunk, taps * width)
    out_shape = [
        jax.ShapeDtypeStruct(split, jnp.bfloat16)
        if last
        else jax.ShapeDtypeStruct(joined, jnp.float32)
    ]
    moves = 0
    if origins:
        moves = taps * 4
        out_shape.append(
            jax.ShapeDtypeStruct((weights.shape[1], taps * width), weights.dtype)
        )
    return pl.pallas_call(
        functools.partial(
            weight_kernel,
            taps=taps,
            tile=min(1024, size) if width % LANES == 0 else min(512, size),
            rows=rows,
            size=size,
            nx=len(xs),
            ng=len(gs),
            layout=layout,
            first=before is None,
            last=last,
            origins=origins,
            span=span,
            stages=stages,
        ),
        out_shape=out_shape,
        in_specs=[SOME] * (len(xs) + len(gs))
        + [VMEM] * (before is not None)
        + [SOME] * (weights is not None),
        out_specs=[VMEM] * len(out_shape),
        scratch_shapes=[
            pltpu.VMEM((rows + 2 * PAD, width), jnp.bfloat16),
            pltpu.VMEM((rows, chunk), jnp.bfloat16),
            pltpu.VMEM(joined, jnp.float32),
            pltpu.SemaphoreType.DMA((len(xs) + len(gs) + moves,)),
        ],
        cost_estimate=LITTLE,
        compiler_params=pltpu.CompilerParams(vmem_limit_bytes=vmem * MIB),
    )(
        *xs,
        *gs,
        *([] if before is None else [before]),
        *([] if weights is None else [weights]),
    )


def merge_pairs(value, scratch):
    size = value.shape[0] // 2
    sums = []
    for at in range(value.shape[1] // LANES):
        scratch[at] = value[:, at * LANES : (at + 1) * LANES]
        even = scratch[at, pl.ds(0, size, stride=2), :]
        sums.append(even + scratch[at, pl.ds(1, size, stride=2), :])
    return jnp.concatenate(sums, axis=1)


def make_pairs(value, scratch):
    size = value.shape[0]
    rows = []
    for at in range(value.shape[1] // LANES):
        part = value[:, at * LANES : (at + 1) * LANES]
        scratch[at, pl.ds(0, size, stride=2), :] = part
        scratch[at, pl.ds(1, size, stride=2), :] = part
        rows.append(scratch[at])
    return jnp.concatenate(rows, axis=1)


def pair_scratch(rows, width):
    return pltpu.VMEM((width // LANES, rows, LANES), jnp.float32)


def each_exon(owners, exons, seen, nblocks, most, act):
    mine = lax.axis_index("seq")
    span, count = exons.shape
    for i in range(seen.shape[0]):
        seen[i] = 0

    def body(t, carry):
        owner = owners[t]
        slot = (owner ^ mine) * most + seen[owner]
        seen[owner] += 1
        for e in range(span):
            where = exons[e, t]

            @pl.when(where // nblocks == mine)
            def _():
                act(t, slot, where % nblocks)

        return carry

    lax.fori_loop(0, count, body, 0)


def front_kernel(owners, exons, pre_act, *refs, nblocks, most, size):
    outs, (slots, pair, seen) = refs[:-3], refs[-3:]
    slots[...] = jnp.zeros_like(slots)

    def act(t, slot, block):
        at = pl.ds(pl.multiple_of(block * (2 * size), 2 * size), 2 * size)
        value = pre_act[at, :].astype(jnp.float32)
        value = value * (0.5 * (1.0 + lax.erf(value * HALF_ROOT)))
        mean = 0.5 * merge_pairs(value, pair)
        slots[pl.ds(pl.multiple_of(slot * size, size), size), :] = mean

    each_exon(owners, exons, seen, nblocks, most, act)
    group = most * size
    for d, out in enumerate(outs):
        out[...] = slots[pl.ds(d * group, group), :].astype(out.dtype)


def front(owners, exons, pre_act, most, size, groups):
    rows, width = pre_act.shape
    return pl.pallas_call(
        functools.partial(
            front_kernel, nblocks=rows // 2 // size, most=most, size=size
        ),
        out_shape=[jax.ShapeDtypeStruct((most * size, width), jnp.bfloat16)] * groups,
        in_specs=[SMEM] * 2 + [VMEM],
        out_specs=[VMEM] * groups,
        scratch_shapes=[
            pltpu.VMEM((groups * most * size, width), jnp.float32),
            pair_scratch(2 * size, width),
            pltpu.SMEM((groups,), jnp.int32),
        ],
        cost_estimate=LITTLE,
        compiler_params=pltpu.CompilerParams(vmem_limit_bytes=16 * MIB),
    )(owners, exons, pre_act)


def plain_kernel(pre_act, out_grad, slope, plain, both):
    value = pre_act[...].astype(jnp.float32)
    normal = 0.5 * (1.0 + lax.erf(value * HALF_ROOT))
    slope[...] = normal + value * (jnp.exp(-0.5 * value * value) * DENSITY)
    pooled = make_pairs(out_grad[...].astype(jnp.float32) * 0.5, both)
    plain[...] = (pooled * slope[...]).astype(plain.dtype)


def plain_gradient(pre_act, out_grad):
    rows, width = pre_act.shape
    return pl.pallas_call(
        plain_kernel,
        out_shape=[
            jax.ShapeDtypeStruct((rows, width), jnp.float32),
            jax.ShapeDtypeStruct((rows, width), jnp.bfloat16),
        ],
        in_specs=[VMEM] * 2,
        out_specs=[VMEM] * 2,
        scratch_shapes=[pair_scratch(rows, width)],
        cost_estimate=LITTLE,
        compiler_params=pltpu.CompilerParams(vmem_limit_bytes=16 * MIB),
    )(pre_act, out_grad)


def gain_kernel(owners, exons, out_grad, slope, *refs, nblocks, most, size):
    splices, (grad, gain, held, both, seen) = refs[:-5], refs[-5:]
    gain[...] = out_grad[...].astype(jnp.float32)
    base = 0
    for splice in splices:
        held[pl.ds(base, splice.shape[0]), :] = splice[...].astype(jnp.float32)
        base += splice.shape[0]

    def add(t, slot, block):
        at = pl.ds(pl.multiple_of(block * size, size), size)
        gain[at, :] += held[pl.ds(pl.multiple_of(slot * size, size), size), :]

    def final(block):
        pooled = 0.5 * gain[pl.ds(pl.multiple_of(block * size, size), size), :]
        at = pl.ds(pl.multiple_of(block * (2 * size), 2 * size), 2 * size)
        return make_pairs(pooled, both) * slope[at, :]

    def renew(t, slot, block):
        at = pl.ds(pl.multiple_of(t * (2 * size), 2 * size), 2 * size)
        grad[at, :] = final(block).astype(grad.dtype)

    each_exon(owners, exons, seen, nblocks, most, add)
    each_exon(owners, exons, seen, nblocks, most, renew)
    count = exons.shape[1]
    row = lax.broadcasted_iota(jnp.int32, (2 * size, grad.shape[1]), 0)
    for at, block, first in ((count, 0, 0), (count + 1, nblocks - 1, 2 * size - 2)):
        rows = final(block)
        rows = jnp.where(row % 2 == 0, rows[first : first + 1], rows[first + 1 : first + 2])
        grad[pl.ds(at * 2 * size, 2 * size), :] = rows.astype(grad.dtype)


def gained_rows(owners, exons, out_grad, slope, splices, most, size, groups):
    rows, width = slope.shape
    return pl.pallas_call(
        functools.partial(gain_kernel, nblocks=rows // 2 // size, most=most, size=size),
        out_shape=jax.ShapeDtypeStruct(((exons.shape[1] + 2) * 2 * size, width), jnp.bfloat16),
        in_specs=[SMEM] * 2 + [VMEM] * (2 + len(splices)),
        out_specs=VMEM,
        scratch_shapes=[
            pltpu.VMEM((rows // 2, width), jnp.float32),
            pltpu.VMEM((groups * most * size, width), jnp.float32),
            pair_scratch(2 * size, width),
            pltpu.SMEM((groups,), jnp.int32),
        ],
        cost_estimate=LONG,
        compiler_params=pltpu.CompilerParams(vmem_limit_bytes=16 * MIB),
    )(owners, exons, out_grad, slope, *splices)


def mend_kernel(exons, *refs, pieces, nblocks, size):
    gained, parts, sent, own = (
        refs[pieces : 2 * pieces],
        refs[2 * pieces : 3 * pieces],
        refs[3 * pieces : -1],
        refs[-1],
    )
    mine = lax.axis_index("seq")
    place = lax.axis_index("ch")
    span, count = exons.shape
    rows = parts[0].shape[0]
    quarter = rows // pieces

    def body(t, carry):
        for e in range(span):
            where = exons[e, t]

            @pl.when(where // nblocks == mine)
            def _():
                to = pl.ds(pl.multiple_of(where % nblocks * (2 * size), 2 * size), 2 * size)
                at = pl.ds(pl.multiple_of(t * (2 * size), 2 * size), 2 * size)
                for part, new in zip(parts, gained):
                    part[to, :] = new[at, :]

        return carry

    lax.fori_loop(0, count, body, 0)
    row = lax.broadcasted_iota(jnp.int32, (PAD, own.shape[1]), 0)
    for d, out in enumerate(sent, 1):
        for tag, part in enumerate(parts):

            @pl.when(mine ^ d ^ place == tag)
            def _():
                at = pl.ds(pl.multiple_of(place * quarter, quarter), quarter)
                out[pl.ds(0, quarter), :] = part[at, :]

        if out.shape[0] > quarter:
            after_me = (mine ^ d) > mine
            edge = jnp.zeros(row.shape, jnp.float32)
            for tag, new in enumerate(gained):
                head = new[pl.ds(count * 2 * size, PAD), :].astype(jnp.float32)
                tail = new[pl.ds((count + 1) * 2 * size, PAD), :].astype(jnp.float32)
                edge = jnp.where(row // 2 == tag, jnp.where(after_me, tail, head), edge)
            out[pl.ds(quarter, PAD), :] = edge.astype(out.dtype)
    for tag, part in enumerate(parts):

        @pl.when(mine ^ place == tag)
        def _():
            own[...] = part[...]


def mend(exons, parts, gained, size):
    rows, width = parts[0].shape
    pieces = len(parts)
    whole = jax.ShapeDtypeStruct((rows, width), jnp.bfloat16)
    quarter = rows // pieces
    sent = [
        jax.ShapeDtypeStruct((quarter + (PAD if d in (1, 3) else 0), width), jnp.bfloat16)
        for d in range(1, pieces)
    ]
    outs = pl.pallas_call(
        functools.partial(mend_kernel, pieces=pieces, nblocks=rows // 2 // size, size=size),
        out_shape=[whole] * pieces + sent + [whole],
        in_specs=[SMEM] + [VMEM] * (2 * pieces),
        out_specs=[VMEM] * (pieces + len(sent) + 1),
        input_output_aliases={1 + at: at for at in range(pieces)},
        cost_estimate=LITTLE,
        compiler_params=pltpu.CompilerParams(vmem_limit_bytes=24 * MIB),
    )(exons, *parts, *gained)
    return outs[:pieces], outs[pieces:-1], outs[-1]


def gathered_gradient(pre_act, out_grad, coverage_obs, owners, exon_blocks):
    rows, width = pre_act.shape
    nseq = lax.axis_size("seq")
    mine = lax.axis_index("seq")
    most, block = coverage_obs.shape[1:3]
    nblocks = rows // 2 // block
    counts = owners.shape[0]
    value = pre_act.astype(jnp.float32)
    normal = 0.5 * (1.0 + jax.scipy.special.erf(value * HALF_ROOT))
    slope = normal + value * jnp.exp(-0.5 * value * value) * DENSITY
    act = value * normal
    pooled = (0.5 * jnp.sum(act.reshape(rows // 2, 2, width), axis=1)).astype(jnp.bfloat16)
    order = jnp.arange(counts, dtype=jnp.int32)
    same = owners[:, None] == owners[None, :]
    rank = jnp.sum((same & (order[:, None] < order[None, :])).astype(jnp.int32), axis=0)
    dest = jnp.arange(nseq, dtype=jnp.int32)
    slots = jnp.arange(most, dtype=jnp.int32)
    route = (owners[None, None, :] == dest[:, None, None]) & (
        rank[None, None, :] == slots[None, :, None]
    )
    route = route.astype(jnp.float32).reshape(nseq * most, counts)
    on_mine = exon_blocks // nblocks == mine
    holds = jnp.any(on_mine, axis=1)
    local_block = jnp.sum(jnp.where(on_mine, exon_blocks % nblocks, 0), axis=1)
    select = (
        holds[:, None] & (local_block[:, None] == jnp.arange(nblocks, dtype=jnp.int32)[None, :])
    ).astype(jnp.float32)
    picker = jnp.dot(route, select, precision=lax.Precision.HIGHEST).astype(jnp.bfloat16)
    pieces = pooled.reshape(nblocks, block * width)
    outgoing = jnp.dot(picker, pieces, preferred_element_type=jnp.float32).astype(jnp.bfloat16)
    outgoing = outgoing.reshape(nseq, most, block, width)
    arrived = lax.all_to_all(outgoing, "seq", split_axis=0, concat_axis=0, tiled=True)
    coverage = jnp.sum(arrived.astype(jnp.float32), axis=0)
    splice = jnp.tanh(coverage - coverage_obs[0]).astype(jnp.bfloat16)
    returned = lax.all_gather(splice, "seq", axis=0).reshape(nseq * most, block * width)
    gained = jnp.dot(picker.T, returned, preferred_element_type=jnp.float32)
    pooled_grad = out_grad.astype(jnp.float32) + gained.reshape(rows // 2, width)
    return (jnp.repeat(pooled_grad, 2, axis=0) * 0.5 * slope).astype(jnp.bfloat16)


def local(x_saved, pre_act, out_grad, conv_w, coverage_obs, owners, exon_blocks):
    rows, width = x_saved.shape
    taps = conv_w.shape[1]
    nseq = lax.axis_size("seq")
    nch = lax.axis_size("ch")
    chunk = conv_w.shape[0] // nseq
    most = coverage_obs.shape[1]
    size = coverage_obs.shape[2]
    direct = nseq == nch == 4 and chunk == width and width % 128 == 0
    exons = exon_blocks.T
    weights = conv_w.transpose(1, 0, 2)
    target = coverage_obs[0].reshape(most * size, width)

    if not direct:
        pre_grad = gathered_gradient(pre_act, out_grad, coverage_obs, owners, exon_blocks)
        x_all = lax.all_gather(x_saved, "seq", axis=0, tiled=True)
        whole = lax.all_gather(pre_grad, "ch", axis=1, tiled=True)
        blocks = whole.reshape(rows, nseq, chunk).transpose(1, 0, 2)
        g_all = lax.all_to_all(blocks, "seq", 0, 0, tiled=True).reshape(nseq * rows, chunk)
        low = shift(whole[rows - PAD :], "seq", 1)
        high = shift(whole[:PAD], "seq", -1)
        in_grad = input_gradient(whole, low, high, weights)
        total = nseq * rows
        (w_grad,) = weight_gradient(
            [x_all], [g_all], lambda: ([PAD], [0], [0], [], []), total, taps, total
        )
        return (in_grad, w_grad.transpose(1, 0, 2))

    outgoing = front(owners, exons, pre_act, most, size, nseq)
    slope, plain = plain_gradient(pre_act, out_grad)
    arrived = [outgoing[0]] + [swap(outgoing[d], "seq", d) for d in range(1, nseq)]
    (source,) = after([x_saved], outgoing)
    up1, down1 = shift(source, "seq", 1), shift(source, "seq", -1)
    *arrived, plain, slope = after([*arrived, plain, slope])
    far, near = swap(plain, "ch", 2), swap(plain, "ch", 1)
    coverage = functools.reduce(jnp.add, [a.astype(jnp.float32) for a in arrived])
    splice = jnp.tanh(coverage - target).astype(jnp.bfloat16)
    (last_splice,) = after([splice], [up1, down1])
    splices = [splice, swap(splice, "seq", 1), swap(splice, "seq", 2), swap(last_splice, "seq", 3)]
    gained = gained_rows(owners, exons, out_grad, slope, splices, most, size, nseq)

    far_gained, near_gained = swap(gained, "ch", 2), swap(gained, "ch", 1)
    up2, down2 = shift(up1, "seq", 1, 1), shift(down1, "seq", -1, 1)
    beyond = swap(far, "ch", 1)
    gained = [gained, near_gained, far_gained, swap(far_gained, "ch", 1)]
    *gained, beyond, up2, down2 = after([*gained, beyond, up2, down2])

    quarter = rows // nch
    parts, sent, own = mend(exons, [plain, near, far, beyond], gained, size)
    *sent, up2, down2 = after([*sent, up2, down2])
    got = [swap(block, "seq", d) for d, block in zip(range(1, nseq), sent)]
    up3, down3 = shift(up2, "seq", 1, 2), shift(down2, "seq", -1, 2)

    def origins():
        return [(lax.axis_index("ch") ^ t) * width for t in range(nch)]

    partial, laid = weight_gradient(
        [up1[rows - PAD :], x_saved, down1[:PAD]],
        [own],
        lambda: ([0, PAD, PAD + rows], [0], [0], [], []),
        rows,
        taps,
        rows,
        last=False,
        vmem=24,
        weights=weights,
        origins=origins,
    )
    center = pieces_gradient(parts, laid, taps)
    first, *rest, partial, center = after([*got, partial, center])
    across_first = swap(first, "ch", 2)
    crossing = jnp.concatenate([block[:quarter] for block in rest])
    across = swap(crossing, "ch", 2)
    beside = swap(crossing, "ch", 1)
    beside_first = swap(first, "ch", 1)
    in_grad = pieces_gradient(parts, laid, taps, [first, rest[1], center])
    across_first, in_grad = after([across_first, in_grad])
    beyond_first = swap(across_first, "ch", 1)

    def layout(hops, blocks):
        mine = lax.axis_index("seq")
        place = lax.axis_index("ch")
        x_rows = [PAD + mine * rows]
        for hop in range(1, hops):
            low_at, high_at = mine - hop, mine + hop
            x_rows += [
                jnp.where(low_at >= 0, PAD + low_at * rows, -1),
                jnp.where(high_at < nseq, PAD + high_at * rows, -1),
            ]
        g_rows = [
            (mine ^ d) * rows + (place ^ tag) * quarter for d in blocks for tag in range(nch)
        ]
        return x_rows, g_rows, [(mine ^ d) * rows for d in blocks], [], []

    (partial,) = weight_gradient(
        [x_saved, up1, down1, up2, down2],
        [first, beside_first, across_first, beyond_first],
        functools.partial(layout, 3, (1,)),
        rows,
        taps,
        nseq * rows,
        before=partial,
        last=False,
        vmem=32,
        span=quarter,
    )
    across, in_grad, partial, up3, down3 = after([across, in_grad, partial, up3, down3])
    beyond = swap(across, "ch", 1)

    g_pieces = []
    for d in range(nseq - 2):
        for piece in (crossing, beside, across, beyond):
            g_pieces.append(piece[d * quarter : (d + 1) * quarter])
    (w_grad,) = weight_gradient(
        [x_saved, up1, down1, up2, down2, up3, down3],
        g_pieces,
        functools.partial(layout, nseq, (2, 3)),
        rows,
        taps,
        nseq * rows,
        before=partial,
        vmem=32,
    )
    return (in_grad, w_grad.transpose(1, 0, 2))


def solution(mesh):
    in_specs = (
        P(("grp", "seq"), "ch"),
        P(("grp", "seq"), "ch"),
        P(("grp", "seq"), "ch"),
        P(None, None, "ch"),
        P(("grp", "seq"), None, None, "ch"),
        P("grp"),
        P("grp", None),
    )
    out_specs = (P(("grp", "seq"), "ch"), P(("grp", "seq"), None, "ch"))
    return jax.shard_map(local, mesh=mesh, in_specs=in_specs, out_specs=out_specs, check_vma=False)
```

```python
import functools

import jax
import jax.numpy as jnp
from jax import lax
from jax.experimental import pallas as pl
from jax.experimental.pallas import tpu as pltpu
from jax.sharding import PartitionSpec as P

PAD = 16
MIB = 1024 * 1024
VMEM = pl.BlockSpec(memory_space=pltpu.VMEM)
SMEM = pl.BlockSpec(memory_space=pltpu.SMEM)
SOME = pl.BlockSpec(memory_space=pl.ANY)
HALF_ROOT = 0.7071067811865476
DENSITY = 0.3989422804014327
LANES = 128
LONG = pl.CostEstimate(flops=4 * 10**9, bytes_accessed=1000, transcendentals=0)
LITTLE = pl.CostEstimate(flops=1000, bytes_accessed=1000, transcendentals=0)


def swap(block, axis, flip):
    count = lax.axis_size(axis)
    return lax.ppermute(block, axis, [(i, i ^ flip) for i in range(count)])


def shift(block, axis, step, first=0):
    count = lax.axis_size(axis)
    if step > 0:
        pairs = [(i, i + 1) for i in range(first, count - 1)]
    else:
        pairs = [(i + 1, i) for i in range(count - 1 - first)]
    return lax.ppermute(block, axis, pairs)


def after(values, others=()):
    return lax.optimization_barrier(tuple(values) + tuple(others))[: len(values)]


def input_kernel(part, low, high, weights, out, block):
    taps = weights.shape[0]
    rows = part.shape[0]
    half = taps // 2
    block[pl.ds(0, PAD), :] = low[...]
    block[pl.ds(PAD, rows), :] = part[...]
    block[pl.ds(PAD + rows, PAD), :] = high[...]
    tile = min(256, rows)

    def body(step, carry):
        start = pl.multiple_of(step * tile, tile)
        rows_in = block[pl.ds(start, tile + 2 * PAD), :]
        total = None
        for tap in range(taps):
            term = jnp.dot(rows_in, weights[tap], preferred_element_type=jnp.float32)
            first = PAD + half - tap
            term = term[first : first + tile]
            total = term if total is None else total + term
        out[pl.ds(start, tile), :] = total.astype(out.dtype)
        return carry

    lax.fori_loop(0, rows // tile, body, 0)


def input_gradient(part, low, high, weights):
    taps, chans, width = weights.shape
    rows = part.shape[0]
    return pl.pallas_call(
        input_kernel,
        out_shape=jax.ShapeDtypeStruct((rows, width), jnp.bfloat16),
        in_specs=[VMEM] * 4,
        out_specs=VMEM,
        scratch_shapes=[pltpu.VMEM((rows + 2 * PAD, chans), jnp.bfloat16)],
        compiler_params=pltpu.CompilerParams(vmem_limit_bytes=32 * MIB),
    )(part, low, high, weights)


def pieces_kernel(*refs, taps, pieces, middle):
    parts, rest = refs[:pieces], refs[pieces:]
    if middle:
        weights, out, block = rest
    else:
        near_edge, far_edge, center, weights, out, block = rest
    rows = parts[0].shape[0]
    width = weights.shape[1] // taps
    half = taps // 2
    quarter = rows // 4
    kept = [(0, rows)] if middle else [(0, quarter + PAD), (rows - quarter - PAD, quarter + PAD)]
    base = 0
    for part in parts:
        span = pl.ds(base, part.shape[1])
        for begin, count in kept:
            block[pl.ds(PAD + begin, count), span] = part[pl.ds(begin, count), :]
        base += part.shape[1]
    if not middle:
        mine = lax.axis_index("seq")
        one = near_edge[pl.ds(quarter, PAD), :].astype(jnp.float32)
        other = far_edge[pl.ds(quarter, PAD), :].astype(jnp.float32)
        low = jnp.where(mine % 2 == 1, one, jnp.where(mine == 2, other, 0.0))
        high = jnp.where(mine % 2 == 0, one, jnp.where(mine == 1, other, 0.0))
        for at in range(pieces):
            span = pl.ds(at * part.shape[1], part.shape[1])
            lower = pltpu.roll(low, PAD - half - half * at, 0)
            upper = pltpu.roll(high, (PAD - half * at) % PAD, 0)
            block[pl.ds(0, PAD), span] = lower.astype(block.dtype)
            block[pl.ds(PAD + rows, PAD), span] = upper.astype(block.dtype)

    def tile(start, count):
        terms = jnp.dot(
            block[pl.ds(start, count + 2 * PAD), :],
            weights[...],
            preferred_element_type=jnp.float32,
        )
        total = None
        for tap in range(taps):
            first = PAD + half - tap
            term = terms[first : first + count, tap * width : (tap + 1) * width]
            total = term if total is None else total + term
        return total.astype(out.dtype)

    if middle:
        out[...] = tile(quarter, 2 * quarter)
    else:
        out[pl.ds(0, quarter), :] = tile(0, quarter)
        out[pl.ds(quarter, 2 * quarter), :] = center[...]
        out[pl.ds(3 * quarter, quarter), :] = tile(3 * quarter, quarter)


def pieces_gradient(parts, weights, taps, rest=()):
    chans = weights.shape[0]
    width = weights.shape[1] // taps
    rows = parts[0].shape[0]
    middle = not rest
    return pl.pallas_call(
        functools.partial(pieces_kernel, taps=taps, pieces=len(parts), middle=middle),
        out_shape=jax.ShapeDtypeStruct((rows // 2 if middle else rows, width), jnp.bfloat16),
        in_specs=[VMEM] * (len(parts) + len(rest) + 1),
        out_specs=VMEM,
        scratch_shapes=[pltpu.VMEM((rows + 2 * PAD, chans), jnp.bfloat16)],
        cost_estimate=LITTLE,
        compiler_params=pltpu.CompilerParams(vmem_limit_bytes=24 * MIB),
    )(*parts, *rest, weights)


def weight_kernel(*refs, taps, tile, rows, size, nx, ng, layout, first, last, origins, span, stages):
    xs, gs, rest = refs[:nx], refs[nx : nx + ng], list(refs[nx + ng :])
    before = None if first else rest.pop(0)
    weights = rest.pop(0) if origins else None
    out = rest.pop(0)
    laid = rest.pop(0) if origins else None
    xbuf, gbuf, acc, sems = rest
    width = xbuf.shape[1]
    half = taps // 2
    x_rows, g_rows, starts, blanks, seams = layout()
    zeros = jnp.zeros((PAD, width), xbuf.dtype)
    xbuf[pl.ds(0, PAD), :] = zeros
    xbuf[pl.ds(PAD + rows, PAD), :] = zeros
    for wanted, row in blanks:

        @pl.when(wanted)
        def _():
            xbuf[pl.ds(row, PAD), :] = zeros

    pieces = [(src, xbuf, row, src.shape[0]) for src, row in zip(xs, x_rows)]
    pieces += [(src, gbuf, row, span or src.shape[0]) for src, row in zip(gs, g_rows)]

    def copy(at):
        src, dst, row, count = pieces[at]
        row = row if isinstance(row, int) else pl.multiple_of(row, 16)
        return pltpu.make_async_copy(
            src.at[pl.ds(0, count), :], dst.at[pl.ds(row, count), :], sems.at[at]
        )

    def each(act, stage=None):
        for at in range(nx + ng):
            if stages and stage is not None and stages[at] != stage:
                continue
            row = pieces[at][2]
            if isinstance(row, int):
                act(at)
            else:
                pl.when(row >= 0)(functools.partial(act, at))

    each(lambda at: copy(at).start())
    moves = []
    if origins:
        where = origins()
        depth = weights.shape[1] // len(where)
        for e, origin in enumerate(where):
            for tap in range(taps):
                moves.append(
                    pltpu.make_async_copy(
                        weights.at[tap, pl.ds(pl.multiple_of(origin, 16), depth), :],
                        laid.at[pl.ds(e * depth, depth), pl.ds(tap * width, width)],
                        sems.at[nx + ng + len(moves)],
                    )
                )
        for move in moves:
            move.start()
    short = size == tile and not seams and width % LANES == 0
    if not short:
        acc[...] = jnp.zeros_like(acc) if first else before[...]
    if not stages:
        each(lambda at: copy(at).wait())

    def add(start, count, side=None, base=None, close=False):
        grad = gbuf[pl.ds(start, count), :].T
        block = xbuf[pl.ds(start, count + 2 * PAD), :].astype(jnp.float32)
        if side is not None:
            row = lax.broadcasted_iota(jnp.int32, block.shape, 0)
            block = jnp.where(row >= count + PAD if side > 0 else row < PAD, block, 0.0)
        moved = []
        for tap in range(taps):
            at = PAD - half + tap
            moved.append(block[at : at + count].astype(jnp.bfloat16))
        if width % LANES:
            for tap in range(taps):
                acc[tap] += jnp.dot(grad, moved[tap], preferred_element_type=jnp.float32)
        else:
            moved = jnp.concatenate(moved, axis=1)
            total = jnp.dot(grad, moved, preferred_element_type=jnp.float32)
            if base is not None:
                total = base[...] + total
            if not close:
                acc[...] = total
            elif last:
                for tap in range(taps):
                    out[tap] = total[:, tap * width : (tap + 1) * width].astype(out.dtype)
            else:
                out[...] = total

    for stage, begin in enumerate(starts):
        if stages:
            each(lambda at: copy(at).wait(), stage)

        if short:
            base = acc if stage else before
            add(pl.multiple_of(begin, 16), tile, None, base, stage == len(starts) - 1)
            continue

        def body(step, carry):
            add(pl.multiple_of(begin + step * tile, 16), tile, None, acc)
            return carry

        lax.fori_loop(0, size // tile, body, 0)
    for wanted, row, side in seams:
        pl.when(wanted)(functools.partial(add, row, PAD, side, acc))
    if short:
        pass
    elif last and width % LANES == 0:
        for tap in range(taps):
            out[tap] = acc[:, tap * width : (tap + 1) * width].astype(out.dtype)
    else:
        out[...] = acc[...].astype(out.dtype)
    for move in moves:
        move.wait()


def weight_gradient(
    xs, gs, layout, size, taps, rows, before=None, last=True, vmem=40, weights=None, origins=None, span=None,
    stages=None
):
    width, chunk = xs[0].shape[1], gs[0].shape[1]
    split = (taps, chunk, width)
    joined = split if width % LANES else (chunk, taps * width)
    out_shape = [
        jax.ShapeDtypeStruct(split, jnp.bfloat16)
        if last
        else jax.ShapeDtypeStruct(joined, jnp.float32)
    ]
    moves = 0
    if origins:
        moves = taps * 4
        out_shape.append(
            jax.ShapeDtypeStruct((weights.shape[1], taps * width), weights.dtype)
        )
    return pl.pallas_call(
        functools.partial(
            weight_kernel,
            taps=taps,
            tile=min(1024, size) if width % LANES == 0 else min(512, size),
            rows=rows,
            size=size,
            nx=len(xs),
            ng=len(gs),
            layout=layout,
            first=before is None,
            last=last,
            origins=origins,
            span=span,
            stages=stages,
        ),
        out_shape=out_shape,
        in_specs=[SOME] * (len(xs) + len(gs))
        + [VMEM] * (before is not None)
        + [SOME] * (weights is not None),
        out_specs=[VMEM] * len(out_shape),
        scratch_shapes=[
            pltpu.VMEM((rows + 2 * PAD, width), jnp.bfloat16),
            pltpu.VMEM((rows, chunk), jnp.bfloat16),
            pltpu.VMEM(joined, jnp.float32),
            pltpu.SemaphoreType.DMA((len(xs) + len(gs) + moves,)),
        ],
        cost_estimate=LITTLE,
        compiler_params=pltpu.CompilerParams(vmem_limit_bytes=vmem * MIB),
    )(
        *xs,
        *gs,
        *([] if before is None else [before]),
        *([] if weights is None else [weights]),
    )


def merge_pairs(value, scratch):
    size = value.shape[0] // 2
    sums = []
    for at in range(value.shape[1] // LANES):
        scratch[at] = value[:, at * LANES : (at + 1) * LANES]
        even = scratch[at, pl.ds(0, size, stride=2), :]
        sums.append(even + scratch[at, pl.ds(1, size, stride=2), :])
    return jnp.concatenate(sums, axis=1)


def make_pairs(value, scratch):
    size = value.shape[0]
    rows = []
    for at in range(value.shape[1] // LANES):
        part = value[:, at * LANES : (at + 1) * LANES]
        scratch[at, pl.ds(0, size, stride=2), :] = part
        scratch[at, pl.ds(1, size, stride=2), :] = part
        rows.append(scratch[at])
    return jnp.concatenate(rows, axis=1)


def pair_scratch(rows, width):
    return pltpu.VMEM((width // LANES, rows, LANES), jnp.float32)


def each_exon(owners, exons, seen, nblocks, most, act):
    mine = lax.axis_index("seq")
    span, count = exons.shape
    for i in range(seen.shape[0]):
        seen[i] = 0

    def body(t, carry):
        owner = owners[t]
        slot = (owner ^ mine) * most + seen[owner]
        seen[owner] += 1
        for e in range(span):
            where = exons[e, t]

            @pl.when(where // nblocks == mine)
            def _():
                act(t, slot, where % nblocks)

        return carry

    lax.fori_loop(0, count, body, 0)


def front_kernel(owners, exons, pre_act, *refs, nblocks, most, size):
    outs, (slots, pair, seen) = refs[:-3], refs[-3:]
    slots[...] = jnp.zeros_like(slots)

    def act(t, slot, block):
        at = pl.ds(pl.multiple_of(block * (2 * size), 2 * size), 2 * size)
        value = pre_act[at, :].astype(jnp.float32)
        value = value * (0.5 * (1.0 + lax.erf(value * HALF_ROOT)))
        mean = 0.5 * merge_pairs(value, pair)
        slots[pl.ds(pl.multiple_of(slot * size, size), size), :] = mean

    each_exon(owners, exons, seen, nblocks, most, act)
    group = most * size
    for d, out in enumerate(outs):
        out[...] = slots[pl.ds(d * group, group), :].astype(out.dtype)


def front(owners, exons, pre_act, most, size, groups):
    rows, width = pre_act.shape
    return pl.pallas_call(
        functools.partial(
            front_kernel, nblocks=rows // 2 // size, most=most, size=size
        ),
        out_shape=[jax.ShapeDtypeStruct((most * size, width), jnp.bfloat16)] * groups,
        in_specs=[SMEM] * 2 + [VMEM],
        out_specs=[VMEM] * groups,
        scratch_shapes=[
            pltpu.VMEM((groups * most * size, width), jnp.float32),
            pair_scratch(2 * size, width),
            pltpu.SMEM((groups,), jnp.int32),
        ],
        cost_estimate=LITTLE,
        compiler_params=pltpu.CompilerParams(vmem_limit_bytes=16 * MIB),
    )(owners, exons, pre_act)


def plain_kernel(pre_act, out_grad, slope, plain, both):
    value = pre_act[...].astype(jnp.float32)
    normal = 0.5 * (1.0 + lax.erf(value * HALF_ROOT))
    slope[...] = normal + value * (jnp.exp(-0.5 * value * value) * DENSITY)
    pooled = make_pairs(out_grad[...].astype(jnp.float32) * 0.5, both)
    plain[...] = (pooled * slope[...]).astype(plain.dtype)


def plain_gradient(pre_act, out_grad):
    rows, width = pre_act.shape
    return pl.pallas_call(
        plain_kernel,
        out_shape=[
            jax.ShapeDtypeStruct((rows, width), jnp.float32),
            jax.ShapeDtypeStruct((rows, width), jnp.bfloat16),
        ],
        in_specs=[VMEM] * 2,
        out_specs=[VMEM] * 2,
        scratch_shapes=[pair_scratch(rows, width)],
        cost_estimate=LITTLE,
        compiler_params=pltpu.CompilerParams(vmem_limit_bytes=16 * MIB),
    )(pre_act, out_grad)


def gain_kernel(owners, exons, out_grad, slope, *refs, nblocks, most, size):
    splices, (grad, gain, held, both, seen) = refs[:-5], refs[-5:]
    gain[...] = out_grad[...].astype(jnp.float32)
    base = 0
    for splice in splices:
        held[pl.ds(base, splice.shape[0]), :] = splice[...].astype(jnp.float32)
        base += splice.shape[0]

    def add(t, slot, block):
        at = pl.ds(pl.multiple_of(block * size, size), size)
        gain[at, :] += held[pl.ds(pl.multiple_of(slot * size, size), size), :]

    def final(block):
        pooled = 0.5 * gain[pl.ds(pl.multiple_of(block * size, size), size), :]
        at = pl.ds(pl.multiple_of(block * (2 * size), 2 * size), 2 * size)
        return make_pairs(pooled, both) * slope[at, :]

    def renew(t, slot, block):
        at = pl.ds(pl.multiple_of(t * (2 * size), 2 * size), 2 * size)
        grad[at, :] = final(block).astype(grad.dtype)

    each_exon(owners, exons, seen, nblocks, most, add)
    each_exon(owners, exons, seen, nblocks, most, renew)
    count = exons.shape[1]
    row = lax.broadcasted_iota(jnp.int32, (2 * size, grad.shape[1]), 0)
    for at, block, first in ((count, 0, 0), (count + 1, nblocks - 1, 2 * size - 2)):
        rows = final(block)
        rows = jnp.where(row % 2 == 0, rows[first : first + 1], rows[first + 1 : first + 2])
        grad[pl.ds(at * 2 * size, 2 * size), :] = rows.astype(grad.dtype)


def gained_rows(owners, exons, out_grad, slope, splices, most, size, groups):
    rows, width = slope.shape
    return pl.pallas_call(
        functools.partial(gain_kernel, nblocks=rows // 2 // size, most=most, size=size),
        out_shape=jax.ShapeDtypeStruct(((exons.shape[1] + 2) * 2 * size, width), jnp.bfloat16),
        in_specs=[SMEM] * 2 + [VMEM] * (2 + len(splices)),
        out_specs=VMEM,
        scratch_shapes=[
            pltpu.VMEM((rows // 2, width), jnp.float32),
            pltpu.VMEM((groups * most * size, width), jnp.float32),
            pair_scratch(2 * size, width),
            pltpu.SMEM((groups,), jnp.int32),
        ],
        cost_estimate=LONG,
        compiler_params=pltpu.CompilerParams(vmem_limit_bytes=16 * MIB),
    )(owners, exons, out_grad, slope, *splices)


def mend_kernel(exons, *refs, pieces, nblocks, size):
    gained, parts, sent, own = (
        refs[pieces : 2 * pieces],
        refs[2 * pieces : 3 * pieces],
        refs[3 * pieces : -1],
        refs[-1],
    )
    mine = lax.axis_index("seq")
    place = lax.axis_index("ch")
    span, count = exons.shape
    rows = parts[0].shape[0]
    quarter = rows // pieces

    def body(t, carry):
        for e in range(span):
            where = exons[e, t]

            @pl.when(where // nblocks == mine)
            def _():
                to = pl.ds(pl.multiple_of(where % nblocks * (2 * size), 2 * size), 2 * size)
                at = pl.ds(pl.multiple_of(t * (2 * size), 2 * size), 2 * size)
                for part, new in zip(parts, gained):
                    part[to, :] = new[at, :]

        return carry

    lax.fori_loop(0, count, body, 0)
    row = lax.broadcasted_iota(jnp.int32, (PAD, own.shape[1]), 0)
    for d, out in enumerate(sent, 1):
        for tag, part in enumerate(parts):

            @pl.when(mine ^ d ^ place == tag)
            def _():
                at = pl.ds(pl.multiple_of(place * quarter, quarter), quarter)
                out[pl.ds(0, quarter), :] = part[at, :]

        if out.shape[0] > quarter:
            after_me = (mine ^ d) > mine
            edge = jnp.zeros(row.shape, jnp.float32)
            for tag, new in enumerate(gained):
                head = new[pl.ds(count * 2 * size, PAD), :].astype(jnp.float32)
                tail = new[pl.ds((count + 1) * 2 * size, PAD), :].astype(jnp.float32)
                edge = jnp.where(row // 2 == tag, jnp.where(after_me, tail, head), edge)
            out[pl.ds(quarter, PAD), :] = edge.astype(out.dtype)
    for tag, part in enumerate(parts):

        @pl.when(mine ^ place == tag)
        def _():
            own[...] = part[...]


def mend(exons, parts, gained, size):
    rows, width = parts[0].shape
    pieces = len(parts)
    whole = jax.ShapeDtypeStruct((rows, width), jnp.bfloat16)
    quarter = rows // pieces
    sent = [
        jax.ShapeDtypeStruct((quarter + (PAD if d in (1, 3) else 0), width), jnp.bfloat16)
        for d in range(1, pieces)
    ]
    outs = pl.pallas_call(
        functools.partial(mend_kernel, pieces=pieces, nblocks=rows // 2 // size, size=size),
        out_shape=[whole] * pieces + sent + [whole],
        in_specs=[SMEM] + [VMEM] * (2 * pieces),
        out_specs=[VMEM] * (pieces + len(sent) + 1),
        input_output_aliases={1 + at: at for at in range(pieces)},
        cost_estimate=LITTLE,
        compiler_params=pltpu.CompilerParams(vmem_limit_bytes=24 * MIB),
    )(exons, *parts, *gained)
    return outs[:pieces], outs[pieces:-1], outs[-1]


def gathered_gradient(pre_act, out_grad, coverage_obs, owners, exon_blocks):
    rows, width = pre_act.shape
    nseq = lax.axis_size("seq")
    mine = lax.axis_index("seq")
    most, block = coverage_obs.shape[1:3]
    nblocks = rows // 2 // block
    counts = owners.shape[0]
    value = pre_act.astype(jnp.float32)
    normal = 0.5 * (1.0 + jax.scipy.special.erf(value * HALF_ROOT))
    slope = normal + value * jnp.exp(-0.5 * value * value) * DENSITY
    act = value * normal
    pooled = (0.5 * jnp.sum(act.reshape(rows // 2, 2, width), axis=1)).astype(jnp.bfloat16)
    order = jnp.arange(counts, dtype=jnp.int32)
    same = owners[:, None] == owners[None, :]
    rank = jnp.sum((same & (order[:, None] < order[None, :])).astype(jnp.int32), axis=0)
    dest = jnp.arange(nseq, dtype=jnp.int32)
    slots = jnp.arange(most, dtype=jnp.int32)
    route = (owners[None, None, :] == dest[:, None, None]) & (
        rank[None, None, :] == slots[None, :, None]
    )
    route = route.astype(jnp.float32).reshape(nseq * most, counts)
    on_mine = exon_blocks // nblocks == mine
    holds = jnp.any(on_mine, axis=1)
    local_block = jnp.sum(jnp.where(on_mine, exon_blocks % nblocks, 0), axis=1)
    select = (
        holds[:, None] & (local_block[:, None] == jnp.arange(nblocks, dtype=jnp.int32)[None, :])
    ).astype(jnp.float32)
    picker = jnp.dot(route, select, precision=lax.Precision.HIGHEST).astype(jnp.bfloat16)
    pieces = pooled.reshape(nblocks, block * width)
    outgoing = jnp.dot(picker, pieces, preferred_element_type=jnp.float32).astype(jnp.bfloat16)
    outgoing = outgoing.reshape(nseq, most, block, width)
    arrived = lax.all_to_all(outgoing, "seq", split_axis=0, concat_axis=0, tiled=True)
    coverage = jnp.sum(arrived.astype(jnp.float32), axis=0)
    splice = jnp.tanh(coverage - coverage_obs[0]).astype(jnp.bfloat16)
    returned = lax.all_gather(splice, "seq", axis=0).reshape(nseq * most, block * width)
    gained = jnp.dot(picker.T, returned, preferred_element_type=jnp.float32)
    pooled_grad = out_grad.astype(jnp.float32) + gained.reshape(rows // 2, width)
    return (jnp.repeat(pooled_grad, 2, axis=0) * 0.5 * slope).astype(jnp.bfloat16)


def local(x_saved, pre_act, out_grad, conv_w, coverage_obs, owners, exon_blocks):
    rows, width = x_saved.shape
    taps = conv_w.shape[1]
    nseq = lax.axis_size("seq")
    nch = lax.axis_size("ch")
    chunk = conv_w.shape[0] // nseq
    most = coverage_obs.shape[1]
    size = coverage_obs.shape[2]
    direct = nseq == nch == 4 and chunk == width and width % 128 == 0
    exons = exon_blocks.T
    weights = conv_w.transpose(1, 0, 2)
    target = coverage_obs[0].reshape(most * size, width)

    if not direct:
        pre_grad = gathered_gradient(pre_act, out_grad, coverage_obs, owners, exon_blocks)
        x_all = lax.all_gather(x_saved, "seq", axis=0, tiled=True)
        whole = lax.all_gather(pre_grad, "ch", axis=1, tiled=True)
        blocks = whole.reshape(rows, nseq, chunk).transpose(1, 0, 2)
        g_all = lax.all_to_all(blocks, "seq", 0, 0, tiled=True).reshape(nseq * rows, chunk)
        low = shift(whole[rows - PAD :], "seq", 1)
        high = shift(whole[:PAD], "seq", -1)
        in_grad = input_gradient(whole, low, high, weights)
        total = nseq * rows
        (w_grad,) = weight_gradient(
            [x_all], [g_all], lambda: ([PAD], [0], [0], [], []), total, taps, total
        )
        return (in_grad, w_grad.transpose(1, 0, 2))

    outgoing = front(owners, exons, pre_act, most, size, nseq)
    slope, plain = plain_gradient(pre_act, out_grad)
    arrived = [outgoing[0]] + [swap(outgoing[d], "seq", d) for d in range(1, nseq)]
    (source,) = after([x_saved], outgoing)
    up1, down1 = shift(source, "seq", 1), shift(source, "seq", -1)
    *arrived, plain, slope = after([*arrived, plain, slope])
    far, near = swap(plain, "ch", 2), swap(plain, "ch", 1)
    coverage = functools.reduce(jnp.add, [a.astype(jnp.float32) for a in arrived])
    splice = jnp.tanh(coverage - target).astype(jnp.bfloat16)
    (last_splice,) = after([splice], [up1, down1])
    splices = [splice, swap(splice, "seq", 1), swap(splice, "seq", 2), swap(last_splice, "seq", 3)]
    gained = gained_rows(owners, exons, out_grad, slope, splices, most, size, nseq)

    far_gained, near_gained = swap(gained, "ch", 2), swap(gained, "ch", 1)
    up2, down2 = shift(up1, "seq", 1, 1), shift(down1, "seq", -1, 1)
    beyond = swap(far, "ch", 1)
    gained = [gained, near_gained, far_gained, swap(far_gained, "ch", 1)]
    *gained, beyond, up2, down2 = after([*gained, beyond, up2, down2])

    quarter = rows // nch
    parts, sent, own = mend(exons, [plain, near, far, beyond], gained, size)
    *sent, up2, down2 = after([*sent, up2, down2])
    got = [swap(block, "seq", d) for d, block in zip(range(1, nseq), sent)]
    up2, down2 = after([up2, down2], got[:1])
    up3, down3 = shift(up2, "seq", 1, 2), shift(down2, "seq", -1, 2)

    def origins():
        return [(lax.axis_index("ch") ^ t) * width for t in range(nch)]

    partial, laid = weight_gradient(
        [up1[rows - PAD :], x_saved, down1[:PAD]],
        [own],
        lambda: ([0, PAD, PAD + rows], [0], [0], [], []),
        rows,
        taps,
        rows,
        last=False,
        vmem=24,
        weights=weights,
        origins=origins,
    )
    center = pieces_gradient(parts, laid, taps)
    first, *rest, partial, center = after([*got, partial, center])
    across_first = swap(first, "ch", 2)
    crossing = jnp.concatenate([block[:quarter] for block in rest])
    across = swap(crossing, "ch", 2)
    beside_first = swap(first, "ch", 1)
    in_grad = pieces_gradient(parts, laid, taps, [first, rest[1], center])
    across_first, in_grad, crossing = after([across_first, in_grad, crossing])
    beside = swap(crossing, "ch", 1)
    beyond_first = swap(across_first, "ch", 1)

    def layout(hops, blocks):
        mine = lax.axis_index("seq")
        place = lax.axis_index("ch")
        x_rows = [PAD + mine * rows]
        for hop in range(1, hops):
            low_at, high_at = mine - hop, mine + hop
            x_rows += [
                jnp.where(low_at >= 0, PAD + low_at * rows, -1),
                jnp.where(high_at < nseq, PAD + high_at * rows, -1),
            ]
        g_rows = [
            (mine ^ d) * rows + (place ^ tag) * quarter for d in blocks for tag in range(nch)
        ]
        return x_rows, g_rows, [(mine ^ d) * rows for d in blocks], [], []

    (partial,) = weight_gradient(
        [x_saved, up1, down1, up2, down2],
        [first, beside_first, across_first, beyond_first],
        functools.partial(layout, 3, (1,)),
        rows,
        taps,
        nseq * rows,
        before=partial,
        last=False,
        vmem=32,
        span=quarter,
    )
    across, in_grad, partial, up3, down3 = after([across, in_grad, partial, up3, down3])
    beyond = swap(across, "ch", 1)

    g_pieces = []
    for d in range(nseq - 2):
        for piece in (crossing, beside, across, beyond):
            g_pieces.append(piece[d * quarter : (d + 1) * quarter])
    (w_grad,) = weight_gradient(
        [x_saved, up1, down1, up2, down2, up3, down3],
        g_pieces,
        functools.partial(layout, nseq, (2, 3)),
        rows,
        taps,
        nseq * rows,
        before=partial,
        vmem=32,
    )
    return (in_grad, w_grad.transpose(1, 0, 2))


def solution(mesh):
    in_specs = (
        P(("grp", "seq"), "ch"),
        P(("grp", "seq"), "ch"),
        P(("grp", "seq"), "ch"),
        P(None, None, "ch"),
        P(("grp", "seq"), None, None, "ch"),
        P("grp"),
        P("grp", None),
    )
    out_specs = (P(("grp", "seq"), "ch"), P(("grp", "seq"), None, "ch"))
    return jax.shard_map(local, mesh=mesh, in_specs=in_specs, out_specs=out_specs, check_vma=False)
```

```python
import functools

import jax
import jax.numpy as jnp
from jax import lax
from jax.experimental import pallas as pl
from jax.experimental.pallas import tpu as pltpu
from jax.sharding import PartitionSpec as P

PAD = 16
MIB = 1024 * 1024
VMEM = pl.BlockSpec(memory_space=pltpu.VMEM)
SMEM = pl.BlockSpec(memory_space=pltpu.SMEM)
SOME = pl.BlockSpec(memory_space=pl.ANY)
HALF_ROOT = 0.7071067811865476
DENSITY = 0.3989422804014327
LANES = 128
LONG = pl.CostEstimate(flops=4 * 10**9, bytes_accessed=1000, transcendentals=0)
LITTLE = pl.CostEstimate(flops=1000, bytes_accessed=1000, transcendentals=0)


def swap(block, axis, flip):
    count = lax.axis_size(axis)
    return lax.ppermute(block, axis, [(i, i ^ flip) for i in range(count)])


def shift(block, axis, step, first=0):
    count = lax.axis_size(axis)
    if step > 0:
        pairs = [(i, i + 1) for i in range(first, count - 1)]
    else:
        pairs = [(i + 1, i) for i in range(count - 1 - first)]
    return lax.ppermute(block, axis, pairs)


def after(values, others=()):
    return lax.optimization_barrier(tuple(values) + tuple(others))[: len(values)]


def input_kernel(part, low, high, weights, out, block):
    taps = weights.shape[0]
    rows = part.shape[0]
    half = taps // 2
    block[pl.ds(0, PAD), :] = low[...]
    block[pl.ds(PAD, rows), :] = part[...]
    block[pl.ds(PAD + rows, PAD), :] = high[...]
    tile = min(256, rows)

    def body(step, carry):
        start = pl.multiple_of(step * tile, tile)
        rows_in = block[pl.ds(start, tile + 2 * PAD), :]
        total = None
        for tap in range(taps):
            term = jnp.dot(rows_in, weights[tap], preferred_element_type=jnp.float32)
            first = PAD + half - tap
            term = term[first : first + tile]
            total = term if total is None else total + term
        out[pl.ds(start, tile), :] = total.astype(out.dtype)
        return carry

    lax.fori_loop(0, rows // tile, body, 0)


def input_gradient(part, low, high, weights):
    taps, chans, width = weights.shape
    rows = part.shape[0]
    return pl.pallas_call(
        input_kernel,
        out_shape=jax.ShapeDtypeStruct((rows, width), jnp.bfloat16),
        in_specs=[VMEM] * 4,
        out_specs=VMEM,
        scratch_shapes=[pltpu.VMEM((rows + 2 * PAD, chans), jnp.bfloat16)],
        compiler_params=pltpu.CompilerParams(vmem_limit_bytes=32 * MIB),
    )(part, low, high, weights)


def pieces_kernel(*refs, taps, pieces, middle):
    parts, rest = refs[:pieces], refs[pieces:]
    if middle:
        weights, out, block = rest
    else:
        near_edge, far_edge, center, weights, out, block = rest
    rows = parts[0].shape[0]
    width = weights.shape[1] // taps
    half = taps // 2
    quarter = rows // 4
    kept = [(0, rows)] if middle else [(0, quarter + PAD), (rows - quarter - PAD, quarter + PAD)]
    base = 0
    for part in parts:
        span = pl.ds(base, part.shape[1])
        for begin, count in kept:
            block[pl.ds(PAD + begin, count), span] = part[pl.ds(begin, count), :]
        base += part.shape[1]
    if not middle:
        mine = lax.axis_index("seq")
        one = near_edge[pl.ds(quarter, PAD), :].astype(jnp.float32)
        other = far_edge[pl.ds(quarter, PAD), :].astype(jnp.float32)
        low = jnp.where(mine % 2 == 1, one, jnp.where(mine == 2, other, 0.0))
        high = jnp.where(mine % 2 == 0, one, jnp.where(mine == 1, other, 0.0))
        for at in range(pieces):
            span = pl.ds(at * part.shape[1], part.shape[1])
            lower = pltpu.roll(low, PAD - half - half * at, 0)
            upper = pltpu.roll(high, (PAD - half * at) % PAD, 0)
            block[pl.ds(0, PAD), span] = lower.astype(block.dtype)
            block[pl.ds(PAD + rows, PAD), span] = upper.astype(block.dtype)

    def tile(start, count):
        terms = jnp.dot(
            block[pl.ds(start, count + 2 * PAD), :],
            weights[...],
            preferred_element_type=jnp.float32,
        )
        total = None
        for tap in range(taps):
            first = PAD + half - tap
            term = terms[first : first + count, tap * width : (tap + 1) * width]
            total = term if total is None else total + term
        return total.astype(out.dtype)

    if middle:
        out[...] = tile(quarter, 2 * quarter)
    else:
        out[pl.ds(0, quarter), :] = tile(0, quarter)
        out[pl.ds(quarter, 2 * quarter), :] = center[...]
        out[pl.ds(3 * quarter, quarter), :] = tile(3 * quarter, quarter)


def pieces_gradient(parts, weights, taps, rest=()):
    chans = weights.shape[0]
    width = weights.shape[1] // taps
    rows = parts[0].shape[0]
    middle = not rest
    return pl.pallas_call(
        functools.partial(pieces_kernel, taps=taps, pieces=len(parts), middle=middle),
        out_shape=jax.ShapeDtypeStruct((rows // 2 if middle else rows, width), jnp.bfloat16),
        in_specs=[VMEM] * (len(parts) + len(rest) + 1),
        out_specs=VMEM,
        scratch_shapes=[pltpu.VMEM((rows + 2 * PAD, chans), jnp.bfloat16)],
        cost_estimate=LITTLE,
        compiler_params=pltpu.CompilerParams(vmem_limit_bytes=24 * MIB),
    )(*parts, *rest, weights)


def weight_kernel(*refs, taps, tile, rows, size, nx, ng, layout, first, last, origins, span, stages):
    xs, gs, rest = refs[:nx], refs[nx : nx + ng], list(refs[nx + ng :])
    before = None if first else rest.pop(0)
    weights = rest.pop(0) if origins else None
    out = rest.pop(0)
    laid = rest.pop(0) if origins else None
    xbuf, gbuf, acc, sems = rest
    width = xbuf.shape[1]
    half = taps // 2
    x_rows, g_rows, starts, blanks, seams = layout()
    zeros = jnp.zeros((PAD, width), xbuf.dtype)
    xbuf[pl.ds(0, PAD), :] = zeros
    xbuf[pl.ds(PAD + rows, PAD), :] = zeros
    for wanted, row in blanks:

        @pl.when(wanted)
        def _():
            xbuf[pl.ds(row, PAD), :] = zeros

    pieces = [(src, xbuf, row, src.shape[0]) for src, row in zip(xs, x_rows)]
    pieces += [(src, gbuf, row, span or src.shape[0]) for src, row in zip(gs, g_rows)]

    def copy(at):
        src, dst, row, count = pieces[at]
        row = row if isinstance(row, int) else pl.multiple_of(row, 16)
        return pltpu.make_async_copy(
            src.at[pl.ds(0, count), :], dst.at[pl.ds(row, count), :], sems.at[at]
        )

    def each(act, stage=None):
        for at in range(nx + ng):
            if stages and stage is not None and stages[at] != stage:
                continue
            row = pieces[at][2]
            if isinstance(row, int):
                act(at)
            else:
                pl.when(row >= 0)(functools.partial(act, at))

    each(lambda at: copy(at).start())
    moves = []
    if origins:
        where = origins()
        depth = weights.shape[1] // len(where)
        for e, origin in enumerate(where):
            for tap in range(taps):
                moves.append(
                    pltpu.make_async_copy(
                        weights.at[tap, pl.ds(pl.multiple_of(origin, 16), depth), :],
                        laid.at[pl.ds(e * depth, depth), pl.ds(tap * width, width)],
                        sems.at[nx + ng + len(moves)],
                    )
                )
        for move in moves:
            move.start()
    short = size == tile and not seams and width % LANES == 0
    if not short:
        acc[...] = jnp.zeros_like(acc) if first else before[...]
    if not stages:
        each(lambda at: copy(at).wait())

    def add(start, count, side=None, base=None, close=False):
        grad = gbuf[pl.ds(start, count), :].T
        block = xbuf[pl.ds(start, count + 2 * PAD), :].astype(jnp.float32)
        if side is not None:
            row = lax.broadcasted_iota(jnp.int32, block.shape, 0)
            block = jnp.where(row >= count + PAD if side > 0 else row < PAD, block, 0.0)
        moved = []
        for tap in range(taps):
            at = PAD - half + tap
            moved.append(block[at : at + count].astype(jnp.bfloat16))
        if width % LANES:
            for tap in range(taps):
                acc[tap] += jnp.dot(grad, moved[tap], preferred_element_type=jnp.float32)
        else:
            moved = jnp.concatenate(moved, axis=1)
            total = jnp.dot(grad, moved, preferred_element_type=jnp.float32)
            if base is not None:
                total = base[...] + total
            if not close:
                acc[...] = total
            elif last:
                for tap in range(taps):
                    out[tap] = total[:, tap * width : (tap + 1) * width].astype(out.dtype)
            else:
                out[...] = total

    for stage, begin in enumerate(starts):
        if stages:
            each(lambda at: copy(at).wait(), stage)

        if short:
            base = acc if stage else before
            add(pl.multiple_of(begin, 16), tile, None, base, stage == len(starts) - 1)
            continue

        def body(step, carry):
            add(pl.multiple_of(begin + step * tile, 16), tile, None, acc)
            return carry

        lax.fori_loop(0, size // tile, body, 0)
    for wanted, row, side in seams:
        pl.when(wanted)(functools.partial(add, row, PAD, side, acc))
    if short:
        pass
    elif last and width % LANES == 0:
        for tap in range(taps):
            out[tap] = acc[:, tap * width : (tap + 1) * width].astype(out.dtype)
    else:
        out[...] = acc[...].astype(out.dtype)
    for move in moves:
        move.wait()


def weight_gradient(
    xs, gs, layout, size, taps, rows, before=None, last=True, vmem=40, weights=None, origins=None, span=None,
    stages=None
):
    width, chunk = xs[0].shape[1], gs[0].shape[1]
    split = (taps, chunk, width)
    joined = split if width % LANES else (chunk, taps * width)
    out_shape = [
        jax.ShapeDtypeStruct(split, jnp.bfloat16)
        if last
        else jax.ShapeDtypeStruct(joined, jnp.float32)
    ]
    moves = 0
    if origins:
        moves = taps * 4
        out_shape.append(
            jax.ShapeDtypeStruct((weights.shape[1], taps * width), weights.dtype)
        )
    return pl.pallas_call(
        functools.partial(
            weight_kernel,
            taps=taps,
            tile=min(1024, size) if width % LANES == 0 else min(512, size),
            rows=rows,
            size=size,
            nx=len(xs),
            ng=len(gs),
            layout=layout,
            first=before is None,
            last=last,
            origins=origins,
            span=span,
            stages=stages,
        ),
        out_shape=out_shape,
        in_specs=[SOME] * (len(xs) + len(gs))
        + [VMEM] * (before is not None)
        + [SOME] * (weights is not None),
        out_specs=[VMEM] * len(out_shape),
        scratch_shapes=[
            pltpu.VMEM((rows + 2 * PAD, width), jnp.bfloat16),
            pltpu.VMEM((rows, chunk), jnp.bfloat16),
            pltpu.VMEM(joined, jnp.float32),
            pltpu.SemaphoreType.DMA((len(xs) + len(gs) + moves,)),
        ],
        cost_estimate=LITTLE,
        compiler_params=pltpu.CompilerParams(vmem_limit_bytes=vmem * MIB),
    )(
        *xs,
        *gs,
        *([] if before is None else [before]),
        *([] if weights is None else [weights]),
    )


def merge_pairs(value, scratch):
    size = value.shape[0] // 2
    sums = []
    for at in range(value.shape[1] // LANES):
        scratch[at] = value[:, at * LANES : (at + 1) * LANES]
        even = scratch[at, pl.ds(0, size, stride=2), :]
        sums.append(even + scratch[at, pl.ds(1, size, stride=2), :])
    return jnp.concatenate(sums, axis=1)


def make_pairs(value, scratch):
    size = value.shape[0]
    rows = []
    for at in range(value.shape[1] // LANES):
        part = value[:, at * LANES : (at + 1) * LANES]
        scratch[at, pl.ds(0, size, stride=2), :] = part
        scratch[at, pl.ds(1, size, stride=2), :] = part
        rows.append(scratch[at])
    return jnp.concatenate(rows, axis=1)


def pair_scratch(rows, width):
    return pltpu.VMEM((width // LANES, rows, LANES), jnp.float32)


def each_exon(owners, exons, seen, nblocks, most, act):
    mine = lax.axis_index("seq")
    span, count = exons.shape
    for i in range(seen.shape[0]):
        seen[i] = 0

    def body(t, carry):
        owner = owners[t]
        slot = (owner ^ mine) * most + seen[owner]
        seen[owner] += 1
        for e in range(span):
            where = exons[e, t]

            @pl.when(where // nblocks == mine)
            def _():
                act(t, slot, where % nblocks)

        return carry

    lax.fori_loop(0, count, body, 0)


def front_kernel(owners, exons, pre_act, *refs, nblocks, most, size):
    outs, (slots, pair, seen) = refs[:-3], refs[-3:]
    slots[...] = jnp.zeros_like(slots)

    def act(t, slot, block):
        at = pl.ds(pl.multiple_of(block * (2 * size), 2 * size), 2 * size)
        value = pre_act[at, :].astype(jnp.float32)
        value = value * (0.5 * (1.0 + lax.erf(value * HALF_ROOT)))
        mean = 0.5 * merge_pairs(value, pair)
        slots[pl.ds(pl.multiple_of(slot * size, size), size), :] = mean

    each_exon(owners, exons, seen, nblocks, most, act)
    group = most * size
    for d, out in enumerate(outs):
        out[...] = slots[pl.ds(d * group, group), :].astype(out.dtype)


def front(owners, exons, pre_act, most, size, groups):
    rows, width = pre_act.shape
    return pl.pallas_call(
        functools.partial(
            front_kernel, nblocks=rows // 2 // size, most=most, size=size
        ),
        out_shape=[jax.ShapeDtypeStruct((most * size, width), jnp.bfloat16)] * groups,
        in_specs=[SMEM] * 2 + [VMEM],
        out_specs=[VMEM] * groups,
        scratch_shapes=[
            pltpu.VMEM((groups * most * size, width), jnp.float32),
            pair_scratch(2 * size, width),
            pltpu.SMEM((groups,), jnp.int32),
        ],
        cost_estimate=LITTLE,
        compiler_params=pltpu.CompilerParams(vmem_limit_bytes=16 * MIB),
    )(owners, exons, pre_act)


def plain_kernel(pre_act, out_grad, slope, plain, both):
    value = pre_act[...].astype(jnp.float32)
    normal = 0.5 * (1.0 + lax.erf(value * HALF_ROOT))
    slope[...] = normal + value * (jnp.exp(-0.5 * value * value) * DENSITY)
    pooled = make_pairs(out_grad[...].astype(jnp.float32) * 0.5, both)
    plain[...] = (pooled * slope[...]).astype(plain.dtype)


def plain_gradient(pre_act, out_grad):
    rows, width = pre_act.shape
    return pl.pallas_call(
        plain_kernel,
        out_shape=[
            jax.ShapeDtypeStruct((rows, width), jnp.float32),
            jax.ShapeDtypeStruct((rows, width), jnp.bfloat16),
        ],
        in_specs=[VMEM] * 2,
        out_specs=[VMEM] * 2,
        scratch_shapes=[pair_scratch(rows, width)],
        cost_estimate=LITTLE,
        compiler_params=pltpu.CompilerParams(vmem_limit_bytes=16 * MIB),
    )(pre_act, out_grad)


def gain_kernel(owners, exons, out_grad, slope, *refs, nblocks, most, size):
    splices, (grad, gain, held, both, seen) = refs[:-5], refs[-5:]
    gain[...] = out_grad[...].astype(jnp.float32)
    base = 0
    for splice in splices:
        held[pl.ds(base, splice.shape[0]), :] = splice[...].astype(jnp.float32)
        base += splice.shape[0]

    def add(t, slot, block):
        at = pl.ds(pl.multiple_of(block * size, size), size)
        gain[at, :] += held[pl.ds(pl.multiple_of(slot * size, size), size), :]

    def final(block):
        pooled = 0.5 * gain[pl.ds(pl.multiple_of(block * size, size), size), :]
        at = pl.ds(pl.multiple_of(block * (2 * size), 2 * size), 2 * size)
        return make_pairs(pooled, both) * slope[at, :]

    def renew(t, slot, block):
        at = pl.ds(pl.multiple_of(t * (2 * size), 2 * size), 2 * size)
        grad[at, :] = final(block).astype(grad.dtype)

    each_exon(owners, exons, seen, nblocks, most, add)
    each_exon(owners, exons, seen, nblocks, most, renew)
    count = exons.shape[1]
    row = lax.broadcasted_iota(jnp.int32, (2 * size, grad.shape[1]), 0)
    for at, block, first in ((count, 0, 0), (count + 1, nblocks - 1, 2 * size - 2)):
        rows = final(block)
        rows = jnp.where(row % 2 == 0, rows[first : first + 1], rows[first + 1 : first + 2])
        grad[pl.ds(at * 2 * size, 2 * size), :] = rows.astype(grad.dtype)


def gained_rows(owners, exons, out_grad, slope, splices, most, size, groups):
    rows, width = slope.shape
    return pl.pallas_call(
        functools.partial(gain_kernel, nblocks=rows // 2 // size, most=most, size=size),
        out_shape=jax.ShapeDtypeStruct(((exons.shape[1] + 2) * 2 * size, width), jnp.bfloat16),
        in_specs=[SMEM] * 2 + [VMEM] * (2 + len(splices)),
        out_specs=VMEM,
        scratch_shapes=[
            pltpu.VMEM((rows // 2, width), jnp.float32),
            pltpu.VMEM((groups * most * size, width), jnp.float32),
            pair_scratch(2 * size, width),
            pltpu.SMEM((groups,), jnp.int32),
        ],
        cost_estimate=LONG,
        compiler_params=pltpu.CompilerParams(vmem_limit_bytes=16 * MIB),
    )(owners, exons, out_grad, slope, *splices)


def mend_kernel(exons, *refs, pieces, nblocks, size):
    gained, parts, sent, own = (
        refs[pieces : 2 * pieces],
        refs[2 * pieces : 3 * pieces],
        refs[3 * pieces : -1],
        refs[-1],
    )
    mine = lax.axis_index("seq")
    place = lax.axis_index("ch")
    span, count = exons.shape
    rows = parts[0].shape[0]
    quarter = rows // pieces

    def body(t, carry):
        for e in range(span):
            where = exons[e, t]

            @pl.when(where // nblocks == mine)
            def _():
                to = pl.ds(pl.multiple_of(where % nblocks * (2 * size), 2 * size), 2 * size)
                at = pl.ds(pl.multiple_of(t * (2 * size), 2 * size), 2 * size)
                for part, new in zip(parts, gained):
                    part[to, :] = new[at, :]

        return carry

    lax.fori_loop(0, count, body, 0)
    row = lax.broadcasted_iota(jnp.int32, (PAD, own.shape[1]), 0)
    for d, out in enumerate(sent, 1):
        for tag, part in enumerate(parts):

            @pl.when(mine ^ d ^ place == tag)
            def _():
                at = pl.ds(pl.multiple_of(place * quarter, quarter), quarter)
                out[pl.ds(0, quarter), :] = part[at, :]

        if out.shape[0] > quarter:
            after_me = (mine ^ d) > mine
            edge = jnp.zeros(row.shape, jnp.float32)
            for tag, new in enumerate(gained):
                head = new[pl.ds(count * 2 * size, PAD), :].astype(jnp.float32)
                tail = new[pl.ds((count + 1) * 2 * size, PAD), :].astype(jnp.float32)
                edge = jnp.where(row // 2 == tag, jnp.where(after_me, tail, head), edge)
            out[pl.ds(quarter, PAD), :] = edge.astype(out.dtype)
    for tag, part in enumerate(parts):

        @pl.when(mine ^ place == tag)
        def _():
            own[...] = part[...]


def mend(exons, parts, gained, size):
    rows, width = parts[0].shape
    pieces = len(parts)
    whole = jax.ShapeDtypeStruct((rows, width), jnp.bfloat16)
    quarter = rows // pieces
    sent = [
        jax.ShapeDtypeStruct((quarter + (PAD if d in (1, 3) else 0), width), jnp.bfloat16)
        for d in range(1, pieces)
    ]
    outs = pl.pallas_call(
        functools.partial(mend_kernel, pieces=pieces, nblocks=rows // 2 // size, size=size),
        out_shape=[whole] * pieces + sent + [whole],
        in_specs=[SMEM] + [VMEM] * (2 * pieces),
        out_specs=[VMEM] * (pieces + len(sent) + 1),
        input_output_aliases={1 + at: at for at in range(pieces)},
        cost_estimate=LITTLE,
        compiler_params=pltpu.CompilerParams(vmem_limit_bytes=24 * MIB),
    )(exons, *parts, *gained)
    return outs[:pieces], outs[pieces:-1], outs[-1]


def gathered_gradient(pre_act, out_grad, coverage_obs, owners, exon_blocks):
    rows, width = pre_act.shape
    nseq = lax.axis_size("seq")
    mine = lax.axis_index("seq")
    most, block = coverage_obs.shape[1:3]
    nblocks = rows // 2 // block
    counts = owners.shape[0]
    value = pre_act.astype(jnp.float32)
    normal = 0.5 * (1.0 + jax.scipy.special.erf(value * HALF_ROOT))
    slope = normal + value * jnp.exp(-0.5 * value * value) * DENSITY
    act = value * normal
    pooled = (0.5 * jnp.sum(act.reshape(rows // 2, 2, width), axis=1)).astype(jnp.bfloat16)
    order = jnp.arange(counts, dtype=jnp.int32)
    same = owners[:, None] == owners[None, :]
    rank = jnp.sum((same & (order[:, None] < order[None, :])).astype(jnp.int32), axis=0)
    dest = jnp.arange(nseq, dtype=jnp.int32)
    slots = jnp.arange(most, dtype=jnp.int32)
    route = (owners[None, None, :] == dest[:, None, None]) & (
        rank[None, None, :] == slots[None, :, None]
    )
    route = route.astype(jnp.float32).reshape(nseq * most, counts)
    on_mine = exon_blocks // nblocks == mine
    holds = jnp.any(on_mine, axis=1)
    local_block = jnp.sum(jnp.where(on_mine, exon_blocks % nblocks, 0), axis=1)
    select = (
        holds[:, None] & (local_block[:, None] == jnp.arange(nblocks, dtype=jnp.int32)[None, :])
    ).astype(jnp.float32)
    picker = jnp.dot(route, select, precision=lax.Precision.HIGHEST).astype(jnp.bfloat16)
    pieces = pooled.reshape(nblocks, block * width)
    outgoing = jnp.dot(picker, pieces, preferred_element_type=jnp.float32).astype(jnp.bfloat16)
    outgoing = outgoing.reshape(nseq, most, block, width)
    arrived = lax.all_to_all(outgoing, "seq", split_axis=0, concat_axis=0, tiled=True)
    coverage = jnp.sum(arrived.astype(jnp.float32), axis=0)
    splice = jnp.tanh(coverage - coverage_obs[0]).astype(jnp.bfloat16)
    returned = lax.all_gather(splice, "seq", axis=0).reshape(nseq * most, block * width)
    gained = jnp.dot(picker.T, returned, preferred_element_type=jnp.float32)
    pooled_grad = out_grad.astype(jnp.float32) + gained.reshape(rows // 2, width)
    return (jnp.repeat(pooled_grad, 2, axis=0) * 0.5 * slope).astype(jnp.bfloat16)


def local(x_saved, pre_act, out_grad, conv_w, coverage_obs, owners, exon_blocks):
    rows, width = x_saved.shape
    taps = conv_w.shape[1]
    nseq = lax.axis_size("seq")
    nch = lax.axis_size("ch")
    chunk = conv_w.shape[0] // nseq
    most = coverage_obs.shape[1]
    size = coverage_obs.shape[2]
    direct = nseq == nch == 4 and chunk == width and width % 128 == 0
    exons = exon_blocks.T
    weights = conv_w.transpose(1, 0, 2)
    target = coverage_obs[0].reshape(most * size, width)

    if not direct:
        pre_grad = gathered_gradient(pre_act, out_grad, coverage_obs, owners, exon_blocks)
        x_all = lax.all_gather(x_saved, "seq", axis=0, tiled=True)
        whole = lax.all_gather(pre_grad, "ch", axis=1, tiled=True)
        blocks = whole.reshape(rows, nseq, chunk).transpose(1, 0, 2)
        g_all = lax.all_to_all(blocks, "seq", 0, 0, tiled=True).reshape(nseq * rows, chunk)
        low = shift(whole[rows - PAD :], "seq", 1)
        high = shift(whole[:PAD], "seq", -1)
        in_grad = input_gradient(whole, low, high, weights)
        total = nseq * rows
        (w_grad,) = weight_gradient(
            [x_all], [g_all], lambda: ([PAD], [0], [0], [], []), total, taps, total
        )
        return (in_grad, w_grad.transpose(1, 0, 2))

    outgoing = front(owners, exons, pre_act, most, size, nseq)
    slope, plain = plain_gradient(pre_act, out_grad)
    arrived = [outgoing[0]] + [swap(outgoing[d], "seq", d) for d in range(1, nseq)]
    (source,) = after([x_saved], outgoing)
    up1, down1 = shift(source, "seq", 1), shift(source, "seq", -1)
    *arrived, plain, slope = after([*arrived, plain, slope])
    far, near = swap(plain, "ch", 2), swap(plain, "ch", 1)
    coverage = functools.reduce(jnp.add, [a.astype(jnp.float32) for a in arrived])
    splice = jnp.tanh(coverage - target).astype(jnp.bfloat16)
    (last_splice,) = after([splice], [up1, down1])
    splices = [splice, swap(splice, "seq", 1), swap(splice, "seq", 2), swap(last_splice, "seq", 3)]
    gained = gained_rows(owners, exons, out_grad, slope, splices, most, size, nseq)

    far_gained, near_gained = swap(gained, "ch", 2), swap(gained, "ch", 1)
    up2, down2 = shift(up1, "seq", 1, 1), shift(down1, "seq", -1, 1)
    beyond = swap(far, "ch", 1)
    gained = [gained, near_gained, far_gained, swap(far_gained, "ch", 1)]
    *gained, beyond, up2, down2 = after([*gained, beyond, up2, down2])

    quarter = rows // nch
    parts, sent, own = mend(exons, [plain, near, far, beyond], gained, size)
    *sent, up2, down2 = after([*sent, up2, down2])
    got = [swap(block, "seq", d) for d, block in zip(range(1, nseq), sent)]
    up2, down2 = after([up2, down2], got[:1])
    up3, down3 = shift(up2, "seq", 1, 2), shift(down2, "seq", -1, 2)

    def origins():
        return [(lax.axis_index("ch") ^ t) * width for t in range(nch)]

    partial, laid = weight_gradient(
        [up1[rows - PAD :], x_saved, down1[:PAD]],
        [own],
        lambda: ([0, PAD, PAD + rows], [0], [0], [], []),
        rows,
        taps,
        rows,
        last=False,
        vmem=24,
        weights=weights,
        origins=origins,
    )
    center = pieces_gradient(parts, laid, taps)
    first, *rest, partial, center = after([*got, partial, center])
    across_first = swap(first, "ch", 2)
    crossing = jnp.concatenate([block[:quarter] for block in rest])
    across = swap(crossing, "ch", 2)
    beside_first = swap(first, "ch", 1)
    in_grad = pieces_gradient(parts, laid, taps, [first, rest[1], center])
    across_first, in_grad, crossing = after([across_first, in_grad, crossing])
    beside = swap(crossing, "ch", 1)
    beyond_first = swap(across_first, "ch", 1)

    def layout(hops, blocks):
        mine = lax.axis_index("seq")
        place = lax.axis_index("ch")
        x_rows = [PAD + mine * rows]
        for hop in range(1, hops):
            low_at, high_at = mine - hop, mine + hop
            x_rows += [
                jnp.where(low_at >= 0, PAD + low_at * rows, -1),
                jnp.where(high_at < nseq, PAD + high_at * rows, -1),
            ]
        g_rows = [
            (mine ^ d) * rows + (place ^ tag) * quarter for d in blocks for tag in range(nch)
        ]
        return x_rows, g_rows, [(mine ^ d) * rows for d in blocks], [], []

    (partial,) = weight_gradient(
        [x_saved, up1, down1, up2, down2],
        [first, beside_first, across_first, beyond_first],
        functools.partial(layout, 3, (1,)),
        rows,
        taps,
        nseq * rows,
        before=partial,
        last=False,
        vmem=32,
        span=quarter,
    )
    across, in_grad, partial, up3, down3 = after([across, in_grad, partial, up3, down3])
    beyond = swap(across, "ch", 1)

    g_pieces = []
    for d in range(nseq - 2):
        for piece in (crossing, beside, across, beyond):
            g_pieces.append(piece[d * quarter : (d + 1) * quarter])
    (w_grad,) = weight_gradient(
        [x_saved, up1, down1, up2, down2, up3, down3],
        g_pieces,
        functools.partial(layout, nseq, (2, 3)),
        rows,
        taps,
        nseq * rows,
        before=partial,
        vmem=32,
        stages=[0] * 11 + [1] * 4,
    )
    return (in_grad, w_grad.transpose(1, 0, 2))


def solution(mesh):
    in_specs = (
        P(("grp", "seq"), "ch"),
        P(("grp", "seq"), "ch"),
        P(("grp", "seq"), "ch"),
        P(None, None, "ch"),
        P(("grp", "seq"), None, None, "ch"),
        P("grp"),
        P("grp", None),
    )
    out_specs = (P(("grp", "seq"), "ch"), P(("grp", "seq"), None, "ch"))
    return jax.shard_map(local, mesh=mesh, in_specs=in_specs, out_specs=out_specs, check_vma=False)
```
